256 devices in a mesh: lon: 16 (over x_hi, y, core), lat: 16 (over z, x_lo).
Axes of the slice: x: 4 (x_hi: 2, x_lo: 2; x = x_hi * 2 + x_lo), y: 4, z: 8, core: 2. Of those that a mesh axis runs over, the one named last changes fastest.
Arguments:
- background: bfloat16 [2, 128, 256, 2048], P(None, None, 'lat', 'lon'), may hold values from -6 to 6
- obs_cell: int32 [16, 16, 1024], P('lat', 'lon'), may hold values from 0 to 2047, as said below
- obs_count: int32 [16, 16], P('lat', 'lon'), may hold values from 128 to 1024, as said below
- obs_value: bfloat16 [16, 16, 1024], P('lat', 'lon'), may hold values from -6 to 6
- obs_err: float32 [16, 16, 1024], P('lat', 'lon'), may hold values from 0.5 to 2
- land: int32 [256, 2048], P('lat', 'lon'), may hold values 0 or 1
Outputs:
- analysis: bfloat16 [2, 128, 256, 2048], P(None, None, 'lat', 'lon')
The draws below stay inside these ranges and needn't reach their ends.
Inputs may be any that keep to these rules, and one draw needn't show every extreme that they name: `obs_cell`: the 1024 cells named by one tile are distinct; a cell is numbered row * 128 + column within its tile. `obs_count`: some tile uses all its slots.
All inputs are finite; a program needn't handle non-finite values. No bound on the sum of `land` on one device may be relied on, other than what follows from the above.
Results may differ from the reference program's by a relative error of at most 0.0052.
Values may be sent and summed in bfloat16 or wider, within the bound.
No kernel may reach another device: no remote copies, remote signals or barrier semaphores. Data moves between devices by JAX's collectives and lax.ppermute only.
A program may use at most 64 MiB of HBM per device.

```python
import math
import jax
import jax.numpy as jnp
from jax import lax

MEMBERS = 128
VARS = 2
TILE_LON = 128
TILE_LAT = 16
PATCH = 16
RADIUS = 15
NS_ITERS = 5
OBS_MAX = 1024
LAT_TILES = 16
LON_TILES = 16
NY = 256
NX = 2048


def draw_obs_cell(key, part):
    key = jax.random.fold_in(key, 11)
    tile_keys = jax.random.split(key, LAT_TILES * LON_TILES)
    chosen = jax.vmap(lambda tile_key: jax.random.permutation(tile_key, TILE_LAT * TILE_LON)[:OBS_MAX])(tile_keys)
    return chosen.reshape(LAT_TILES, LON_TILES, OBS_MAX).astype(jnp.int32)


def draw_obs_count(key, part):
    key = jax.random.fold_in(key, 23)
    first_key, second_key, full_key = jax.random.split(key, 3)
    lowest = OBS_MAX // 8
    span_width = OBS_MAX - lowest
    first_draw = jax.random.randint(first_key, (LAT_TILES * LON_TILES,), 0, span_width + 1)
    second_draw = jax.random.randint(second_key, (LAT_TILES * LON_TILES,), 0, span_width + 1)
    counts = lowest + first_draw * second_draw // span_width
    full_tile = jax.random.randint(full_key, (), 0, LAT_TILES * LON_TILES)
    counts = counts.at[full_tile].set(OBS_MAX)
    return counts.reshape(LAT_TILES, LON_TILES).astype(jnp.int32)


def plant(values, stream_key, least, high):
    spot = [jax.random.randint(jax.random.fold_in(stream_key, axis), (), 0, length) for axis, length in enumerate(values.shape)]
    main_axis = values.shape.index(max(values.shape))
    next_to = spot[:main_axis] + [(spot[main_axis] + 1) % values.shape[main_axis]] + spot[main_axis + 1:]
    return values.at[tuple(spot)].set(least).at[tuple(next_to)].set(high)


def level_of(stream_key, extent, cuts, smallest, top_value):
    def one(position, shards_of):
        steps = jax.random.uniform(jax.random.fold_in(jax.random.fold_in(stream_key, 6), position), (shards_of,), jnp.float32, smallest / len(cuts), top_value / len(cuts))
        return jnp.repeat(jnp.exp(steps), extent[position] // shards_of).reshape((-1,) + (1,) * (len(extent) - position - 1))

    factor_of = one(*cuts[0])
    for cut in cuts[1:]:
        factor_of = factor_of * one(*cut)
    return factor_of


def bell_draw(rng, extent, scale, most, cuts=(), held_as=jnp.bfloat16):
    entries = scale * jax.random.normal(rng, extent, jnp.float32)
    if cuts:
        entries = entries * level_of(rng, extent, cuts, -0.22, 0.18)
    return jnp.clip(entries, -most, most).astype(held_as)


def setup_inputs(seed: int = 0) -> dict:
    streams_of = jax.random.split(jax.random.key(seed), 7)
    background = bell_draw(streams_of[0], (VARS, MEMBERS, NY, NX), 1.0, 6.0, ((2, 16), (3, 16)))
    obs_cell = draw_obs_cell(jax.random.fold_in(streams_of[6], 71), 0)
    obs_count = draw_obs_count(jax.random.fold_in(streams_of[6], 71), 0)
    obs_value = bell_draw(streams_of[3], (LAT_TILES, LON_TILES, OBS_MAX), 1.0, 6.0, ((0, 16), (1, 16)))
    obs_err = jnp.clip(jnp.exp(math.log(2.0) - 1.3862944 * jax.random.uniform(streams_of[4], (LAT_TILES, LON_TILES, OBS_MAX), jnp.float32) ** level_of(streams_of[4], (LAT_TILES, LON_TILES, OBS_MAX), ((0, 16), (1, 16)), -0.2, 0.2)), 0.5, 2.0)
    land = plant((jax.random.randint(streams_of[5], (NY, NX), 0, 4) < 3).astype(jnp.int32), jax.random.fold_in(streams_of[5], 1), 0, 1)
    return {"background": background, "obs_cell": obs_cell, "obs_count": obs_count, "obs_value": obs_value, "obs_err": obs_err, "land": land}


def footprint(lai_rim, first_row, band_rows):
    widened = lai_rim.astype(jnp.float32)
    across = widened[:, :, :-2] + widened[:, :, 1:-1] + widened[:, :, 2:]
    summed = across[:, :-2] + across[:, 1:-1] + across[:, 2:]
    row_ids = first_row + jnp.arange(summed.shape[1], dtype=jnp.int32)

    def present(row_pos):
        return ((row_pos >= 0) & (row_pos < band_rows)).astype(jnp.float32)
    row_count = present(row_ids - 1) + present(row_ids) + present(row_ids + 1)
    return summed / (3.0 * jnp.maximum(row_count, 1.0))[None, :, None]

def perturb(footprint_mean, observed):
    footprint_avg = lax.optimization_barrier(jnp.mean(footprint_mean, axis=0))
    ypert = (footprint_mean - footprint_avg[None]).astype(jnp.bfloat16)
    innovation = (observed.astype(jnp.float32) - footprint_avg).astype(jnp.bfloat16)
    return (ypert, innovation)

def observed_grids(obs_cell, obs_count, obs_value, obs_err, land, tile_rows, tile_cols):
    lat_tiles, lon_tiles, slot_total = obs_cell.shape
    slot_index = jnp.arange(slot_total, dtype=jnp.int32)
    in_use = slot_index[None, None, :] < obs_count[:, :, None]
    tile_lat = jnp.arange(lat_tiles, dtype=jnp.int32)[:, None, None]
    tile_lon = jnp.arange(lon_tiles, dtype=jnp.int32)[None, :, None]
    cell_row = tile_lat * tile_rows + obs_cell // tile_cols
    cell_col = tile_lon * tile_cols + obs_cell % tile_cols
    flat_index = (cell_row * (lon_tiles * tile_cols) + cell_col).reshape(-1)
    inverse_var = jnp.where(in_use, 1.0 / (obs_err * obs_err), 0.0).reshape(-1)
    values_in = jnp.where(in_use, obs_value.astype(jnp.float32), 0.0).reshape(-1)
    total_cells = lat_tiles * tile_rows * lon_tiles * tile_cols
    precision = jnp.zeros((total_cells,), jnp.float32).at[flat_index].add(inverse_var).reshape(land.shape)
    precision = (precision * land.astype(jnp.float32)).astype(jnp.bfloat16)
    observed = jnp.zeros((total_cells,), jnp.float32).at[flat_index].add(values_in).reshape(land.shape)
    return (precision, observed.astype(jnp.bfloat16))

def taper(window, reach):
    offsets = jnp.arange(window, dtype=jnp.float32) - (window - 1) / 2.0
    return 1.0 - jnp.abs(offsets) / (2.0 * reach)

def solve_patch(pert_window, innov_window, prec_window, reach, iters):
    members = pert_window.shape[0]
    window = pert_window.shape[1]
    taper_line = taper(window, reach)
    weight = prec_window.astype(jnp.float32) * taper_line[:, None] * taper_line[None, :]
    flat_pert = pert_window.reshape(members, window * window)
    scaled = (flat_pert.astype(jnp.float32) * weight.reshape(-1)[None, :]).astype(jnp.bfloat16)
    gram_matrix = lax.dot_general(scaled, flat_pert, (((1,), (1,)), ((), ())), preferred_element_type=jnp.float32)
    forcing = jnp.dot(scaled, innov_window.reshape(-1), preferred_element_type=jnp.float32)
    identity = jnp.eye(members, dtype=jnp.float32)
    system = (members - 1.0) * identity + gram_matrix
    frob_norm = jnp.sqrt(jnp.sum(system * system))
    upper = system / frob_norm
    lower = identity
    for sweep in range(iters):
        middle = 1.5 * identity - 0.5 * jnp.dot(lower, upper, precision=lax.Precision.HIGHEST)
        upper = jnp.dot(upper, middle, precision=lax.Precision.HIGHEST)
        lower = jnp.dot(middle, lower, precision=lax.Precision.HIGHEST)
    covariance = jnp.dot(lower, lower, precision=lax.Precision.HIGHEST) / frob_norm
    mean_weight = jnp.dot(covariance, forcing, precision=lax.Precision.HIGHEST)
    transform = jnp.sqrt(members - 1.0) * lower / jnp.sqrt(frob_norm) + mean_weight[:, None]
    return transform.astype(jnp.bfloat16)

def patch_weights(extended, patch, radius, iters):
    channels = extended.shape[0]
    members = channels - 2
    window = patch + 2 * radius
    reach = radius + patch / 2.0
    patch_rows = (extended.shape[1] - 2 * radius) // patch
    patch_cols = (extended.shape[2] - 2 * radius) // patch
    col_starts = jnp.arange(patch_cols, dtype=jnp.int32) * patch
    zero_start = jnp.zeros((), jnp.int32)

    def one_patch(row_start, col_start):
        piece = lax.dynamic_slice(extended, (zero_start, row_start, col_start), (channels, window, window))
        return solve_patch(piece[:members], piece[members], piece[members + 1], reach, iters)

    def one_row(row_index):
        return jax.vmap(lambda col_start: one_patch(row_index * patch, col_start))(col_starts)
    return lax.map(one_row, jnp.arange(patch_rows, dtype=jnp.int32))

def wrap_pad(stacked, width):
    across = jnp.concatenate([stacked[:, :, -width:], stacked, stacked[:, :, :width]], 2)
    return jnp.pad(across, ((0, 0), (width, width), (0, 0)))

def reference(background, obs_cell, obs_count, obs_value, obs_err, land):
    variables, members, grid_rows, grid_cols = background.shape
    mean_state = lax.optimization_barrier(jnp.mean(background.astype(jnp.float32), axis=1))
    pert_state = (background.astype(jnp.float32) - mean_state[:, None]).astype(jnp.bfloat16)
    precision, observed = observed_grids(obs_cell, obs_count, obs_value, obs_err, land, TILE_LAT, TILE_LON)
    lai_rim = wrap_pad(background[0], 1)
    ypert, innovation = perturb(footprint(lai_rim, 0, grid_rows), observed)
    stacked = jnp.concatenate([ypert, innovation[None], precision[None]], 0)
    extended = wrap_pad(stacked, RADIUS)
    transform = patch_weights(extended, PATCH, RADIUS, NS_ITERS)
    patch_rows = grid_rows // PATCH
    patch_cols = grid_cols // PATCH
    tiled_pert = pert_state.reshape(variables, members, patch_rows, PATCH, patch_cols, PATCH)
    increment = jnp.einsum('vkaibj,abkm->vmaibj', tiled_pert.astype(jnp.float32), transform.astype(jnp.float32), precision=lax.Precision.HIGHEST)
    increment = increment.reshape(variables, members, grid_rows, grid_cols)
    updated = mean_state[:, None] + increment
    kept = jnp.where((land != 0)[None, None], updated, background.astype(jnp.float32))
    return kept.astype(jnp.bfloat16)
```

```python
import jax
import jax.numpy as jnp
import numpy as np
from jax import lax
from jax.experimental import pallas as pl
from jax.experimental.pallas import tpu as pltpu
from jax.sharding import PartitionSpec as P

MEMBERS = 128
PATCH = 16
RADIUS = 15
NS_ITERS = 5
ROWS = 16
COLS = 128
PATCHES = COLS // PATCH
CELLS = PATCH * PATCH
EXTRA = 16
CHANNELS = MEMBERS + EXTRA
PACKED = (PATCHES // 2) * MEMBERS + 16
NT = (((1,), (1,)), ((), ()))
VMEM_LIMIT = 48 * 1024 * 1024
F32 = jnp.float32
BF16 = jnp.bfloat16


def taper_table():
    line = np.arange(PATCH, dtype=np.float32)
    span = np.float32(2.0 * (RADIUS + PATCH / 2.0))
    half = np.float32((PATCH - 1) / 2.0)
    ahead = np.where(line >= 1, 1 - (PATCH + half - line) / span, 0)
    inside = 1 - np.abs(line - half) / span
    behind = np.where(line <= PATCH - 2, 1 - (line + PATCH - half) / span, 0)
    lon = np.stack([ahead, inside, behind])
    lat = np.stack([behind, inside, ahead])
    table = lat[:, None, :, None] * lon[None, :, None, :]
    full = np.zeros((8, 3 * CELLS), np.float32)
    full[:3] = table.reshape(3, 3 * CELLS)
    return full


def stencil_tables():
    rows, cols = np.divmod(np.arange(CELLS), PATCH)
    near = np.abs(rows[:, None] - rows[None, :]) <= 1
    main, rim = [], []
    for side in (-1, 0, 1):
        beside = np.abs(side * PATCH + cols[:, None] - cols[None, :]) <= 1
        main.append(near & beside)
        edge = np.zeros((COLS, CELLS), bool)
        column = np.arange(PATCH)
        reach = np.abs(side * PATCH + column[:, None] - cols[None, :]) <= 1
        edge[:PATCH] = reach & (rows == 0)[None, :]
        edge[PATCH : 2 * PATCH] = reach & (rows == ROWS - 1)[None, :]
        rim.append(edge)
    return np.concatenate(main, 0), np.concatenate(rim, 0)


def swap_groups(arrays):
    lane = lax.broadcasted_iota(jnp.int32, arrays[0].shape, 1)
    for step in (1, 2, 4):
        width = PATCH * step
        high = (lane & width) != 0
        mixed = list(arrays)
        for i in range(8):
            if i & step == 0:
                first, second = arrays[i], arrays[i + step]
                mixed[i] = jnp.where(high, pltpu.roll(second, width, 1), first)
                mixed[i + step] = jnp.where(high, second, pltpu.roll(first, COLS - width, 1))
        arrays = mixed
    return arrays


def to_blocks(field_ref, index, out_ref, scratch):
    for m in range(MEMBERS // 16):
        piece = field_ref[index, pl.ds(m * 16, 16)].astype(F32)
        scratch[pl.ds(m * 256, 256), :] = piece.reshape(256, COLS)
    for m in range(MEMBERS // 16):
        halves = []
        for g in range(2):
            lines = [
                scratch[pl.ds(m * 256 + g * 8 + r, 16, stride=16), :] for r in range(8)
            ]
            halves.append(swap_groups(lines))
        for b in range(PATCHES):
            both = jnp.concatenate([halves[0][b], halves[1][b]], axis=1)
            out_ref[pl.ds(m * 16, 16), pl.ds(b * CELLS, CELLS)] = both.astype(BF16)


def layout_kernel(field_ref, cell_ref, count_ref, value_ref, err_ref, land_ref, blocks_ref, mask_ref, scratch):
    to_blocks(field_ref, 0, blocks_ref, scratch)
    land = land_ref[...].astype(F32)
    halves = []
    for g in range(2):
        lines = [jnp.broadcast_to(land[g * 8 + r : g * 8 + r + 1], (8, COLS)) for r in range(8)]
        halves.append(swap_groups(lines))
    which = lax.broadcasted_iota(jnp.int32, (8, CELLS), 0)
    mask = jnp.zeros((8, CELLS), F32)
    for b in range(PATCHES):
        mask = jnp.where(which == b, jnp.concatenate([halves[0][b], halves[1][b]], axis=1), mask)
    mask_ref[...] = mask
    cell = cell_ref[...]
    slots = cell.shape[1]
    used = lax.broadcasted_iota(jnp.int32, (1, slots), 1) < count_ref[0, 0]
    err = err_ref[...]
    inverse = jnp.where(used, 1.0 / (err * err), 0.0)
    value = jnp.where(used, value_ref[...].astype(F32), 0.0)
    column = cell & (COLS - 1)
    block = column >> 4
    place = ((cell >> 7) << 4) + (column & (PATCH - 1))
    slot_block = lax.broadcasted_iota(jnp.int32, (16, slots), 0)
    chosen = (slot_block & 7) == block
    amount = jnp.where(slot_block < 8, inverse, value)
    left = jnp.where(chosen, amount, 0.0).astype(BF16)
    spot = lax.broadcasted_iota(jnp.int32, (CELLS, slots), 0) == place
    right = jnp.where(spot, 1.0, 0.0).astype(BF16)
    grids = lax.dot_general(left, right, NT, preferred_element_type=F32)
    precision = grids[:8] * mask
    observed = grids[8:]
    row = lax.broadcasted_iota(jnp.int32, (EXTRA, CELLS), 0)
    for b in range(PATCHES):
        tail = jnp.where(row == 0, precision[b : b + 1], jnp.where(row == 1, observed[b : b + 1], 0.0))
        blocks_ref[pl.ds(MEMBERS, EXTRA), pl.ds(b * CELLS, CELLS)] = tail.astype(BF16)


def rim_kernel(first_ref, second_ref, blocks_ref, rim_ref, even_ref, odd_ref):
    lat_odd = (lax.axis_index("lat") & 1) == 1
    lon_odd = (lax.axis_index("lon") & 1) == 1
    first = first_ref[...].astype(F32)
    second = second_ref[...].astype(F32)
    above = jnp.where(lat_odd, first, second)
    below = jnp.where(lat_odd, second, first)
    lane = lax.broadcasted_iota(jnp.int32, (MEMBERS, COLS), 1)
    for b in range(PATCHES):
        top = pltpu.roll(above, (COLS - PATCH * b) % COLS, 1)
        low = pltpu.roll(below, (COLS - PATCH * b + PATCH) % COLS, 1)
        edge = jnp.where(lane < PATCH, top, jnp.where(lane < 2 * PATCH, low, 0.0)).astype(BF16)
        rim_ref[:, pl.ds(b * COLS, COLS)] = edge
        if b == 0:
            west_rim = edge
        if b == PATCHES - 1:
            east_rim = edge
    west = blocks_ref[:, pl.ds(0, CELLS)]
    east = blocks_ref[:, pl.ds((PATCHES - 1) * CELLS, CELLS)]
    even_ref[:, pl.ds(0, CELLS)] = jnp.where(lon_odd, west, east)
    odd_ref[:, pl.ds(0, CELLS)] = jnp.where(lon_odd, east, west)
    even_ref[pl.ds(0, MEMBERS), pl.ds(CELLS, COLS)] = jnp.where(lon_odd, west_rim, east_rim)
    odd_ref[pl.ds(0, MEMBERS), pl.ds(CELLS, COLS)] = jnp.where(lon_odd, east_rim, west_rim)
    blank = jnp.zeros((EXTRA, COLS), BF16)
    even_ref[pl.ds(MEMBERS, EXTRA), pl.ds(CELLS, COLS)] = blank
    odd_ref[pl.ds(MEMBERS, EXTRA), pl.ds(CELLS, COLS)] = blank


def gram_kernel(
    blocks_ref, rim_ref, first_ref, second_ref, taper_ref, main_ref, edge_ref,
    even_ref, odd_ref, gram_ref, force_ref, wide, wide_rim, pert,
):
    lat = lax.axis_index("lat")
    lat_odd = (lat & 1) == 1
    lon_odd = (lax.axis_index("lon") & 1) == 1
    span = PATCHES * CELLS
    wide[:, pl.ds(0, CELLS)] = jnp.zeros((CHANNELS, CELLS), BF16)
    wide[:, pl.ds(span + 3 * CELLS, CELLS)] = jnp.zeros((CHANNELS, CELLS), BF16)
    wide[:, pl.ds(2 * CELLS, span)] = blocks_ref[...]
    one = first_ref[:, pl.ds(0, CELLS)]
    two = second_ref[:, pl.ds(0, CELLS)]
    wide[:, pl.ds(CELLS, CELLS)] = jnp.where(lon_odd, one, two)
    wide[:, pl.ds(span + 2 * CELLS, CELLS)] = jnp.where(lon_odd, two, one)
    rim_span = PATCHES * COLS
    blank = jnp.zeros((MEMBERS, COLS), BF16)
    wide_rim[:, pl.ds(0, COLS)] = blank
    wide_rim[:, pl.ds(rim_span + 3 * COLS, COLS)] = blank
    wide_rim[:, pl.ds(2 * COLS, rim_span)] = rim_ref[...]
    one = first_ref[pl.ds(0, MEMBERS), pl.ds(CELLS, COLS)]
    two = second_ref[pl.ds(0, MEMBERS), pl.ds(CELLS, COLS)]
    wide_rim[:, pl.ds(COLS, COLS)] = jnp.where(lon_odd, one, two)
    wide_rim[:, pl.ds(rim_span + 2 * COLS, COLS)] = jnp.where(lon_odd, two, one)

    lane = lax.broadcasted_iota(jnp.int32, (1, CELLS), 1)
    row = lane >> 4
    last = lax.axis_size("lat") - 1
    short = ((row == 0) & (lat == 0)) | ((row == ROWS - 1) & (lat == last))
    share = jnp.where(short, 1.0 / 6.0, 1.0 / 9.0)
    tail_row = lax.broadcasted_iota(jnp.int32, (EXTRA, CELLS), 0)
    for e in range(PATCHES + 2):
        summed = jnp.dot(
            wide[pl.ds(0, MEMBERS), pl.ds(e * CELLS, 3 * CELLS)], main_ref[...], preferred_element_type=F32
        )
        summed = summed + jnp.dot(
            wide_rim[:, pl.ds(e * COLS, 3 * COLS)], edge_ref[...], preferred_element_type=F32
        )
        mean = summed * share
        average = jnp.sum(mean, axis=0, keepdims=True) * (1.0 / MEMBERS)
        pert[pl.ds(0, MEMBERS), pl.ds(e * CELLS, CELLS)] = (mean - average).astype(BF16)
        tail = wide[pl.ds(MEMBERS, EXTRA), pl.ds((e + 1) * CELLS, CELLS)].astype(F32)
        innovation = tail[1:2] - average
        pert[pl.ds(MEMBERS, EXTRA), pl.ds(e * CELLS, CELLS)] = jnp.where(
            tail_row == 0, innovation, 0.0
        ).astype(BF16)

    r = lax.broadcasted_iota(jnp.int32, (MEMBERS, MEMBERS), 0)
    c = lax.broadcasted_iota(jnp.int32, (MEMBERS, MEMBERS), 1)
    lower = r >= c
    same = r == c
    base = (PATCHES // 2) * MEMBERS
    tails = [[], [], []]
    diagonals = [[], [], []]
    for pair in range(PATCHES // 2):
        kept = [None, None, None]
        for p in (2 * pair, 2 * pair + 1):
            window = pert[:, pl.ds(p * CELLS, 3 * CELLS)]
            members = window[:MEMBERS].astype(F32)
            precision = wide[pl.ds(MEMBERS, EXTRA), pl.ds((p + 1) * CELLS, 3 * CELLS)].astype(F32)[0:1]
            for s in range(3):
                weight = precision * taper_ref[s : s + 1, :]
                scaled = (members * weight).astype(BF16)
                full = lax.dot_general(scaled, window, NT, preferred_element_type=F32)
                gram = full[:, :MEMBERS]
                forcing = jnp.sum(jnp.where(same, full[:, MEMBERS : MEMBERS + 1], 0.0), axis=0, keepdims=True)
                tails[s].append(forcing)
                if s == 1:
                    gram_ref[p] = gram
                elif p == 2 * pair:
                    kept[s] = gram
                else:
                    diagonals[s].append(jnp.sum(jnp.where(same, gram, 0.0), axis=0, keepdims=True))
                    kept[s] = jnp.where(lower, kept[s], gram)
        even_ref[pl.ds(pair * MEMBERS, MEMBERS), :] = jnp.where(lat_odd, kept[0], kept[2]).astype(BF16)
        odd_ref[pl.ds(pair * MEMBERS, MEMBERS), :] = jnp.where(lat_odd, kept[2], kept[0]).astype(BF16)
    force_ref[...] = jnp.concatenate(tails[1], axis=0)
    gap = [jnp.zeros((4, MEMBERS), F32)]
    up = jnp.concatenate(tails[0] + diagonals[0] + gap, axis=0)
    down = jnp.concatenate(tails[2] + diagonals[2] + gap, axis=0)
    even_ref[pl.ds(base, 16), :] = jnp.where(lat_odd, up, down).astype(BF16)
    odd_ref[pl.ds(base, 16), :] = jnp.where(lat_odd, down, up).astype(BF16)


def split(a):
    high = a.astype(BF16)
    return high, (a - high.astype(F32)).astype(BF16)


def product(a, b):
    a_high, a_low = split(a)
    b_high, b_low = split(b)
    wide = jnp.concatenate([b_high, b_low], axis=1)
    out = jnp.dot(
        jnp.concatenate([a_high, a_low], axis=1),
        jnp.concatenate([wide, wide], axis=0),
        preferred_element_type=F32,
    )
    return out[:, :MEMBERS] + out[:, MEMBERS:]


def solve_kernel(first_ref, second_ref, gram_ref, force_ref, field_ref, blocks_ref, mask_ref, out_ref,
                 upper, lower_ref, soil, scratch, spread):
    to_blocks(field_ref, 0, soil, scratch)
    r = lax.broadcasted_iota(jnp.int32, (MEMBERS, MEMBERS), 0)
    c = lax.broadcasted_iota(jnp.int32, (MEMBERS, MEMBERS), 1)
    eye = jnp.where(r == c, 1.0, 0.0)
    base = (PATCHES // 2) * MEMBERS
    tail = first_ref[pl.ds(base, 16), :].astype(F32) + second_ref[pl.ds(base, 16), :].astype(F32)
    norms = []
    for pair in range(PATCHES // 2):
        rows = pl.ds(pair * MEMBERS, MEMBERS)
        mixed = first_ref[rows, :].astype(F32) + second_ref[rows, :].astype(F32)
        turned = mixed.T
        diagonal = tail[8 + pair : 9 + pair]
        gains = (
            jnp.where(r >= c, mixed, turned),
            jnp.where(r > c, turned, jnp.where(r < c, mixed, diagonal)),
        )
        for k in range(2):
            p = 2 * pair + k
            system = (MEMBERS - 1.0) * eye + (gram_ref[p] + gains[k])
            total = jnp.sum(jnp.sum(system * system, axis=0, keepdims=True), axis=1, keepdims=True)
            norm = jnp.sqrt(total)
            norms.append(norm)
            scaled = system * (1.0 / norm)
            upper[p] = 1.5 * scaled - 0.5 * product(scaled, scaled)
            lower_ref[p] = 1.5 * eye - 0.5 * scaled

    def sweep(_, carry):
        middles = [1.5 * eye - 0.5 * product(lower_ref[p], upper[p]) for p in range(PATCHES)]
        for p in range(PATCHES):
            both = product(jnp.concatenate([upper[p], lower_ref[p]], axis=0), middles[p])
            upper[p] = both[:MEMBERS]
            lower_ref[p] = both[MEMBERS:]
        return carry

    lax.fori_loop(0, NS_ITERS - 2, sweep, 0)
    for p in range(PATCHES):
        middle = 1.5 * eye - 0.5 * product(lower_ref[p], upper[p])
        lower = product(lower_ref[p], middle)
        forcing = jnp.broadcast_to(force_ref[p : p + 1] + tail[p : p + 1], (16, MEMBERS))
        mean_weight = product(product(forcing, lower), lower)[0:1] * (1.0 / norms[p])
        scale = jnp.sqrt(MEMBERS - 1.0) / jnp.sqrt(norms[p])
        transform = (lower * scale + mean_weight).astype(BF16)
        cells = pl.ds(p * CELLS, CELLS)
        raw = jnp.concatenate([blocks_ref[pl.ds(0, MEMBERS), cells], soil[:, cells]], axis=1).astype(F32)
        mean = jnp.sum(raw, axis=0, keepdims=True) * (1.0 / MEMBERS)
        departure = (raw - mean).astype(BF16)
        updated = mean + jnp.dot(transform, departure, preferred_element_type=F32)
        land = mask_ref[p : p + 1, :]
        keep = jnp.concatenate([land, land], axis=1) != 0.0
        spread[:, pl.ds(p * 2 * CELLS, 2 * CELLS)] = jnp.where(keep, updated, raw)

    for v in range(2):
        for m in range(MEMBERS // 16):
            rows = pl.ds(m * 16, 16)
            for g in range(2):
                groups = [
                    spread[rows, pl.ds(b * 2 * CELLS + v * CELLS + g * COLS, COLS)] for b in range(PATCHES)
                ]
                lines = swap_groups(groups)
                for k in range(8):
                    scratch[pl.ds(m * 256 + g * 8 + k, 16, stride=16), :] = lines[k]
            out_ref[v, rows] = scratch[pl.ds(m * 256, 256), :].reshape(16, ROWS, COLS).astype(BF16)


def call(kernel, out_shape, scratch, flops, moved, *operands, in_specs=None):
    vmem = pl.BlockSpec(memory_space=pltpu.VMEM)
    return pl.pallas_call(
        kernel,
        out_shape=out_shape,
        grid=(1,),
        in_specs=in_specs or [vmem] * len(operands),
        out_specs=[vmem] * len(out_shape),
        scratch_shapes=scratch,
        compiler_params=pltpu.CompilerParams(vmem_limit_bytes=VMEM_LIMIT),
        cost_estimate=pl.CostEstimate(flops=flops, bytes_accessed=moved, transcendentals=0),
    )(*operands)


def pairs_inside(size):
    return [(i, i ^ 1) for i in range(size)]


def pairs_across(size, wrap):
    pairs = []
    for i in range(1, size - 1, 2):
        pairs += [(i, i + 1), (i + 1, i)]
    if wrap:
        pairs += [(size - 1, 0), (0, size - 1)]
    return pairs


def exchange(even, odd, axis, wrap):
    size = lax.axis_size(axis)
    return (
        lax.ppermute(even, axis, pairs_inside(size)),
        lax.ppermute(odd, axis, pairs_across(size, wrap)),
    )


def body(background, obs_cell, obs_count, obs_value, obs_err, land):
    vmem = pl.BlockSpec(memory_space=pltpu.VMEM)
    smem = pl.BlockSpec(memory_space=pltpu.SMEM)
    slots = obs_cell.shape[-1]
    span = PATCHES * CELLS
    shape = jax.ShapeDtypeStruct
    lat_odd = (lax.axis_index("lat") & 1) == 1
    top, bottom = background[0, :, 0], background[0, :, ROWS - 1]
    rows = exchange(
        jnp.where(lat_odd, top, bottom), jnp.where(lat_odd, bottom, top), "lat", False
    )
    blocks, mask = call(
        layout_kernel,
        [shape((CHANNELS, span), BF16), shape((8, CELLS), F32)],
        [pltpu.VMEM((MEMBERS * ROWS, COLS), F32)],
        10**7, 2 * 10**6,
        background, obs_cell.reshape(1, slots), obs_count, obs_value.reshape(1, slots),
        obs_err.reshape(1, slots), land,
        in_specs=[pl.BlockSpec((1, MEMBERS, ROWS, COLS), lambda i: (0, 0, 0, 0)), vmem, smem, vmem, vmem, vmem],
    )
    rim, even, odd = call(
        rim_kernel,
        [shape((MEMBERS, PATCHES * COLS), BF16)] + [shape((CHANNELS, CELLS + COLS), BF16)] * 2,
        [], 10**6, 10**6, *rows, blocks,
    )
    sides = exchange(even, odd, "lon", True)
    main, edge = stencil_tables()
    even, odd, gram, force = call(
        gram_kernel,
        [shape((PACKED, MEMBERS), BF16)] * 2
        + [shape((PATCHES, MEMBERS, MEMBERS), F32), shape((PATCHES, MEMBERS), F32)],
        [
            pltpu.VMEM((CHANNELS, span + 4 * CELLS), BF16),
            pltpu.VMEM((MEMBERS, (PATCHES + 4) * COLS), BF16),
            pltpu.VMEM((CHANNELS, span + 2 * CELLS), BF16),
        ],
        10**9, 3 * 10**6,
        blocks, rim, *sides, jnp.asarray(taper_table()), jnp.asarray(main, BF16), jnp.asarray(edge, BF16),
    )
    packed = exchange(even, odd, "lat", False)
    (analysis,) = call(
        solve_kernel,
        [shape(background.shape, BF16)],
        [
            pltpu.VMEM((PATCHES, MEMBERS, MEMBERS), F32),
            pltpu.VMEM((PATCHES, MEMBERS, MEMBERS), F32),
            pltpu.VMEM((MEMBERS, span), BF16),
            pltpu.VMEM((MEMBERS * ROWS, COLS), F32),
            pltpu.VMEM((MEMBERS, 2 * span), F32),
        ],
        2 * 10**9, 5 * 10**6,
        *packed, gram, force, background, blocks, mask,
        in_specs=[vmem] * 4 + [pl.BlockSpec((1, MEMBERS, ROWS, COLS), lambda i: (1, 0, 0, 0)), vmem, vmem],
    )
    return analysis


def solution(mesh):
    return jax.shard_map(
        body,
        mesh=mesh,
        in_specs=(
            P(None, None, "lat", "lon"),
            P("lat", "lon", None),
            P("lat", "lon"),
            P("lat", "lon", None),
            P("lat", "lon", None),
            P("lat", "lon"),
        ),
        out_specs=P(None, None, "lat", "lon"),
        check_vma=False,
    )
```

```python
import jax
import jax.numpy as jnp
import numpy as np
from jax import lax
from jax.experimental import pallas as pl
from jax.experimental.pallas import tpu as pltpu
from jax.sharding import PartitionSpec as P

MEMBERS = 128
PATCH = 16
RADIUS = 15
NS_ITERS = 5
ROWS = 16
COLS = 128
PATCHES = COLS // PATCH
CELLS = PATCH * PATCH
EXTRA = 16
CHANNELS = MEMBERS + EXTRA
PACKED = (PATCHES // 2) * MEMBERS + 16
NT = (((1,), (1,)), ((), ()))
PARTS = 4
VMEM_LIMIT = 48 * 1024 * 1024
F32 = jnp.float32
BF16 = jnp.bfloat16


def tapers():
    lane = lax.broadcasted_iota(jnp.int32, (1, 3 * CELLS), 1)
    side = lane >> 8
    row, column = (lane >> 4) & (PATCH - 1), lane & (PATCH - 1)
    span = 2.0 * (RADIUS + PATCH / 2.0)
    half = (PATCH - 1) / 2.0

    def line(place, shift):
        offset = jnp.abs(place.astype(F32) + (PATCH * shift - half))
        return jnp.where(offset < RADIUS + PATCH / 2.0, 1.0 - offset / span, 0.0)

    lon = jnp.where(side == 0, line(column, -1), jnp.where(side == 1, line(column, 0), line(column, 1)))
    return [line(row, shift) * lon for shift in (1, 0, -1)]


def stencil_rows(first):
    cell = first + lax.broadcasted_iota(jnp.int32, (COLS, CELLS), 0)
    lane = lax.broadcasted_iota(jnp.int32, (COLS, CELLS), 1)
    row, column = lane >> 4, lane & (PATCH - 1)
    if first < 3 * CELLS:
        side = first // CELLS - 1
        place = ((cell & (CELLS - 1)) >> 4) - row
        near = jnp.abs(place) <= 1
    else:
        side = (first - 3 * CELLS) // COLS - 1
        slot = (cell & (COLS - 1)) >> 4
        near = ((slot == 0) & (row == 0)) | ((slot == 1) & (row == ROWS - 1))
    beside = jnp.abs(side * PATCH + (cell & (PATCH - 1)) - column) <= 1
    return jnp.where(near & beside, 1.0, 0.0).astype(BF16)


def swap_groups(arrays):
    lane = lax.broadcasted_iota(jnp.int32, arrays[0].shape, 1)
    for step in (1, 2, 4):
        width = PATCH * step
        high = (lane & width) != 0
        mixed = list(arrays)
        for i in range(8):
            if i & step == 0:
                first, second = arrays[i], arrays[i + step]
                mixed[i] = jnp.where(high, pltpu.roll(second, width, 1), first)
                mixed[i + step] = jnp.where(high, second, pltpu.roll(first, COLS - width, 1))
        arrays = mixed
    return arrays


def fetch(source, target, sem):
    copy = pltpu.make_async_copy(source, target, sem)
    copy.start()
    return copy


def fetch_field(background_ref, variable, held, sems):
    part = MEMBERS // PARTS
    return [
        fetch(
            background_ref.at[variable, pl.ds(k * part, part)], held.at[pl.ds(k * part, part)], sems.at[k]
        )
        for k in range(PARTS)
    ]


def widen_lines(copies, held, lines):
    part = MEMBERS // PARTS
    for k in range(PARTS):
        if copies:
            copies[k].wait()
        for m in range(k * part // 16, (k + 1) * part // 16):
            piece = held[pl.ds(m * 16, 16)].astype(F32)
            lines[pl.ds(m * 256, 256), :] = piece.reshape(256, COLS)


def to_blocks(lines, out_ref):
    for m in range(MEMBERS // 16):
        halves = []
        for g in range(2):
            rows = [lines[pl.ds(m * 256 + g * 8 + r, 16, stride=16), :] for r in range(8)]
            halves.append(swap_groups(rows))
        for b in range(PATCHES):
            both = jnp.concatenate([halves[0][b], halves[1][b]], axis=1)
            out_ref[pl.ds(m * 16, 16), pl.ds(b * CELLS, CELLS)] = both.astype(BF16)


def strip_kernel(background_ref, pack_ref, land_ref, held, sides_ref, tails_ref, mask_ref, lines, sems):
    copies = fetch_field(background_ref, 0, held, sems)
    land = land_ref[...].astype(F32)
    halves = []
    for g in range(2):
        rows = [jnp.broadcast_to(land[g * 8 + r : g * 8 + r + 1], (8, COLS)) for r in range(8)]
        halves.append(swap_groups(rows))
    which = lax.broadcasted_iota(jnp.int32, (8, CELLS), 0)
    mask = jnp.zeros((8, CELLS), F32)
    for b in range(PATCHES):
        mask = jnp.where(which == b, jnp.concatenate([halves[0][b], halves[1][b]], axis=1), mask)
    mask_ref[...] = mask
    pack = pack_ref[...]
    slots = pack.shape[1]
    cell, value, err, count = (pack[k : k + 1] for k in range(4))
    cell = cell.astype(jnp.int32)
    used = lax.broadcasted_iota(jnp.int32, (1, slots), 1) < count.astype(jnp.int32)
    inverse = jnp.where(used, 1.0 / (err * err), 0.0)
    value = jnp.where(used, value, 0.0)
    column = cell & (COLS - 1)
    block = column >> 4
    place = ((cell >> 7) << 4) + (column & (PATCH - 1))
    slot_block = lax.broadcasted_iota(jnp.int32, (16, value.shape[1]), 0)
    chosen = (slot_block & 7) == block
    amount = jnp.where(slot_block < 8, inverse, value)
    left = jnp.where(chosen, amount, 0.0).astype(BF16)
    spot = lax.broadcasted_iota(jnp.int32, (CELLS, value.shape[1]), 0) == place
    right = jnp.where(spot, 1.0, 0.0).astype(BF16)
    grids = lax.dot_general(left, right, NT, preferred_element_type=F32)
    precision = grids[:8] * mask
    observed = grids[8:]
    channel = lax.broadcasted_iota(jnp.int32, (EXTRA, CELLS), 0)
    for b in range(PATCHES):
        tail = jnp.where(
            channel == 0, precision[b : b + 1], jnp.where(channel == 1, observed[b : b + 1], 0.0)
        ).astype(BF16)
        tails_ref[:, pl.ds(b * CELLS, CELLS)] = tail
        if b == 0:
            sides_ref[pl.ds(MEMBERS, EXTRA), pl.ds(0, CELLS)] = tail
        if b == PATCHES - 1:
            sides_ref[pl.ds(MEMBERS, EXTRA), pl.ds(CELLS, CELLS)] = tail

    widen_lines(copies, held, lines)
    group = lax.broadcasted_iota(jnp.int32, (16, COLS), 1) >> 4
    for m in range(MEMBERS // 16):
        for g in range(2):
            west = jnp.zeros((16, COLS), F32)
            east = west
            for r in range(8):
                row = lines[pl.ds(m * 256 + g * 8 + r, 16, stride=16), :]
                here = group == r
                west = jnp.where(here, pltpu.roll(row, PATCH * r, 1) if r else row, west)
                east = jnp.where(here, pltpu.roll(row, PATCH * (r + 1), 1) if r < 7 else row, east)
            sides_ref[pl.ds(m * 16, 16), pl.ds(g * COLS, COLS)] = west.astype(BF16)
            sides_ref[pl.ds(m * 16, 16), pl.ds(CELLS + g * COLS, COLS)] = east.astype(BF16)


def block_kernel(held, tails_ref, blocks_ref, table_ref, lines):
    for first in range(0, 3 * (CELLS + COLS), COLS):
        table_ref[pl.ds(first, COLS), :] = stencil_rows(first)
    widen_lines((), held, lines)
    to_blocks(lines, blocks_ref)
    blocks_ref[pl.ds(MEMBERS, EXTRA), :] = tails_ref[...]


def rim_kernel(first_ref, second_ref, sides_ref, rim_ref, even_ref, odd_ref):
    lat_odd = (lax.axis_index("lat") & 1) == 1
    lon_odd = (lax.axis_index("lon") & 1) == 1
    first = first_ref[...].astype(F32)
    second = second_ref[...].astype(F32)
    above = jnp.where(lat_odd, first, second)
    below = jnp.where(lat_odd, second, first)
    lane = lax.broadcasted_iota(jnp.int32, (MEMBERS, COLS), 1)
    for b in range(PATCHES):
        top = pltpu.roll(above, (COLS - PATCH * b) % COLS, 1)
        low = pltpu.roll(below, (COLS - PATCH * b + PATCH) % COLS, 1)
        edge = jnp.where(lane < PATCH, top, jnp.where(lane < 2 * PATCH, low, 0.0)).astype(BF16)
        rim_ref[:, pl.ds(b * COLS, COLS)] = edge
        if b == 0:
            west_rim = edge
        if b == PATCHES - 1:
            east_rim = edge
    west = sides_ref[:, pl.ds(0, CELLS)]
    east = sides_ref[:, pl.ds(CELLS, CELLS)]
    even_ref[:, pl.ds(0, CELLS)] = jnp.where(lon_odd, west, east)
    odd_ref[:, pl.ds(0, CELLS)] = jnp.where(lon_odd, east, west)
    even_ref[pl.ds(0, MEMBERS), pl.ds(CELLS, COLS)] = jnp.where(lon_odd, west_rim, east_rim)
    odd_ref[pl.ds(0, MEMBERS), pl.ds(CELLS, COLS)] = jnp.where(lon_odd, east_rim, west_rim)
    blank = jnp.zeros((EXTRA, COLS), BF16)
    even_ref[pl.ds(MEMBERS, EXTRA), pl.ds(CELLS, COLS)] = blank
    odd_ref[pl.ds(MEMBERS, EXTRA), pl.ds(CELLS, COLS)] = blank


def gram_kernel(
    blocks_ref, rim_ref, first_ref, second_ref, table_ref,
    even_ref, odd_ref, pert, wide, wide_rim,
):
    lat = lax.axis_index("lat")
    lat_odd = (lat & 1) == 1
    lon_odd = (lax.axis_index("lon") & 1) == 1
    span = PATCHES * CELLS
    wide[:, pl.ds(0, CELLS)] = jnp.zeros((CHANNELS, CELLS), BF16)
    wide[:, pl.ds(span + 3 * CELLS, CELLS)] = jnp.zeros((CHANNELS, CELLS), BF16)
    wide[:, pl.ds(2 * CELLS, span)] = blocks_ref[...]
    one = first_ref[:, pl.ds(0, CELLS)]
    two = second_ref[:, pl.ds(0, CELLS)]
    wide[:, pl.ds(CELLS, CELLS)] = jnp.where(lon_odd, one, two)
    wide[:, pl.ds(span + 2 * CELLS, CELLS)] = jnp.where(lon_odd, two, one)
    rim_span = PATCHES * COLS
    blank = jnp.zeros((MEMBERS, COLS), BF16)
    wide_rim[:, pl.ds(0, COLS)] = blank
    wide_rim[:, pl.ds(rim_span + 3 * COLS, COLS)] = blank
    wide_rim[:, pl.ds(2 * COLS, rim_span)] = rim_ref[...]
    one = first_ref[pl.ds(0, MEMBERS), pl.ds(CELLS, COLS)]
    two = second_ref[pl.ds(0, MEMBERS), pl.ds(CELLS, COLS)]
    wide_rim[:, pl.ds(COLS, COLS)] = jnp.where(lon_odd, one, two)
    wide_rim[:, pl.ds(rim_span + 2 * COLS, COLS)] = jnp.where(lon_odd, two, one)

    lane = lax.broadcasted_iota(jnp.int32, (1, CELLS), 1)
    row = lane >> 4
    last = lax.axis_size("lat") - 1
    short = ((row == 0) & (lat == 0)) | ((row == ROWS - 1) & (lat == last))
    share = jnp.where(short, 1.0 / 6.0, 1.0 / 9.0)
    tail_row = lax.broadcasted_iota(jnp.int32, (EXTRA, CELLS), 0)
    for e in range(PATCHES + 2):
        summed = jnp.dot(
            wide[pl.ds(0, MEMBERS), pl.ds(e * CELLS, 3 * CELLS)], table_ref[pl.ds(0, 3 * CELLS), :], preferred_element_type=F32
        )
        summed = summed + jnp.dot(
            wide_rim[:, pl.ds(e * COLS, 3 * COLS)], table_ref[pl.ds(3 * CELLS, 3 * COLS), :], preferred_element_type=F32
        )
        mean = summed * share
        average = jnp.sum(mean, axis=0, keepdims=True) * (1.0 / MEMBERS)
        pert[pl.ds(0, MEMBERS), pl.ds(e * CELLS, CELLS)] = (mean - average).astype(BF16)
        tail = wide[pl.ds(MEMBERS, EXTRA), pl.ds((e + 1) * CELLS, CELLS)].astype(F32)
        innovation = tail[1:2] - average
        pert[pl.ds(MEMBERS, EXTRA), pl.ds(e * CELLS, CELLS)] = jnp.where(
            tail_row == 0, innovation, jnp.where(tail_row == 1, tail[0:1], 0.0)
        ).astype(BF16)

    r = lax.broadcasted_iota(jnp.int32, (MEMBERS, MEMBERS), 0)
    c = lax.broadcasted_iota(jnp.int32, (MEMBERS, MEMBERS), 1)
    lower = r >= c
    same = r == c
    base = (PATCHES // 2) * MEMBERS
    above, _, below = tapers()
    for out_ref, near, far in ((even_ref, above, below), (odd_ref, below, above)):
        taper = jnp.where(lat_odd, near, far)
        forcings, diagonals = [], []
        for pair in range(PATCHES // 2):
            first, forcing = patch_gram(pert, 2 * pair, taper, same)
            forcings.append(forcing)
            second, forcing = patch_gram(pert, 2 * pair + 1, taper, same)
            forcings.append(forcing)
            diagonals.append(jnp.sum(jnp.where(same, second, 0.0), axis=0, keepdims=True))
            out_ref[pl.ds(pair * MEMBERS, MEMBERS), :] = jnp.where(lower, first, second).astype(BF16)
        tail = forcings + diagonals + [jnp.zeros((4, MEMBERS), F32)]
        out_ref[pl.ds(base, 16), :] = jnp.concatenate(tail, axis=0).astype(BF16)


def patch_gram(pert, p, taper, same):
    window = pert[:, pl.ds(p * CELLS, 3 * CELLS)]
    precision = window[MEMBERS:].astype(F32)[1:2]
    scaled = (window[:MEMBERS].astype(F32) * (precision * taper)).astype(BF16)
    full = lax.dot_general(scaled, window, NT, preferred_element_type=F32)
    forcing = jnp.sum(jnp.where(same, full[:, MEMBERS : MEMBERS + 1], 0.0), axis=0, keepdims=True)
    return full[:, :MEMBERS], forcing


def centre_kernel(pert, blocks_ref, background_ref, mask_ref,
                  gram_ref, force_ref, departure_ref, base_ref, soil, held, lines, sems):
    copies = fetch_field(background_ref, 1, held, sems)
    r = lax.broadcasted_iota(jnp.int32, (MEMBERS, MEMBERS), 0)
    c = lax.broadcasted_iota(jnp.int32, (MEMBERS, MEMBERS), 1)
    same = r == c
    taper = tapers()[1]
    forcings = []
    for p in range(PATCHES):
        gram, forcing = patch_gram(pert, p, taper, same)
        gram_ref[p] = gram + jnp.where(same, MEMBERS - 1.0, 0.0)
        forcings.append(forcing)
    force_ref[...] = jnp.concatenate(forcings, axis=0)
    widen_lines(copies, held, lines)
    to_blocks(lines, soil)
    for p in range(PATCHES):
        cells = pl.ds(p * CELLS, CELLS)
        land = mask_ref[p : p + 1, :] != 0.0
        for v, raw in enumerate((blocks_ref[pl.ds(0, MEMBERS), cells], soil[:, cells])):
            raw = raw.astype(F32)
            mean = jnp.sum(raw, axis=0, keepdims=True) * (1.0 / MEMBERS)
            place = pl.ds((2 * p + v) * CELLS, CELLS)
            departure_ref[:, place] = jnp.where(land, raw - mean, 0.0).astype(BF16)
            base_ref[:, place] = jnp.where(land, mean, raw)


def split(a):
    high = a.astype(BF16)
    return high, (a - high.astype(F32)).astype(BF16)


def product(a, b):
    a_high, a_low = split(a)
    b_high, b_low = split(b)
    wide = jnp.concatenate([b_high, b_low], axis=1)
    out = jnp.dot(
        jnp.concatenate([a_high, a_low], axis=1),
        jnp.concatenate([wide, wide], axis=0),
        preferred_element_type=F32,
    )
    return out[:, :MEMBERS] + out[:, MEMBERS:]


def halves(a):
    return jnp.concatenate(split(a), axis=1)


def product(a, b):
    out = jnp.dot(a, jnp.concatenate([b, b], axis=0), preferred_element_type=F32)
    return out[:, :MEMBERS] + out[:, MEMBERS:]


def solve_kernel(first_ref, second_ref, gram_ref, force_ref, departure_ref, base_ref, out_ref,
                 pair_ref, scratch, spread, held, sems):
    r = lax.broadcasted_iota(jnp.int32, (MEMBERS, MEMBERS), 0)
    c = lax.broadcasted_iota(jnp.int32, (MEMBERS, MEMBERS), 1)
    eye = jnp.where(r == c, 1.0, 0.0)
    base = (PATCHES // 2) * MEMBERS
    tail = first_ref[pl.ds(base, 16), :].astype(F32) + second_ref[pl.ds(base, 16), :].astype(F32)
    norms = []
    for pair in range(PATCHES // 2):
        rows = pl.ds(pair * MEMBERS, MEMBERS)
        mixed = first_ref[rows, :].astype(F32) + second_ref[rows, :].astype(F32)
        turned = mixed.T
        diagonal = tail[8 + pair : 9 + pair]
        gains = (
            jnp.where(r >= c, mixed, turned),
            jnp.where(r > c, turned, jnp.where(r < c, mixed, diagonal)),
        )
        for k in range(2):
            p = 2 * pair + k
            system = gram_ref[p] + gains[k]
            total = jnp.sum(jnp.sum(system * system, axis=0, keepdims=True), axis=1, keepdims=True)
            norm = jnp.sqrt(total)
            norms.append(norm)
            scaled = system * (1.0 / norm)
            split_scaled = halves(scaled)
            pair_ref[p, :MEMBERS] = halves(1.5 * scaled - 0.5 * product(split_scaled, split_scaled))
            pair_ref[p, MEMBERS:] = halves(1.5 * eye - 0.5 * scaled)

    def sweep(_, carry):
        middles = [
            halves(1.5 * eye - 0.5 * product(pair_ref[p, MEMBERS:], pair_ref[p, :MEMBERS]))
            for p in range(PATCHES)
        ]
        for p in range(PATCHES):
            pair_ref[p] = halves(product(pair_ref[p], middles[p]))
        return carry

    lax.fori_loop(0, NS_ITERS - 2, sweep, 0)
    middles = [
        halves(1.5 * eye - 0.5 * product(pair_ref[p, MEMBERS:], pair_ref[p, :MEMBERS]))
        for p in range(PATCHES)
    ]
    for p in range(PATCHES):
        lower = product(pair_ref[p, MEMBERS:], middles[p])
        split_lower = halves(lower)
        forcing = jnp.broadcast_to(force_ref[p : p + 1] + tail[p : p + 1], (16, MEMBERS))
        once = product(halves(forcing), split_lower)
        mean_weight = product(halves(once), split_lower)[0:1] * (1.0 / norms[p])
        scale = jnp.sqrt(MEMBERS - 1.0) / jnp.sqrt(norms[p])
        transform = (lower * scale + mean_weight).astype(BF16)
        cells = pl.ds(p * 2 * CELLS, 2 * CELLS)
        spread[:, cells] = base_ref[:, cells] + jnp.dot(
            transform, departure_ref[:, cells], preferred_element_type=F32
        )

    copies = []
    for v in range(2):
        for m in range(MEMBERS // 16):
            rows = pl.ds(m * 16, 16)
            for g in range(2):
                groups = [
                    spread[rows, pl.ds(b * 2 * CELLS + v * CELLS + g * COLS, COLS)] for b in range(PATCHES)
                ]
                lines = swap_groups(groups)
                for k in range(8):
                    scratch[pl.ds(m * 256 + g * 8 + k, 16, stride=16), :] = lines[k]
            held[v, rows] = scratch[pl.ds(m * 256, 256), :].reshape(16, ROWS, COLS).astype(BF16)
            copies.append(fetch(held.at[v, rows], out_ref.at[v, rows], sems.at[v * (MEMBERS // 16) + m]))
    for copy in copies:
        copy.wait()


LIMITS = {strip_kernel: 53 * 1024 * 1024}


def call(kernel, out_shape, scratch, flops, moved, *operands, far=(), scalars=(), out_far=False):
    vmem = pl.BlockSpec(memory_space=pltpu.VMEM)
    smem = pl.BlockSpec(memory_space=pltpu.SMEM)
    anywhere = pl.BlockSpec(memory_space=pltpu.HBM)
    return pl.pallas_call(
        kernel,
        out_shape=out_shape,
        in_specs=[
            anywhere if i in far else smem if i in scalars else vmem for i in range(len(operands))
        ],
        out_specs=[anywhere if out_far else vmem] * len(out_shape),
        scratch_shapes=scratch,
        compiler_params=pltpu.CompilerParams(vmem_limit_bytes=LIMITS.get(kernel, VMEM_LIMIT)),
        cost_estimate=pl.CostEstimate(flops=flops, bytes_accessed=moved, transcendentals=0),
    )(*operands)


def pairs_inside(size):
    return [(i, i ^ 1) for i in range(size)]


def pairs_across(size, wrap):
    pairs = []
    for i in range(1, size - 1, 2):
        pairs += [(i, i + 1), (i + 1, i)]
    if wrap:
        pairs += [(size - 1, 0), (0, size - 1)]
    return pairs


def exchange(even, odd, axis, wrap):
    size = lax.axis_size(axis)
    return (
        lax.ppermute(even, axis, pairs_inside(size)),
        lax.ppermute(odd, axis, pairs_across(size, wrap)),
    )


def body(background, obs_cell, obs_count, obs_value, obs_err, land):
    slots = obs_cell.shape[-1]
    span = PATCHES * CELLS
    shape = jax.ShapeDtypeStruct
    field = pltpu.VMEM((MEMBERS, ROWS, COLS), BF16)
    lines_shape = (MEMBERS * ROWS, COLS)
    copies = pltpu.SemaphoreType.DMA
    lat_odd = (lax.axis_index("lat") & 1) == 1
    line = lax.broadcasted_iota(jnp.int32, (8, slots), 0)
    pack = jnp.zeros((8, slots), F32)
    for k, array in enumerate((obs_cell, obs_value, obs_err, obs_count)):
        pack = jnp.where(line == k, array.reshape(1, -1).astype(F32), pack)
    top, bottom = background[0, :, 0], background[0, :, ROWS - 1]
    rows = exchange(
        jnp.where(lat_odd, top, bottom), jnp.where(lat_odd, bottom, top), "lat", False
    )
    held, sides, tails, mask = call(
        strip_kernel,
        [
            shape((MEMBERS, ROWS, COLS), BF16),
            shape((CHANNELS, 2 * CELLS), BF16),
            shape((EXTRA, span), BF16),
            shape((8, CELLS), F32),
        ],
        [pltpu.VMEM(lines_shape, F32), copies((PARTS,))],
        10**7, 2 * 10**6,
        background, pack, land,
        far=(0,),
    )
    rim, even, odd = call(
        rim_kernel,
        [shape((MEMBERS, PATCHES * COLS), BF16)] + [shape((CHANNELS, CELLS + COLS), BF16)] * 2,
        [], 10**6, 10**6, *rows, sides,
    )
    neighbours = exchange(even, odd, "lon", True)
    blocks, table = call(
        block_kernel,
        [shape((CHANNELS, span), BF16), shape((3 * (CELLS + COLS), CELLS), BF16)],
        [pltpu.VMEM(lines_shape, F32)],
        10**8, 4 * 10**6,
        held, tails,
    )
    even, odd, pert = call(
        gram_kernel,
        [shape((PACKED, MEMBERS), BF16)] * 2 + [shape((CHANNELS, span + 2 * CELLS), BF16)],
        [
            pltpu.VMEM((CHANNELS, span + 4 * CELLS), BF16),
            pltpu.VMEM((MEMBERS, (PATCHES + 4) * COLS), BF16),
        ],
        10**9, 3 * 10**6,
        blocks, rim, *neighbours, table,
    )
    packed = exchange(even, odd, "lat", False)
    gram, force, departure, base = call(
        centre_kernel,
        [
            shape((PATCHES, MEMBERS, MEMBERS), F32),
            shape((PATCHES, MEMBERS), F32),
            shape((MEMBERS, 2 * span), BF16),
            shape((MEMBERS, 2 * span), F32),
        ],
        [pltpu.VMEM((MEMBERS, span), BF16), field, pltpu.VMEM(lines_shape, F32), copies((PARTS,))],
        10**9, 5 * 10**6,
        pert, blocks, background, mask,
        far=(2,),
    )
    (analysis,) = call(
        solve_kernel,
        [shape(background.shape, BF16)],
        [
            pltpu.VMEM((PATCHES, 2 * MEMBERS, 2 * MEMBERS), BF16),
            pltpu.VMEM(lines_shape, F32),
            pltpu.VMEM((MEMBERS, 2 * span), F32),
            pltpu.VMEM(background.shape, BF16),
            copies((2 * MEMBERS // 16,)),
        ],
        2 * 10**9, 5 * 10**6,
        *packed, gram, force, departure, base,
        out_far=True,
    )
    return analysis


def solution(mesh):
    return jax.shard_map(
        body,
        mesh=mesh,
        in_specs=(
            P(None, None, "lat", "lon"),
            P("lat", "lon", None),
            P("lat", "lon"),
            P("lat", "lon", None),
            P("lat", "lon", None),
            P("lat", "lon"),
        ),
        out_specs=P(None, None, "lat", "lon"),
        check_vma=False,
    )
```

```python
import jax
import jax.numpy as jnp
import numpy as np
from jax import lax
from jax.experimental import pallas as pl
from jax.experimental.pallas import tpu as pltpu
from jax.sharding import PartitionSpec as P

MEMBERS = 128
PATCH = 16
RADIUS = 15
NS_ITERS = 5
ROWS = 16
COLS = 128
PATCHES = COLS // PATCH
CELLS = PATCH * PATCH
EXTRA = 16
CHANNELS = MEMBERS + EXTRA
PACKED = (PATCHES // 2) * MEMBERS + 16
NT = (((1,), (1,)), ((), ()))
PARTS = 4
VMEM_LIMIT = 48 * 1024 * 1024
F32 = jnp.float32
BF16 = jnp.bfloat16


def tapers():
    lane = lax.broadcasted_iota(jnp.int32, (1, 3 * CELLS), 1)
    side = lane >> 8
    row, column = (lane >> 4) & (PATCH - 1), lane & (PATCH - 1)
    span = 2.0 * (RADIUS + PATCH / 2.0)
    half = (PATCH - 1) / 2.0

    def line(place, shift):
        offset = jnp.abs(place.astype(F32) + (PATCH * shift - half))
        return jnp.where(offset < RADIUS + PATCH / 2.0, 1.0 - offset / span, 0.0)

    lon = jnp.where(side == 0, line(column, -1), jnp.where(side == 1, line(column, 0), line(column, 1)))
    return [line(row, shift) * lon for shift in (1, 0, -1)]


def stencil_rows(first):
    cell = first + lax.broadcasted_iota(jnp.int32, (COLS, CELLS), 0)
    lane = lax.broadcasted_iota(jnp.int32, (COLS, CELLS), 1)
    row, column = lane >> 4, lane & (PATCH - 1)
    if first < 3 * CELLS:
        side = first // CELLS - 1
        place = ((cell & (CELLS - 1)) >> 4) - row
        near = jnp.abs(place) <= 1
    else:
        side = (first - 3 * CELLS) // COLS - 1
        slot = (cell & (COLS - 1)) >> 4
        near = ((slot == 0) & (row == 0)) | ((slot == 1) & (row == ROWS - 1))
    beside = jnp.abs(side * PATCH + (cell & (PATCH - 1)) - column) <= 1
    return jnp.where(near & beside, 1.0, 0.0).astype(BF16)


def swap_groups(arrays):
    lane = lax.broadcasted_iota(jnp.int32, arrays[0].shape, 1)
    for step in (1, 2, 4):
        width = PATCH * step
        high = (lane & width) != 0
        mixed = list(arrays)
        for i in range(8):
            if i & step == 0:
                first, second = arrays[i], arrays[i + step]
                mixed[i] = jnp.where(high, pltpu.roll(second, width, 1), first)
                mixed[i + step] = jnp.where(high, second, pltpu.roll(first, COLS - width, 1))
        arrays = mixed
    return arrays


def fetch(source, target, sem):
    copy = pltpu.make_async_copy(source, target, sem)
    copy.start()
    return copy


def fetch_field(background_ref, variable, held, sems):
    part = MEMBERS // PARTS
    return [
        fetch(
            background_ref.at[variable, pl.ds(k * part, part)], held.at[pl.ds(k * part, part)], sems.at[k]
        )
        for k in range(PARTS)
    ]


def widen_lines(copies, held, lines):
    part = MEMBERS // PARTS
    for k in range(PARTS):
        if copies:
            copies[k].wait()
        for m in range(k * part // 16, (k + 1) * part // 16):
            piece = held[pl.ds(m * 16, 16)].astype(F32)
            lines[pl.ds(m * 256, 256), :] = piece.reshape(256, COLS)


def to_blocks(lines, out_ref):
    for m in range(MEMBERS // 16):
        halves = []
        for g in range(2):
            rows = [lines[pl.ds(m * 256 + g * 8 + r, 16, stride=16), :].astype(BF16) for r in range(8)]
            halves.append(swap_groups(rows))
        for b in range(PATCHES):
            both = jnp.concatenate([halves[0][b], halves[1][b]], axis=1)
            out_ref[pl.ds(m * 16, 16), pl.ds(b * CELLS, CELLS)] = both


def strip_kernel(background_ref, pack_ref, held, sides_ref, tails_ref, mask_ref, lines, sems):
    copies = fetch_field(background_ref, 0, held, sems)
    slots = (pack_ref.shape[1] - ROWS * COLS) // 3
    halves = []
    for g in range(2):
        rows = [
            jnp.broadcast_to(pack_ref[:, pl.ds(3 * slots + (g * 8 + r) * COLS, COLS)], (8, COLS))
            for r in range(8)
        ]
        halves.append(swap_groups(rows))
    which = lax.broadcasted_iota(jnp.int32, (8, CELLS), 0)
    mask = jnp.zeros((8, CELLS), F32)
    for b in range(PATCHES):
        mask = jnp.where(which == b, jnp.concatenate([halves[0][b], halves[1][b]], axis=1), mask)
    mask_ref[...] = mask
    cell = pack_ref[:, pl.ds(0, slots)].astype(jnp.int32)
    inverse = pack_ref[:, pl.ds(slots, slots)]
    value = pack_ref[:, pl.ds(2 * slots, slots)]
    column = cell & (COLS - 1)
    block = column >> 4
    place = ((cell >> 7) << 4) + (column & (PATCH - 1))
    slot_block = lax.broadcasted_iota(jnp.int32, (16, value.shape[1]), 0)
    chosen = (slot_block & 7) == block
    amount = jnp.where(slot_block < 8, inverse, value)
    left = jnp.where(chosen, amount, 0.0).astype(BF16)
    spot = lax.broadcasted_iota(jnp.int32, (CELLS, value.shape[1]), 0) == place
    right = jnp.where(spot, 1.0, 0.0).astype(BF16)
    grids = lax.dot_general(left, right, NT, preferred_element_type=F32)
    precision = grids[:8] * mask
    observed = grids[8:]
    channel = lax.broadcasted_iota(jnp.int32, (EXTRA, CELLS), 0)
    for b in range(PATCHES):
        tail = jnp.where(
            channel == 0, precision[b : b + 1], jnp.where(channel == 1, observed[b : b + 1], 0.0)
        ).astype(BF16)
        tails_ref[:, pl.ds(b * CELLS, CELLS)] = tail
        if b == 0:
            sides_ref[pl.ds(MEMBERS, EXTRA), pl.ds(0, CELLS)] = tail
        if b == PATCHES - 1:
            sides_ref[pl.ds(MEMBERS, EXTRA), pl.ds(CELLS, CELLS)] = tail

    widen_lines(copies, held, lines)
    group = lax.broadcasted_iota(jnp.int32, (16, COLS), 1) >> 4
    for m in range(MEMBERS // 16):
        for g in range(2):
            west = jnp.zeros((16, COLS), BF16)
            east = west
            for r in range(8):
                row = lines[pl.ds(m * 256 + g * 8 + r, 16, stride=16), :].astype(BF16)
                here = group == r
                west = jnp.where(here, pltpu.roll(row, PATCH * r, 1) if r else row, west)
                east = jnp.where(here, pltpu.roll(row, PATCH * (r + 1), 1) if r < 7 else row, east)
            sides_ref[pl.ds(m * 16, 16), pl.ds(g * COLS, COLS)] = west
            sides_ref[pl.ds(m * 16, 16), pl.ds(CELLS + g * COLS, COLS)] = east


def block_kernel(held, tails_ref, blocks_ref, table_ref, lines):
    for first in range(0, 3 * (CELLS + COLS), COLS):
        table_ref[pl.ds(first, COLS), :] = stencil_rows(first)
    widen_lines((), held, lines)
    to_blocks(lines, blocks_ref)
    blocks_ref[pl.ds(MEMBERS, EXTRA), :] = tails_ref[...]


def rim_kernel(first_ref, second_ref, sides_ref, rim_ref, even_ref, odd_ref):
    lat_odd = (lax.axis_index("lat") & 1) == 1
    lon_odd = (lax.axis_index("lon") & 1) == 1
    first = first_ref[...].astype(F32)
    second = second_ref[...].astype(F32)
    above = jnp.where(lat_odd, first, second)
    below = jnp.where(lat_odd, second, first)
    lane = lax.broadcasted_iota(jnp.int32, (MEMBERS, COLS), 1)
    for b in range(PATCHES):
        top = pltpu.roll(above, (COLS - PATCH * b) % COLS, 1)
        low = pltpu.roll(below, (COLS - PATCH * b + PATCH) % COLS, 1)
        edge = jnp.where(lane < PATCH, top, jnp.where(lane < 2 * PATCH, low, 0.0)).astype(BF16)
        rim_ref[:, pl.ds(b * COLS, COLS)] = edge
        if b == 0:
            west_rim = edge
        if b == PATCHES - 1:
            east_rim = edge
    west = sides_ref[:, pl.ds(0, CELLS)]
    east = sides_ref[:, pl.ds(CELLS, CELLS)]
    even_ref[:, pl.ds(0, CELLS)] = jnp.where(lon_odd, west, east)
    odd_ref[:, pl.ds(0, CELLS)] = jnp.where(lon_odd, east, west)
    even_ref[pl.ds(0, MEMBERS), pl.ds(CELLS, COLS)] = jnp.where(lon_odd, west_rim, east_rim)
    odd_ref[pl.ds(0, MEMBERS), pl.ds(CELLS, COLS)] = jnp.where(lon_odd, east_rim, west_rim)
    blank = jnp.zeros((EXTRA, COLS), BF16)
    even_ref[pl.ds(MEMBERS, EXTRA), pl.ds(CELLS, COLS)] = blank
    odd_ref[pl.ds(MEMBERS, EXTRA), pl.ds(CELLS, COLS)] = blank


def gram_kernel(
    blocks_ref, rim_ref, first_ref, second_ref, table_ref,
    even_ref, odd_ref, pert, wide, wide_rim,
):
    lat = lax.axis_index("lat")
    lat_odd = (lat & 1) == 1
    lon_odd = (lax.axis_index("lon") & 1) == 1
    span = PATCHES * CELLS
    wide[:, pl.ds(0, CELLS)] = jnp.zeros((CHANNELS, CELLS), BF16)
    wide[:, pl.ds(span + 3 * CELLS, CELLS)] = jnp.zeros((CHANNELS, CELLS), BF16)
    wide[:, pl.ds(2 * CELLS, span)] = blocks_ref[...]
    one = first_ref[:, pl.ds(0, CELLS)]
    two = second_ref[:, pl.ds(0, CELLS)]
    wide[:, pl.ds(CELLS, CELLS)] = jnp.where(lon_odd, one, two)
    wide[:, pl.ds(span + 2 * CELLS, CELLS)] = jnp.where(lon_odd, two, one)
    rim_span = PATCHES * COLS
    blank = jnp.zeros((MEMBERS, COLS), BF16)
    wide_rim[:, pl.ds(0, COLS)] = blank
    wide_rim[:, pl.ds(rim_span + 3 * COLS, COLS)] = blank
    wide_rim[:, pl.ds(2 * COLS, rim_span)] = rim_ref[...]
    one = first_ref[pl.ds(0, MEMBERS), pl.ds(CELLS, COLS)]
    two = second_ref[pl.ds(0, MEMBERS), pl.ds(CELLS, COLS)]
    wide_rim[:, pl.ds(COLS, COLS)] = jnp.where(lon_odd, one, two)
    wide_rim[:, pl.ds(rim_span + 2 * COLS, COLS)] = jnp.where(lon_odd, two, one)

    lane = lax.broadcasted_iota(jnp.int32, (1, CELLS), 1)
    row = lane >> 4
    last = lax.axis_size("lat") - 1
    short = ((row == 0) & (lat == 0)) | ((row == ROWS - 1) & (lat == last))
    share = jnp.where(short, 1.0 / 6.0, 1.0 / 9.0)
    tail_row = lax.broadcasted_iota(jnp.int32, (EXTRA, CELLS), 0)
    for e in range(PATCHES + 2):
        summed = jnp.dot(
            wide[pl.ds(0, MEMBERS), pl.ds(e * CELLS, 3 * CELLS)], table_ref[pl.ds(0, 3 * CELLS), :], preferred_element_type=F32
        )
        summed = summed + jnp.dot(
            wide_rim[:, pl.ds(e * COLS, 3 * COLS)], table_ref[pl.ds(3 * CELLS, 3 * COLS), :], preferred_element_type=F32
        )
        mean = summed * share
        average = jnp.sum(mean, axis=0, keepdims=True) * (1.0 / MEMBERS)
        pert[pl.ds(0, MEMBERS), pl.ds(e * CELLS, CELLS)] = (mean - average).astype(BF16)
        tail = wide[pl.ds(MEMBERS, EXTRA), pl.ds((e + 1) * CELLS, CELLS)].astype(F32)
        innovation = tail[1:2] - average
        pert[pl.ds(MEMBERS, EXTRA), pl.ds(e * CELLS, CELLS)] = jnp.where(
            tail_row == 0, innovation, jnp.where(tail_row == 1, tail[0:1], 0.0)
        ).astype(BF16)

    r = lax.broadcasted_iota(jnp.int32, (MEMBERS, MEMBERS), 0)
    c = lax.broadcasted_iota(jnp.int32, (MEMBERS, MEMBERS), 1)
    lower = r >= c
    same = r == c
    base = (PATCHES // 2) * MEMBERS
    above, _, below = tapers()
    for out_ref, near, far in ((even_ref, above, below), (odd_ref, below, above)):
        taper = jnp.where(lat_odd, near, far)
        forcings, diagonals = [], []
        for pair in range(PATCHES // 2):
            first, forcing = patch_gram(pert, 2 * pair, taper, same)
            forcings.append(forcing)
            second, forcing = patch_gram(pert, 2 * pair + 1, taper, same)
            forcings.append(forcing)
            diagonals.append(jnp.sum(jnp.where(same, second, 0.0), axis=0, keepdims=True))
            out_ref[pl.ds(pair * MEMBERS, MEMBERS), :] = jnp.where(lower, first, second).astype(BF16)
        tail = forcings + diagonals + [jnp.zeros((4, MEMBERS), F32)]
        out_ref[pl.ds(base, 16), :] = jnp.concatenate(tail, axis=0).astype(BF16)


def patch_gram(pert, p, taper, same):
    window = pert[:, pl.ds(p * CELLS, 3 * CELLS)]
    precision = window[MEMBERS:].astype(F32)[1:2]
    scaled = (window[:MEMBERS].astype(F32) * (precision * taper)).astype(BF16)
    full = lax.dot_general(scaled, window, NT, preferred_element_type=F32)
    forcing = jnp.sum(jnp.where(same, full[:, MEMBERS : MEMBERS + 1], 0.0), axis=0, keepdims=True)
    return full[:, :MEMBERS], forcing


def centre_kernel(pert, blocks_ref, background_ref, mask_ref,
                  gram_ref, force_ref, departure_ref, base_ref, rest_ref, soil, held, lines, sems):
    copies = fetch_field(background_ref, 1, held, sems)
    r = lax.broadcasted_iota(jnp.int32, (MEMBERS, MEMBERS), 0)
    c = lax.broadcasted_iota(jnp.int32, (MEMBERS, MEMBERS), 1)
    same = r == c
    taper = tapers()[1]
    forcings = []
    for p in range(PATCHES):
        gram, forcing = patch_gram(pert, p, taper, same)
        gram_ref[p] = gram + jnp.where(same, MEMBERS - 1.0, 0.0)
        forcings.append(forcing)
    force_ref[...] = jnp.concatenate(forcings, axis=0)
    widen_lines(copies, held, lines)
    to_blocks(lines, soil)
    for p in range(PATCHES):
        cells = pl.ds(p * CELLS, CELLS)
        land = mask_ref[p : p + 1, :] != 0.0
        for v, raw in enumerate((blocks_ref[pl.ds(0, MEMBERS), cells], soil[:, cells])):
            raw = raw.astype(F32)
            mean = jnp.sum(raw, axis=0, keepdims=True) * (1.0 / MEMBERS)
            place = pl.ds((2 * p + v) * CELLS, CELLS)
            coarse = mean.astype(BF16).astype(F32)
            departure_ref[:, place] = jnp.where(land, raw - mean, 0.0).astype(BF16)
            base_ref[:, place] = jnp.where(land, coarse, raw).astype(BF16)
            rest_ref[:, place] = jnp.broadcast_to(jnp.where(land, mean - coarse, 0.0), (8, CELLS))


def split(a):
    high = a.astype(BF16)
    return high, (a - high.astype(F32)).astype(BF16)


def product(a, b):
    a_high, a_low = split(a)
    b_high, b_low = split(b)
    wide = jnp.concatenate([b_high, b_low], axis=1)
    out = jnp.dot(
        jnp.concatenate([a_high, a_low], axis=1),
        jnp.concatenate([wide, wide], axis=0),
        preferred_element_type=F32,
    )
    return out[:, :MEMBERS] + out[:, MEMBERS:]


def halves(a):
    return jnp.concatenate(split(a), axis=1)


def product(a, b):
    out = jnp.dot(a, jnp.concatenate([b, b], axis=0), preferred_element_type=F32)
    return out[:, :MEMBERS] + out[:, MEMBERS:]


def solve_kernel(first_ref, second_ref, gram_ref, force_ref, departure_ref, base_ref, rest_ref, out_ref,
                 pair_ref, scratch, spread, held, sems):
    r = lax.broadcasted_iota(jnp.int32, (MEMBERS, MEMBERS), 0)
    c = lax.broadcasted_iota(jnp.int32, (MEMBERS, MEMBERS), 1)
    eye = jnp.where(r == c, 1.0, 0.0)
    unit = eye.astype(BF16)
    base = (PATCHES // 2) * MEMBERS
    tail = first_ref[pl.ds(base, 16), :].astype(F32) + second_ref[pl.ds(base, 16), :].astype(F32)
    norms = []
    for pair in range(PATCHES // 2):
        rows = pl.ds(pair * MEMBERS, MEMBERS)
        mixed = first_ref[rows, :].astype(F32) + second_ref[rows, :].astype(F32)
        turned = mixed.T
        diagonal = tail[8 + pair : 9 + pair]
        gains = (
            jnp.where(r >= c, mixed, turned),
            jnp.where(r > c, turned, jnp.where(r < c, mixed, diagonal)),
        )
        for k in range(2):
            p = 2 * pair + k
            system = gram_ref[p] + gains[k]
            total = jnp.sum(jnp.sum(system * system, axis=0, keepdims=True), axis=1, keepdims=True)
            norm = jnp.sqrt(total)
            norms.append(norm)
            scaled = system * (1.0 / norm)
            split_scaled = halves(scaled)
            pair_ref[p, :MEMBERS] = halves(1.5 * scaled - 0.5 * product(split_scaled, split_scaled))
            pair_ref[p, MEMBERS:] = halves(1.5 * eye - 0.5 * scaled)

    def sweep():
        middles = [
            halves(1.5 * eye - 0.5 * product(pair_ref[p, MEMBERS:], pair_ref[p, :MEMBERS]))
            for p in range(PATCHES)
        ]
        for p in range(PATCHES):
            pair_ref[p] = halves(product(pair_ref[p], middles[p]))

    for _ in range(NS_ITERS - 2):
        sweep()
    middles = [
        halves(1.5 * eye - 0.5 * product(pair_ref[p, MEMBERS:], pair_ref[p, :MEMBERS]))
        for p in range(PATCHES)
    ]
    transforms = []
    for p in range(PATCHES):
        lower = product(pair_ref[p, MEMBERS:], middles[p])
        forcing = force_ref[p : p + 1] + tail[p : p + 1]
        once = jnp.sum(lower * forcing, axis=1, keepdims=True)
        mean_weight = jnp.sum(lower * once, axis=0, keepdims=True) * (1.0 / norms[p])
        scale = jnp.sqrt(MEMBERS - 1.0) / jnp.sqrt(norms[p])
        transform = (lower * scale + mean_weight).astype(BF16)
        transforms.append(jnp.concatenate([transform, unit], axis=1))

    copies = []
    for v in range(2):
        for p in range(PATCHES):
            cells = pl.ds((2 * p + v) * CELLS, CELLS)
            updated = jnp.dot(
                transforms[p],
                jnp.concatenate([departure_ref[:, cells], base_ref[:, cells]], axis=0),
                preferred_element_type=F32,
            )
            spread[v, :, pl.ds(p * CELLS, CELLS)] = updated + rest_ref[0:1, cells]
        for m in range(MEMBERS // 16):
            rows = pl.ds(m * 16, 16)
            for g in range(2):
                lines = swap_groups(
                    [spread[v, rows, pl.ds(b * CELLS + g * COLS, COLS)] for b in range(PATCHES)]
                )
                for k in range(8):
                    scratch[v, pl.ds(m * 256 + g * 8 + k, 16, stride=16), :] = lines[k]
            held[v, rows] = scratch[v, pl.ds(m * 256, 256), :].reshape(16, ROWS, COLS).astype(BF16)
            copies.append(fetch(held.at[v, rows], out_ref.at[v, rows], sems.at[v * (MEMBERS // 16) + m]))
    for copy in copies:
        copy.wait()


LIMITS = {strip_kernel: 53 * 1024 * 1024}


def call(kernel, out_shape, scratch, flops, moved, *operands, far=(), scalars=(), out_far=False):
    vmem = pl.BlockSpec(memory_space=pltpu.VMEM)
    smem = pl.BlockSpec(memory_space=pltpu.SMEM)
    anywhere = pl.BlockSpec(memory_space=pltpu.HBM)
    return pl.pallas_call(
        kernel,
        out_shape=out_shape,
        in_specs=[
            anywhere if i in far else smem if i in scalars else vmem for i in range(len(operands))
        ],
        out_specs=[anywhere if out_far else vmem] * len(out_shape),
        scratch_shapes=scratch,
        compiler_params=pltpu.CompilerParams(vmem_limit_bytes=LIMITS.get(kernel, VMEM_LIMIT)),
        cost_estimate=pl.CostEstimate(flops=flops, bytes_accessed=moved, transcendentals=0),
    )(*operands)


def pairs_inside(size):
    return [(i, i ^ 1) for i in range(size)]


def pairs_across(size, wrap):
    pairs = []
    for i in range(1, size - 1, 2):
        pairs += [(i, i + 1), (i + 1, i)]
    if wrap:
        pairs += [(size - 1, 0), (0, size - 1)]
    return pairs


def exchange(even, odd, axis, wrap):
    size = lax.axis_size(axis)
    return (
        lax.ppermute(even, axis, pairs_inside(size)),
        lax.ppermute(odd, axis, pairs_across(size, wrap)),
    )


def body(background, obs_cell, obs_count, obs_value, obs_err, land):
    slots = obs_cell.shape[-1]
    span = PATCHES * CELLS
    shape = jax.ShapeDtypeStruct
    field = pltpu.VMEM((MEMBERS, ROWS, COLS), BF16)
    lines_shape = (MEMBERS * ROWS, COLS)
    copies = pltpu.SemaphoreType.DMA
    lat_odd = (lax.axis_index("lat") & 1) == 1
    cell, value, err = (array.reshape(1, slots).astype(F32) for array in (obs_cell, obs_value, obs_err))
    used = lax.broadcasted_iota(jnp.int32, (1, slots), 1) < obs_count
    parts = [cell, jnp.where(used, 1.0 / (err * err), 0.0), jnp.where(used, value, 0.0)]
    parts.append(land.reshape(1, ROWS * COLS).astype(F32))
    room = sum(part.shape[1] for part in parts)
    pack, start = 0.0, 0
    for part in parts:
        pack = pack + jnp.pad(part, ((0, 0), (start, room - start - part.shape[1])))
        start += part.shape[1]
    top, bottom = background[0, :, 0], background[0, :, ROWS - 1]
    rows = exchange(
        jnp.where(lat_odd, top, bottom), jnp.where(lat_odd, bottom, top), "lat", False
    )
    held, sides, tails, mask = call(
        strip_kernel,
        [
            shape((MEMBERS, ROWS, COLS), BF16),
            shape((CHANNELS, 2 * CELLS), BF16),
            shape((EXTRA, span), BF16),
            shape((8, CELLS), F32),
        ],
        [pltpu.VMEM(lines_shape, F32), copies((PARTS,))],
        10**7, 2 * 10**6,
        background, pack,
        far=(0,),
    )
    rim, even, odd = call(
        rim_kernel,
        [shape((MEMBERS, PATCHES * COLS), BF16)] + [shape((CHANNELS, CELLS + COLS), BF16)] * 2,
        [], 10**6, 10**6, *rows, sides,
    )
    neighbours = exchange(even, odd, "lon", True)
    blocks, table = call(
        block_kernel,
        [shape((CHANNELS, span), BF16), shape((3 * (CELLS + COLS), CELLS), BF16)],
        [pltpu.VMEM(lines_shape, F32)],
        10**8, 4 * 10**6,
        held, tails,
    )
    even, odd, pert = call(
        gram_kernel,
        [shape((PACKED, MEMBERS), BF16)] * 2 + [shape((CHANNELS, span + 2 * CELLS), BF16)],
        [
            pltpu.VMEM((CHANNELS, span + 4 * CELLS), BF16),
            pltpu.VMEM((MEMBERS, (PATCHES + 4) * COLS), BF16),
        ],
        10**9, 3 * 10**6,
        blocks, rim, *neighbours, table,
    )
    packed = exchange(even, odd, "lat", False)
    gram, force, departure, base, rest = call(
        centre_kernel,
        [
            shape((PATCHES, MEMBERS, MEMBERS), F32),
            shape((PATCHES, MEMBERS), F32),
            shape((MEMBERS, 2 * span), BF16),
            shape((MEMBERS, 2 * span), BF16),
            shape((8, 2 * span), F32),
        ],
        [pltpu.VMEM((MEMBERS, span), BF16), field, pltpu.VMEM(lines_shape, F32), copies((PARTS,))],
        10**9, 5 * 10**6,
        pert, blocks, background, mask,
        far=(2,),
    )
    (analysis,) = call(
        solve_kernel,
        [shape(background.shape, BF16)],
        [
            pltpu.VMEM((PATCHES, 2 * MEMBERS, 2 * MEMBERS), BF16),
            pltpu.VMEM((2,) + lines_shape, F32),
            pltpu.VMEM((2, MEMBERS, span), F32),
            pltpu.VMEM(background.shape, BF16),
            copies((2 * MEMBERS // 16,)),
        ],
        2 * 10**9, 5 * 10**6,
        *packed, gram, force, departure, base, rest,
        out_far=True,
    )
    return analysis


def solution(mesh):
    return jax.shard_map(
        body,
        mesh=mesh,
        in_specs=(
            P(None, None, "lat", "lon"),
            P("lat", "lon", None),
            P("lat", "lon"),
            P("lat", "lon", None),
            P("lat", "lon", None),
            P("lat", "lon"),
        ),
        out_specs=P(None, None, "lat", "lon"),
        check_vma=False,
    )
```

```python
import jax
import jax.numpy as jnp
import numpy as np
from jax import lax
from jax.experimental import pallas as pl
from jax.experimental.pallas import tpu as pltpu
from jax.sharding import PartitionSpec as P

MEMBERS = 128
PATCH = 16
RADIUS = 15
NS_ITERS = 5
ROWS = 16
COLS = 128
PATCHES = COLS // PATCH
CELLS = PATCH * PATCH
EXTRA = 16
CHANNELS = MEMBERS + EXTRA
RIMS = (PATCHES // 2) * MEMBERS + 16
PACKED = RIMS + 2 * MEMBERS + MEMBERS // 2 + EXTRA
NT = (((1,), (1,)), ((), ()))
PARTS = 4
VMEM_LIMIT = 48 * 1024 * 1024
F32 = jnp.float32
BF16 = jnp.bfloat16


def tapers():
    lane = lax.broadcasted_iota(jnp.int32, (1, 3 * CELLS), 1)
    side = lane >> 8
    row, column = (lane >> 4) & (PATCH - 1), lane & (PATCH - 1)
    span = 2.0 * (RADIUS + PATCH / 2.0)
    half = (PATCH - 1) / 2.0

    def line(place, shift):
        offset = jnp.abs(place.astype(F32) + (PATCH * shift - half))
        return jnp.where(offset < RADIUS + PATCH / 2.0, 1.0 - offset / span, 0.0)

    lon = jnp.where(side == 0, line(column, -1), jnp.where(side == 1, line(column, 0), line(column, 1)))
    inner = (row > 0) & (row < ROWS - 1)
    return [jnp.where(inner, line(row, shift) * lon, 0.0) for shift in (1, 0, -1)]


def rim_taper(first):
    lane = lax.broadcasted_iota(jnp.int32, (1, 2 * COLS), 1)
    side = (lane >> 6) - first - 1
    row, column = (lane >> 4) & 3, lane & (PATCH - 1)
    span = 2.0 * (RADIUS + PATCH / 2.0)
    half = (PATCH - 1) / 2.0
    across = jnp.where((row == 0) | (row == 3), 1.0 - (half + 1.0) / span, 1.0 - half / span)
    offset = jnp.abs(column.astype(F32) + side.astype(F32) * PATCH - half)
    along = jnp.where(offset < RADIUS + PATCH / 2.0, 1.0 - offset / span, 0.0)
    return across * along


def stencil_rows(first):
    cell = first + lax.broadcasted_iota(jnp.int32, (COLS, CELLS), 0)
    lane = lax.broadcasted_iota(jnp.int32, (COLS, CELLS), 1)
    side = first // CELLS - 1
    near = jnp.abs(((cell & (CELLS - 1)) >> 4) - (lane >> 4)) <= 1
    beside = jnp.abs(side * PATCH + (cell & (PATCH - 1)) - (lane & (PATCH - 1))) <= 1
    return jnp.where(near & beside, 1.0, 0.0).astype(BF16)


def rim_stencil_rows(place):
    cell = lax.broadcasted_iota(jnp.int32, (COLS, COLS), 0)
    lane = lax.broadcasted_iota(jnp.int32, (COLS, COLS), 1)
    row = (lane >> 4) & 3
    step = (cell >> 4) - jnp.where(row < 2, row, row + 2)
    side = place - 1 - (lane >> 6)
    beside = jnp.abs(side * PATCH + (cell & (PATCH - 1)) - (lane & (PATCH - 1))) <= 1
    return jnp.where((step >= 0) & (step <= 2) & beside, 1.0, 0.0).astype(BF16)


def swap_groups(arrays):
    lane = lax.broadcasted_iota(jnp.int32, arrays[0].shape, 1)
    for step in (1, 2, 4):
        width = PATCH * step
        high = (lane & width) != 0
        mixed = list(arrays)
        for i in range(8):
            if i & step == 0:
                first, second = arrays[i], arrays[i + step]
                mixed[i] = jnp.where(high, pltpu.roll(second, width, 1), first)
                mixed[i + step] = jnp.where(high, second, pltpu.roll(first, COLS - width, 1))
        arrays = mixed
    return arrays


def fetch(source, target, sem):
    copy = pltpu.make_async_copy(source, target, sem)
    copy.start()
    return copy


def fetch_field(background_ref, variable, held, sems):
    part = MEMBERS // PARTS
    return [
        fetch(
            background_ref.at[variable, pl.ds(k * part, part)], held.at[pl.ds(k * part, part)], sems.at[k]
        )
        for k in range(PARTS)
    ]


def widen_lines(copies, held, lines):
    part = MEMBERS // PARTS
    for k in range(PARTS):
        if copies:
            copies[k].wait()
        for m in range(k * part // 16, (k + 1) * part // 16):
            piece = held[pl.ds(m * 16, 16)].astype(F32)
            lines[pl.ds(m * 256, 256), :] = piece.reshape(256, COLS)


def to_blocks(lines, out_ref):
    for m in range(MEMBERS // 16):
        halves = []
        for g in range(2):
            rows = [lines[pl.ds(m * 256 + g * 8 + r, 16, stride=16), :].astype(BF16) for r in range(8)]
            halves.append(swap_groups(rows))
        for b in range(PATCHES):
            both = jnp.concatenate([halves[0][b], halves[1][b]], axis=1)
            out_ref[pl.ds(m * 16, 16), pl.ds(b * CELLS, CELLS)] = both


def strip_kernel(background_ref, pack_ref, held, even_ref, odd_ref, tails_ref, mask_ref, lines, sems):
    lon_odd = (lax.axis_index("lon") & 1) == 1
    copies = fetch_field(background_ref, 0, held, sems)
    slots = (pack_ref.shape[1] - (ROWS + 1) * COLS) // 3
    halves = []
    for g in range(2):
        rows = [
            jnp.broadcast_to(pack_ref[:, pl.ds(3 * slots + (g * 8 + r) * COLS, COLS)], (8, COLS))
            for r in range(8)
        ]
        halves.append(swap_groups(rows))
    which = lax.broadcasted_iota(jnp.int32, (8, CELLS), 0)
    mask = jnp.zeros((8, CELLS), F32)
    for b in range(PATCHES):
        mask = jnp.where(which == b, jnp.concatenate([halves[0][b], halves[1][b]], axis=1), mask)
    mask_ref[...] = mask
    cell = pack_ref[:, pl.ds(0, slots)].astype(jnp.int32)
    count = pack_ref[:, pl.ds(3 * slots + ROWS * COLS, COLS)][:, 0:1].astype(jnp.int32)
    used = lax.broadcasted_iota(jnp.int32, (1, slots), 1) < count
    err = pack_ref[:, pl.ds(2 * slots, slots)]
    inverse = jnp.where(used, 1.0 / (err * err), 0.0)
    value = jnp.where(used, pack_ref[:, pl.ds(slots, slots)], 0.0)
    column = cell & (COLS - 1)
    block = column >> 4
    place = ((cell >> 7) << 4) + (column & (PATCH - 1))
    slot_block = lax.broadcasted_iota(jnp.int32, (16, value.shape[1]), 0)
    chosen = (slot_block & 7) == block
    amount = jnp.where(slot_block < 8, inverse, value)
    left = jnp.where(chosen, amount, 0.0).astype(BF16)
    spot = lax.broadcasted_iota(jnp.int32, (CELLS, value.shape[1]), 0) == place
    right = jnp.where(spot, 1.0, 0.0).astype(BF16)
    grids = lax.dot_general(left, right, NT, preferred_element_type=F32)
    precision = grids[:8] * mask
    observed = grids[8:]
    channel = lax.broadcasted_iota(jnp.int32, (EXTRA, CELLS), 0)
    for b in range(PATCHES):
        tail = jnp.where(
            channel == 0, precision[b : b + 1], jnp.where(channel == 1, observed[b : b + 1], 0.0)
        ).astype(BF16)
        tails_ref[:, pl.ds(b * CELLS, CELLS)] = tail
        if b == 0:
            west = tail
    even_ref[pl.ds(MEMBERS, EXTRA), :] = jnp.where(lon_odd, west, tail)
    odd_ref[pl.ds(MEMBERS, EXTRA), :] = jnp.where(lon_odd, tail, west)

    widen_lines(copies, held, lines)
    group = lax.broadcasted_iota(jnp.int32, (16, COLS), 1) >> 4
    for m in range(MEMBERS // 16):
        for g in range(2):
            west = jnp.zeros((16, COLS), BF16)
            east = west
            for r in range(8):
                row = lines[pl.ds(m * 256 + g * 8 + r, 16, stride=16), :].astype(BF16)
                here = group == r
                west = jnp.where(here, pltpu.roll(row, PATCH * r, 1) if r else row, west)
                east = jnp.where(here, pltpu.roll(row, PATCH * (r + 1), 1) if r < 7 else row, east)
            even_ref[pl.ds(m * 16, 16), pl.ds(g * COLS, COLS)] = jnp.where(lon_odd, west, east)
            odd_ref[pl.ds(m * 16, 16), pl.ds(g * COLS, COLS)] = jnp.where(lon_odd, east, west)


def block_kernel(held, tails_ref, blocks_ref, table_ref, lines):
    for first in range(0, 3 * CELLS, COLS):
        table_ref[pl.ds(first, COLS), :] = stencil_rows(first)
    widen_lines((), held, lines)
    to_blocks(lines, blocks_ref)
    blocks_ref[pl.ds(MEMBERS, EXTRA), :] = tails_ref[...]


def shift(piece, lanes):
    return pltpu.roll(piece, lanes % COLS, 1) if lanes % COLS else piece


def quarters(pieces, offset, lane):
    tile = shift(pieces[0], -offset)
    for q in range(1, len(pieces)):
        tile = jnp.where((lane >> 5) == q, shift(pieces[q], 32 * q - offset), tile)
    return tile


def gram_kernel(blocks_ref, first_ref, second_ref, table_ref, even_ref, odd_ref, pert, wide):
    lat_odd = (lax.axis_index("lat") & 1) == 1
    lon_odd = (lax.axis_index("lon") & 1) == 1
    span = PATCHES * CELLS
    wide[:, pl.ds(0, CELLS)] = jnp.zeros((CHANNELS, CELLS), BF16)
    wide[:, pl.ds(span + 3 * CELLS, CELLS)] = jnp.zeros((CHANNELS, CELLS), BF16)
    wide[:, pl.ds(2 * CELLS, span)] = blocks_ref[...]
    one, two = first_ref[...], second_ref[...]
    wide[:, pl.ds(CELLS, CELLS)] = jnp.where(lon_odd, one, two)
    wide[:, pl.ds(span + 2 * CELLS, CELLS)] = jnp.where(lon_odd, two, one)

    tail_row = lax.broadcasted_iota(jnp.int32, (EXTRA, CELLS), 0)
    for e in range(PATCHES + 2):
        summed = jnp.dot(
            wide[pl.ds(0, MEMBERS), pl.ds(e * CELLS, 3 * CELLS)], table_ref[...], preferred_element_type=F32
        )
        mean = summed * (1.0 / 9.0)
        average = jnp.sum(mean, axis=0, keepdims=True) * (1.0 / MEMBERS)
        pert[pl.ds(0, MEMBERS), pl.ds(e * CELLS, CELLS)] = (mean - average).astype(BF16)
        tail = wide[pl.ds(MEMBERS, EXTRA), pl.ds((e + 1) * CELLS, CELLS)].astype(F32)
        innovation = tail[1:2] - average
        pert[pl.ds(MEMBERS, EXTRA), pl.ds(e * CELLS, CELLS)] = jnp.where(
            tail_row == 0, innovation, jnp.where(tail_row == 1, tail[0:1], 0.0)
        ).astype(BF16)

    lane = lax.broadcasted_iota(jnp.int32, (MEMBERS, COLS), 1)
    tail_lane = lax.broadcasted_iota(jnp.int32, (EXTRA, COLS), 1)
    rims, rim_tails = [], []
    for part, offset in ((0, 0), (1, COLS - 32)):
        tiles, tails = [], []
        for t in range(3):
            some = range(4 * t, min(4 * t + 4, PATCHES + 2))
            places = [pl.ds((e + 1) * CELLS + part * COLS, COLS) for e in some]
            tiles.append(quarters([wide[pl.ds(0, MEMBERS), place] for place in places], offset, lane))
            tail = [wide[pl.ds(MEMBERS, EXTRA), place].astype(F32) for place in places]
            tails.append(quarters(tail, offset, tail_lane)[0:2])
        half = MEMBERS // 2
        tiles[2] = jnp.where(lane[:half] < 64, tiles[2][:half], shift(tiles[2][half:], 64))
        rims.append(tiles)
        rim_tails.append(jnp.concatenate(tails + [jnp.zeros((EXTRA - 6, COLS), F32)], axis=0).astype(BF16))
    start = RIMS
    for t in range(3):
        size = rims[0][t].shape[0]
        even_ref[pl.ds(start, size), :] = jnp.where(lat_odd, rims[0][t], rims[1][t])
        odd_ref[pl.ds(start, size), :] = jnp.where(lat_odd, rims[1][t], rims[0][t])
        start += size
    even_ref[pl.ds(start, EXTRA), :] = jnp.where(lat_odd, rim_tails[0], rim_tails[1])
    odd_ref[pl.ds(start, EXTRA), :] = jnp.where(lat_odd, rim_tails[1], rim_tails[0])

    r = lax.broadcasted_iota(jnp.int32, (MEMBERS, MEMBERS), 0)
    c = lax.broadcasted_iota(jnp.int32, (MEMBERS, MEMBERS), 1)
    lower = r >= c
    same = r == c
    base = (PATCHES // 2) * MEMBERS
    above, _, below = tapers()
    for out_ref, near, far in ((even_ref, above, below), (odd_ref, below, above)):
        taper = jnp.where(lat_odd, near, far)
        forcings, diagonals = [], []
        for pair in range(PATCHES // 2):
            first, forcing = patch_gram(pert, window_of(2 * pair), taper, same)
            forcings.append(forcing)
            second, forcing = patch_gram(pert, window_of(2 * pair + 1), taper, same)
            forcings.append(forcing)
            diagonals.append(jnp.sum(jnp.where(same, second, 0.0), axis=0, keepdims=True))
            out_ref[pl.ds(pair * MEMBERS, MEMBERS), :] = jnp.where(lower, first, second).astype(BF16)
        tail = forcings + diagonals + [jnp.zeros((4, MEMBERS), F32)]
        out_ref[pl.ds(base, 16), :] = jnp.concatenate(tail, axis=0).astype(BF16)


def patch_gram(pert, lanes, taper, same):
    window = pert[:, lanes]
    precision = window[MEMBERS:].astype(F32)[1:2]
    scaled = (window[:MEMBERS].astype(F32) * (precision * taper)).astype(BF16)
    full = lax.dot_general(scaled, window, NT, preferred_element_type=F32)
    forcing = jnp.sum(jnp.where(same, full[:, MEMBERS : MEMBERS + 1], 0.0), axis=0, keepdims=True)
    return full[:, :MEMBERS], forcing


def window_of(p):
    return pl.ds(p * CELLS, 3 * CELLS)


def centre_kernel(pert, wide, blocks_ref, background_ref, mask_ref,
                  gram_ref, force_ref, departure_ref, base_ref, rest_ref, rim_ref, rim_table_ref,
                  soil, held, lines, sems):
    copies = fetch_field(background_ref, 1, held, sems)
    r = lax.broadcasted_iota(jnp.int32, (MEMBERS, MEMBERS), 0)
    c = lax.broadcasted_iota(jnp.int32, (MEMBERS, MEMBERS), 1)
    same = r == c
    taper = tapers()[1]
    forcings = []
    for p in range(PATCHES):
        gram, forcing = patch_gram(pert, window_of(p), taper, same)
        gram_ref[p] = gram + jnp.where(same, MEMBERS - 1.0, 0.0)
        forcings.append(forcing)
    force_ref[...] = jnp.concatenate(forcings, axis=0)
    for place in range(4):
        rim_table_ref[pl.ds(place * COLS, COLS), :] = rim_stencil_rows(place)
    lane = lax.broadcasted_iota(jnp.int32, (CHANNELS, COLS), 1)
    for e in range(PATCHES + 4):
        upper = shift(wide[:, pl.ds(e * CELLS, COLS)], 32)
        lower = shift(wide[:, pl.ds(e * CELLS + COLS, COLS)], -32)
        rim_ref[:, pl.ds(e * COLS, COLS)] = jnp.where(lane < 64, upper, lower)
    widen_lines(copies, held, lines)
    to_blocks(lines, soil)
    for p in range(PATCHES):
        cells = pl.ds(p * CELLS, CELLS)
        land = mask_ref[p : p + 1, :] != 0.0
        for v, raw in enumerate((blocks_ref[pl.ds(0, MEMBERS), cells], soil[:, cells])):
            raw = raw.astype(F32)
            mean = jnp.sum(raw, axis=0, keepdims=True) * (1.0 / MEMBERS)
            place = pl.ds((2 * p + v) * CELLS, CELLS)
            coarse = mean.astype(BF16).astype(F32)
            departure_ref[:, place] = jnp.where(land, raw - mean, 0.0).astype(BF16)
            base_ref[:, place] = jnp.where(land, coarse, raw).astype(BF16)
            rest_ref[:, place] = jnp.broadcast_to(jnp.where(land, mean - coarse, 0.0), (8, CELLS))


def split(a):
    high = a.astype(BF16)
    return high, (a - high.astype(F32)).astype(BF16)


def product(a, b):
    a_high, a_low = split(a)
    b_high, b_low = split(b)
    wide = jnp.concatenate([b_high, b_low], axis=1)
    out = jnp.dot(
        jnp.concatenate([a_high, a_low], axis=1),
        jnp.concatenate([wide, wide], axis=0),
        preferred_element_type=F32,
    )
    return out[:, :MEMBERS] + out[:, MEMBERS:]


def halves(a):
    return jnp.concatenate(split(a), axis=1)


def product(a, b):
    out = jnp.dot(a, jnp.concatenate([b, b], axis=0), preferred_element_type=F32)
    return out[:, :MEMBERS] + out[:, MEMBERS:]


def rim_perts(first_ref, second_ref, rim_ref, rim_table_ref, wide_rim, pert):
    lat = lax.axis_index("lat")
    lat_odd = (lat & 1) == 1
    last = lax.axis_size("lat") - 1
    half = MEMBERS // 2

    def tiles_of(source):
        folded = source(RIMS + 2 * MEMBERS, half)
        tails = source(RIMS + 2 * MEMBERS + half, EXTRA).astype(F32)
        tiles = [source(RIMS, MEMBERS), source(RIMS + MEMBERS, MEMBERS)]
        return tiles + [jnp.concatenate([folded, shift(folded, 64)], axis=0)], tails

    def above(start, size):
        rows = pl.ds(start, size)
        return jnp.where(lat_odd, first_ref[rows, :], second_ref[rows, :])

    def below(start, size):
        rows = pl.ds(start, size)
        return jnp.where(lat_odd, second_ref[rows, :], first_ref[rows, :])

    top, top_tails = tiles_of(above)
    low, low_tails = tiles_of(below)
    lane = lax.broadcasted_iota(jnp.int32, (MEMBERS, COLS), 1)
    tail_lane = lax.broadcasted_iota(jnp.int32, (8, COLS), 1)
    wide_rim[:, pl.ds(0, COLS)] = jnp.zeros((MEMBERS, COLS), BF16)
    wide_rim[:, pl.ds((PATCHES + 3) * COLS, COLS)] = jnp.zeros((MEMBERS, COLS), BF16)
    tails = []
    for e in range(PATCHES + 2):
        t, q = divmod(e, 4)
        place = pl.ds((e + 1) * COLS, COLS)
        own = rim_ref[pl.ds(0, MEMBERS), place]
        mixed = jnp.where(lane < 32, shift(top[t], -32 * q), jnp.where(lane < 96, own, shift(low[t], 96 - 32 * q)))
        wide_rim[:, place] = mixed
        own = rim_ref[pl.ds(MEMBERS, EXTRA), place].astype(F32)[:8]
        row = jnp.zeros((6, COLS), F32)
        upper = shift(jnp.concatenate([top_tails[2 * t : 2 * t + 2], row], axis=0), -32 * q)
        lower = shift(jnp.concatenate([low_tails[2 * t : 2 * t + 2], row], axis=0), 96 - 32 * q)
        tails.append(jnp.where(tail_lane < 32, upper, jnp.where(tail_lane < 96, own, lower)))
    line = lax.broadcasted_iota(jnp.int32, (1, COLS), 1)
    row = (line >> 4) & 3
    short = ((row == 1) & (lat == 0)) | ((row == 2) & (lat == last))
    share = jnp.where(short, 1.0 / 6.0, 1.0 / 9.0)
    tail_row = lax.broadcasted_iota(jnp.int32, (EXTRA, COLS), 0)
    for t in range(PATCHES // 2 + 1):
        place = pl.ds(t * COLS, COLS)
        summed = jnp.dot(
            wide_rim[:, pl.ds(2 * t * COLS, 4 * COLS)], rim_table_ref[...], preferred_element_type=F32
        )
        mean = summed * share
        average = jnp.sum(mean, axis=0, keepdims=True) * (1.0 / MEMBERS)
        pert[pl.ds(0, MEMBERS), place] = (mean - average).astype(BF16)
        left, right = tails[2 * t], tails[2 * t + 1]
        group = tail_lane >> 5
        tail = jnp.where(
            group == 0,
            shift(left, -16),
            jnp.where(group == 1, shift(left, -48), jnp.where(group == 2, shift(right, 48), shift(right, 16))),
        )
        innovation = tail[1:2] - average
        pert[pl.ds(MEMBERS, EXTRA), place] = jnp.where(
            tail_row == 0, innovation, jnp.where(tail_row == 1, tail[0:1], 0.0)
        ).astype(BF16)


def solve_kernel(first_ref, second_ref, gram_ref, force_ref, departure_ref, base_ref, rest_ref,
                 rim_ref, rim_table_ref, out_ref,
                 pair_ref, scratch, spread, held, wide_rim, pert, sems):
    rim_perts(first_ref, second_ref, rim_ref, rim_table_ref, wide_rim, pert)
    r = lax.broadcasted_iota(jnp.int32, (MEMBERS, MEMBERS), 0)
    c = lax.broadcasted_iota(jnp.int32, (MEMBERS, MEMBERS), 1)
    eye = jnp.where(r == c, 1.0, 0.0)
    unit = eye.astype(BF16)
    base = (PATCHES // 2) * MEMBERS
    tail = first_ref[pl.ds(base, 16), :].astype(F32) + second_ref[pl.ds(base, 16), :].astype(F32)
    norms, rim_forcings = [], []
    for pair in range(PATCHES // 2):
        rows = pl.ds(pair * MEMBERS, MEMBERS)
        mixed = first_ref[rows, :].astype(F32) + second_ref[rows, :].astype(F32)
        turned = mixed.T
        diagonal = tail[8 + pair : 9 + pair]
        gains = (
            jnp.where(r >= c, mixed, turned),
            jnp.where(r > c, turned, jnp.where(r < c, mixed, diagonal)),
        )
        for k in range(2):
            p = 2 * pair + k
            lanes = pl.ds((p - k) // 2 * COLS, 2 * COLS)
            rim_gram, rim_forcing = patch_gram(pert, lanes, rim_taper(k), r == c)
            rim_forcings.append(rim_forcing)
            system = gram_ref[p] + gains[k] + rim_gram
            total = jnp.sum(jnp.sum(system * system, axis=0, keepdims=True), axis=1, keepdims=True)
            norm = jnp.sqrt(total)
            norms.append(norm)
            scaled = system * (1.0 / norm)
            split_scaled = halves(scaled)
            pair_ref[p, :MEMBERS] = halves(1.5 * scaled - 0.5 * product(split_scaled, split_scaled))
            pair_ref[p, MEMBERS:] = halves(1.5 * eye - 0.5 * scaled)

    def sweep():
        middles = [
            halves(1.5 * eye - 0.5 * product(pair_ref[p, MEMBERS:], pair_ref[p, :MEMBERS]))
            for p in range(PATCHES)
        ]
        for p in range(PATCHES):
            pair_ref[p] = halves(product(pair_ref[p], middles[p]))

    for _ in range(NS_ITERS - 2):
        sweep()
    middles = [
        halves(1.5 * eye - 0.5 * product(pair_ref[p, MEMBERS:], pair_ref[p, :MEMBERS]))
        for p in range(PATCHES)
    ]
    transforms = []
    for p in range(PATCHES):
        lower = product(pair_ref[p, MEMBERS:], middles[p])
        forcing = force_ref[p : p + 1] + tail[p : p + 1] + rim_forcings[p]
        once = jnp.sum(lower * forcing, axis=1, keepdims=True)
        mean_weight = jnp.sum(lower * once, axis=0, keepdims=True) * (1.0 / norms[p])
        scale = jnp.sqrt(MEMBERS - 1.0) / jnp.sqrt(norms[p])
        transform = (lower * scale + mean_weight).astype(BF16)
        transforms.append(jnp.concatenate([transform, unit], axis=1))

    copies = []
    for v in range(2):
        for p in range(PATCHES):
            cells = pl.ds((2 * p + v) * CELLS, CELLS)
            updated = jnp.dot(
                transforms[p],
                jnp.concatenate([departure_ref[:, cells], base_ref[:, cells]], axis=0),
                preferred_element_type=F32,
            )
            spread[v, :, pl.ds(p * CELLS, CELLS)] = updated + rest_ref[0:1, cells]
        for m in range(MEMBERS // 16):
            rows = pl.ds(m * 16, 16)
            for g in range(2):
                lines = swap_groups(
                    [spread[v, rows, pl.ds(b * CELLS + g * COLS, COLS)] for b in range(PATCHES)]
                )
                for k in range(8):
                    scratch[v, pl.ds(m * 256 + g * 8 + k, 16, stride=16), :] = lines[k]
            held[v, rows] = scratch[v, pl.ds(m * 256, 256), :].reshape(16, ROWS, COLS).astype(BF16)
            copies.append(fetch(held.at[v, rows], out_ref.at[v, rows], sems.at[v * (MEMBERS // 16) + m]))
    for copy in copies:
        copy.wait()


LIMITS = {strip_kernel: 53 * 1024 * 1024}


def call(kernel, out_shape, scratch, flops, moved, *operands, far=(), scalars=(), out_far=False):
    vmem = pl.BlockSpec(memory_space=pltpu.VMEM)
    smem = pl.BlockSpec(memory_space=pltpu.SMEM)
    anywhere = pl.BlockSpec(memory_space=pltpu.HBM)
    return pl.pallas_call(
        kernel,
        out_shape=out_shape,
        in_specs=[
            anywhere if i in far else smem if i in scalars else vmem for i in range(len(operands))
        ],
        out_specs=[anywhere if out_far else vmem] * len(out_shape),
        scratch_shapes=scratch,
        compiler_params=pltpu.CompilerParams(vmem_limit_bytes=LIMITS.get(kernel, VMEM_LIMIT)),
        cost_estimate=pl.CostEstimate(flops=flops, bytes_accessed=moved, transcendentals=0),
    )(*operands)


def pairs_inside(size):
    return [(i, i ^ 1) for i in range(size)]


def pairs_across(size, wrap):
    pairs = []
    for i in range(1, size - 1, 2):
        pairs += [(i, i + 1), (i + 1, i)]
    if wrap:
        pairs += [(size - 1, 0), (0, size - 1)]
    return pairs


def exchange(even, odd, axis, wrap):
    size = lax.axis_size(axis)
    return (
        lax.ppermute(even, axis, pairs_inside(size)),
        lax.ppermute(odd, axis, pairs_across(size, wrap)),
    )


def body(background, obs_cell, obs_count, obs_value, obs_err, land):
    slots = obs_cell.shape[-1]
    span = PATCHES * CELLS
    shape = jax.ShapeDtypeStruct
    field = pltpu.VMEM((MEMBERS, ROWS, COLS), BF16)
    lines_shape = (MEMBERS * ROWS, COLS)
    copies = pltpu.SemaphoreType.DMA
    parts = [array.reshape(1, -1).astype(F32) for array in (obs_cell, obs_value, obs_err, land, obs_count)]
    room = 3 * slots + (ROWS + 1) * COLS
    pack, start = 0.0, 0
    for part in parts:
        pack = pack + jnp.pad(part, ((0, 0), (start, room - start - part.shape[1])))
        start += part.shape[1]
    held, even, odd, tails, mask = call(
        strip_kernel,
        [
            shape((MEMBERS, ROWS, COLS), BF16),
            shape((CHANNELS, CELLS), BF16),
            shape((CHANNELS, CELLS), BF16),
            shape((EXTRA, span), BF16),
            shape((8, CELLS), F32),
        ],
        [pltpu.VMEM(lines_shape, F32), copies((PARTS,))],
        10**7, 2 * 10**6,
        background, pack,
        far=(0,),
    )
    neighbours = exchange(even, odd, "lon", True)
    blocks, table = call(
        block_kernel,
        [shape((CHANNELS, span), BF16), shape((3 * CELLS, CELLS), BF16)],
        [pltpu.VMEM(lines_shape, F32)],
        10**8, 4 * 10**6,
        held, tails,
    )
    even, odd, pert, wide = call(
        gram_kernel,
        [shape((PACKED, MEMBERS), BF16)] * 2
        + [shape((CHANNELS, span + 2 * CELLS), BF16), shape((CHANNELS, span + 4 * CELLS), BF16)],
        [],
        10**9, 3 * 10**6,
        blocks, *neighbours, table,
    )
    packed = exchange(even, odd, "lat", False)
    gram, force, departure, base, rest, rim, rim_table = call(
        centre_kernel,
        [
            shape((PATCHES, MEMBERS, MEMBERS), F32),
            shape((PATCHES, MEMBERS), F32),
            shape((MEMBERS, 2 * span), BF16),
            shape((MEMBERS, 2 * span), BF16),
            shape((8, 2 * span), F32),
            shape((CHANNELS, (PATCHES + 4) * COLS), BF16),
            shape((4 * COLS, COLS), BF16),
        ],
        [pltpu.VMEM((MEMBERS, span), BF16), field, pltpu.VMEM(lines_shape, F32), copies((PARTS,))],
        10**9, 5 * 10**6,
        pert, wide, blocks, background, mask,
        far=(3,),
    )
    (analysis,) = call(
        solve_kernel,
        [shape(background.shape, BF16)],
        [
            pltpu.VMEM((PATCHES, 2 * MEMBERS, 2 * MEMBERS), BF16),
            pltpu.VMEM((2,) + lines_shape, F32),
            pltpu.VMEM((2, MEMBERS, span), F32),
            pltpu.VMEM(background.shape, BF16),
            pltpu.VMEM((MEMBERS, (PATCHES + 4) * COLS), BF16),
            pltpu.VMEM((CHANNELS, (PATCHES // 2 + 1) * COLS), BF16),
            copies((2 * MEMBERS // 16,)),
        ],
        2 * 10**9, 5 * 10**6,
        *packed, gram, force, departure, base, rest, rim, rim_table,
        out_far=True,
    )
    return analysis


def solution(mesh):
    return jax.shard_map(
        body,
        mesh=mesh,
        in_specs=(
            P(None, None, "lat", "lon"),
            P("lat", "lon", None),
            P("lat", "lon"),
            P("lat", "lon", None),
            P("lat", "lon", None),
            P("lat", "lon"),
        ),
        out_specs=P(None, None, "lat", "lon"),
        check_vma=False,
    )
```

```python
import jax
import jax.numpy as jnp
import numpy as np
from jax import lax
from jax.experimental import pallas as pl
from jax.experimental.pallas import tpu as pltpu
from jax.sharding import PartitionSpec as P

MEMBERS = 128
PATCH = 16
RADIUS = 15
NS_ITERS = 5
ROWS = 16
COLS = 128
PATCHES = COLS // PATCH
CELLS = PATCH * PATCH
EXTRA = 16
CHANNELS = MEMBERS + EXTRA
RIMS = (PATCHES // 2) * MEMBERS + 16
PACKED = RIMS + 2 * MEMBERS + MEMBERS // 2 + EXTRA
NT = (((1,), (1,)), ((), ()))
PARTS = 4
VMEM_LIMIT = 48 * 1024 * 1024
F32 = jnp.float32
BF16 = jnp.bfloat16


def tapers():
    lane = lax.broadcasted_iota(jnp.int32, (1, 3 * CELLS), 1)
    side = lane >> 8
    row, column = (lane >> 4) & (PATCH - 1), lane & (PATCH - 1)
    span = 2.0 * (RADIUS + PATCH / 2.0)
    half = (PATCH - 1) / 2.0

    def line(place, shift):
        offset = jnp.abs(place.astype(F32) + (PATCH * shift - half))
        return jnp.where(offset < RADIUS + PATCH / 2.0, 1.0 - offset / span, 0.0)

    lon = jnp.where(side == 0, line(column, -1), jnp.where(side == 1, line(column, 0), line(column, 1)))
    inner = (row > 0) & (row < ROWS - 1)
    return [jnp.where(inner, line(row, shift) * lon, 0.0) for shift in (1, 0, -1)]


def rim_taper(first):
    lane = lax.broadcasted_iota(jnp.int32, (1, 2 * COLS), 1)
    side = (lane >> 6) - first - 1
    row, column = (lane >> 4) & 3, lane & (PATCH - 1)
    span = 2.0 * (RADIUS + PATCH / 2.0)
    half = (PATCH - 1) / 2.0
    across = jnp.where((row == 0) | (row == 3), 1.0 - (half + 1.0) / span, 1.0 - half / span)
    offset = jnp.abs(column.astype(F32) + side.astype(F32) * PATCH - half)
    along = jnp.where(offset < RADIUS + PATCH / 2.0, 1.0 - offset / span, 0.0)
    return across * along


def stencil_rows(first):
    cell = (first & (CELLS - 1)) + lax.broadcasted_iota(jnp.int32, (COLS, CELLS), 0)
    lane = lax.broadcasted_iota(jnp.int32, (COLS, CELLS), 1)
    near = jnp.abs((cell >> 4) - (lane >> 4)) <= 1
    apart = jnp.abs((cell & (PATCH - 1)) - (lane & (PATCH - 1)))
    beside = apart <= 1 if first < CELLS else apart == PATCH - 1
    return jnp.where(near & beside, 1.0, 0.0).astype(BF16)


def rim_stencil_rows(place):
    cell = lax.broadcasted_iota(jnp.int32, (COLS, COLS), 0)
    lane = lax.broadcasted_iota(jnp.int32, (COLS, COLS), 1)
    row = (lane >> 4) & 3
    step = (cell >> 4) - jnp.where(row < 2, row, row + 2)
    side = place - 1 - (lane >> 6)
    beside = jnp.abs(side * PATCH + (cell & (PATCH - 1)) - (lane & (PATCH - 1))) <= 1
    return jnp.where((step >= 0) & (step <= 2) & beside, 1.0, 0.0).astype(BF16)


def swap_groups(arrays):
    lane = lax.broadcasted_iota(jnp.int32, arrays[0].shape, 1)
    for step in (1, 2, 4):
        width = PATCH * step
        high = (lane & width) != 0
        mixed = list(arrays)
        for i in range(8):
            if i & step == 0:
                first, second = arrays[i], arrays[i + step]
                mixed[i] = jnp.where(high, pltpu.roll(second, width, 1), first)
                mixed[i + step] = jnp.where(high, second, pltpu.roll(first, COLS - width, 1))
        arrays = mixed
    return arrays


def fetch(source, target, sem):
    copy = pltpu.make_async_copy(source, target, sem)
    copy.start()
    return copy


def fetch_field(background_ref, variable, held, sems):
    part = MEMBERS // PARTS
    return [
        fetch(
            background_ref.at[variable, pl.ds(k * part, part)], held.at[pl.ds(k * part, part)], sems.at[k]
        )
        for k in range(PARTS)
    ]


def widen_lines(copies, held, lines):
    part = MEMBERS // PARTS
    for k in range(PARTS):
        if copies:
            copies[k].wait()
        for m in range(k * part // 16, (k + 1) * part // 16):
            piece = held[pl.ds(m * 16, 16)].astype(F32)
            lines[pl.ds(m * 256, 256), :] = piece.reshape(256, COLS)


def to_blocks(lines, out_ref):
    for m in range(MEMBERS // 16):
        halves = []
        for g in range(2):
            rows = [lines[pl.ds(m * 256 + g * 8 + r, 16, stride=16), :].astype(BF16) for r in range(8)]
            halves.append(swap_groups(rows))
        for b in range(PATCHES):
            both = jnp.concatenate([halves[0][b], halves[1][b]], axis=1)
            out_ref[pl.ds(m * 16, 16), pl.ds(b * CELLS, CELLS)] = both


def strip_kernel(background_ref, pack_ref, value_ref, err_ref,
                 held, even_ref, odd_ref, tails_ref, mask_ref, lines, sems):
    lon_odd = (lax.axis_index("lon") & 1) == 1
    copies = fetch_field(background_ref, 0, held, sems)
    slots = value_ref.shape[1]
    halves = []
    for g in range(2):
        rows = [
            jnp.broadcast_to(pack_ref[:, pl.ds(slots + (g * 8 + r) * COLS, COLS)].astype(F32), (8, COLS))
            for r in range(8)
        ]
        halves.append(swap_groups(rows))
    which = lax.broadcasted_iota(jnp.int32, (8, CELLS), 0)
    mask = jnp.zeros((8, CELLS), F32)
    for b in range(PATCHES):
        mask = jnp.where(which == b, jnp.concatenate([halves[0][b], halves[1][b]], axis=1), mask)
    mask_ref[...] = mask
    cell = pack_ref[:, pl.ds(0, slots)]
    count = pack_ref[:, pl.ds(slots + ROWS * COLS, COLS)][:, 0:1]
    used = lax.broadcasted_iota(jnp.int32, (1, slots), 1) < count
    err = err_ref[...]
    inverse = jnp.where(used, 1.0 / (err * err), 0.0)
    value = jnp.where(used, value_ref[...].astype(F32), 0.0)
    column = cell & (COLS - 1)
    block = column >> 4
    place = ((cell >> 7) << 4) + (column & (PATCH - 1))
    slot_block = lax.broadcasted_iota(jnp.int32, (16, value.shape[1]), 0)
    chosen = (slot_block & 7) == block
    amount = jnp.where(slot_block < 8, inverse, value)
    left = jnp.where(chosen, amount, 0.0).astype(BF16)
    spot = lax.broadcasted_iota(jnp.int32, (CELLS, value.shape[1]), 0) == place
    right = jnp.where(spot, 1.0, 0.0).astype(BF16)
    grids = lax.dot_general(left, right, NT, preferred_element_type=F32)
    precision = grids[:8] * mask
    observed = grids[8:]
    channel = lax.broadcasted_iota(jnp.int32, (EXTRA, CELLS), 0)
    for b in range(PATCHES):
        tail = jnp.where(
            channel == 0, precision[b : b + 1], jnp.where(channel == 1, observed[b : b + 1], 0.0)
        ).astype(BF16)
        tails_ref[:, pl.ds(b * CELLS, CELLS)] = tail
        if b == 0:
            west = tail
    even_ref[pl.ds(MEMBERS, EXTRA), :] = jnp.where(lon_odd, west, tail)
    odd_ref[pl.ds(MEMBERS, EXTRA), :] = jnp.where(lon_odd, tail, west)

    widen_lines(copies, held, lines)
    group = lax.broadcasted_iota(jnp.int32, (16, COLS), 1) >> 4
    for m in range(MEMBERS // 16):
        for g in range(2):
            west = jnp.zeros((16, COLS), BF16)
            east = west
            for r in range(8):
                row = lines[pl.ds(m * 256 + g * 8 + r, 16, stride=16), :].astype(BF16)
                here = group == r
                west = jnp.where(here, pltpu.roll(row, PATCH * r, 1) if r else row, west)
                east = jnp.where(here, pltpu.roll(row, PATCH * (r + 1), 1) if r < 7 else row, east)
            even_ref[pl.ds(m * 16, 16), pl.ds(g * COLS, COLS)] = jnp.where(lon_odd, west, east)
            odd_ref[pl.ds(m * 16, 16), pl.ds(g * COLS, COLS)] = jnp.where(lon_odd, east, west)


def block_kernel(held, tails_ref, blocks_ref, table_ref, lines):
    for first in range(0, 2 * CELLS, COLS):
        table_ref[pl.ds(first, COLS), :] = stencil_rows(first)
    widen_lines((), held, lines)
    to_blocks(lines, blocks_ref)
    blocks_ref[pl.ds(MEMBERS, EXTRA), :] = tails_ref[...]


def shift(piece, lanes):
    return pltpu.roll(piece, lanes % COLS, 1) if lanes % COLS else piece


def quarters(pieces, lane):
    tile = pieces[0]
    for q in range(1, len(pieces)):
        tile = jnp.where((lane >> 5) == q, shift(pieces[q], 32 * q), tile)
    return tile


def gram_kernel(blocks_ref, first_ref, second_ref, table_ref, even_ref, odd_ref, pert, wide):
    lat_odd = (lax.axis_index("lat") & 1) == 1
    lon_odd = (lax.axis_index("lon") & 1) == 1
    span = PATCHES * CELLS
    wide[:, pl.ds(0, CELLS)] = jnp.zeros((CHANNELS, CELLS), BF16)
    wide[:, pl.ds(span + 3 * CELLS, CELLS)] = jnp.zeros((CHANNELS, CELLS), BF16)
    wide[:, pl.ds(2 * CELLS, span)] = blocks_ref[...]
    one, two = first_ref[...], second_ref[...]
    wide[:, pl.ds(CELLS, CELLS)] = jnp.where(lon_odd, one, two)
    wide[:, pl.ds(span + 2 * CELLS, CELLS)] = jnp.where(lon_odd, two, one)

    tail_row = lax.broadcasted_iota(jnp.int32, (EXTRA, CELLS), 0)
    column = lax.broadcasted_iota(jnp.int32, (MEMBERS, CELLS), 1) & (PATCH - 1)
    rows = pl.ds(0, MEMBERS)
    for e in range(PATCHES + 2):
        left, own, right = (wide[rows, pl.ds((e + k) * CELLS, CELLS)] for k in range(3))
        beside = jnp.where(column == PATCH - 1, left, jnp.where(column == 0, right, jnp.zeros_like(own)))
        summed = jnp.dot(
            jnp.concatenate([own, beside], axis=1), table_ref[...], preferred_element_type=F32
        )
        mean = summed * (1.0 / 9.0)
        average = jnp.sum(mean, axis=0, keepdims=True) * (1.0 / MEMBERS)
        pert[pl.ds(0, MEMBERS), pl.ds(e * CELLS, CELLS)] = (mean - average).astype(BF16)
        tail = wide[pl.ds(MEMBERS, EXTRA), pl.ds((e + 1) * CELLS, CELLS)].astype(F32)
        innovation = tail[1:2] - average
        pert[pl.ds(MEMBERS, EXTRA), pl.ds(e * CELLS, CELLS)] = jnp.where(
            tail_row == 0, innovation, jnp.where(tail_row == 1, tail[0:1], 0.0)
        ).astype(BF16)

    write_message(pert, wide, even_ref, lat_odd)
    write_message(pert, wide, odd_ref, jnp.logical_not(lat_odd))


def write_message(pert, wide, out_ref, upward):
    lane = lax.broadcasted_iota(jnp.int32, (MEMBERS, COLS), 1)
    tail_lane = lax.broadcasted_iota(jnp.int32, (EXTRA, COLS), 1)

    def near_rows(rows, e):
        first, last = (wide[rows, pl.ds((e + 1) * CELLS + part * COLS, COLS)] for part in range(2))
        return jnp.where(upward, first, shift(last, 32))

    tiles, tails = [], []
    for t in range(3):
        some = range(4 * t, min(4 * t + 4, PATCHES + 2))
        tiles.append(quarters([near_rows(pl.ds(0, MEMBERS), e) for e in some], lane))
        tail = [near_rows(pl.ds(MEMBERS, EXTRA), e).astype(F32) for e in some]
        tails.append(quarters(tail, tail_lane)[0:2])
    half = MEMBERS // 2
    tiles[2] = jnp.where(lane[:half] < 64, tiles[2][:half], shift(tiles[2][half:], 64))
    tiles.append(jnp.concatenate(tails + [jnp.zeros((EXTRA - 6, COLS), F32)], axis=0).astype(BF16))
    start = RIMS
    for tile in tiles:
        out_ref[pl.ds(start, tile.shape[0]), :] = tile
        start += tile.shape[0]

    r = lax.broadcasted_iota(jnp.int32, (MEMBERS, MEMBERS), 0)
    c = lax.broadcasted_iota(jnp.int32, (MEMBERS, MEMBERS), 1)
    lower = r >= c
    same = r == c
    above, _, below = tapers()
    taper = jnp.where(upward, above, below)
    forcings, diagonals = [], []
    for pair in range(PATCHES // 2):
        first, forcing = patch_gram(pert, window_of(2 * pair), taper, same)
        forcings.append(forcing)
        second, forcing = patch_gram(pert, window_of(2 * pair + 1), taper, same)
        forcings.append(forcing)
        diagonals.append(jnp.sum(jnp.where(same, second, 0.0), axis=0, keepdims=True))
        out_ref[pl.ds(pair * MEMBERS, MEMBERS), :] = jnp.where(lower, first, second).astype(BF16)
    tail = forcings + diagonals + [jnp.zeros((4, MEMBERS), F32)]
    out_ref[pl.ds((PATCHES // 2) * MEMBERS, 16), :] = jnp.concatenate(tail, axis=0).astype(BF16)


def patch_gram(pert, lanes, taper, same):
    window = pert[:, lanes]
    precision = window[MEMBERS:].astype(F32)[1:2]
    scaled = (window[:MEMBERS].astype(F32) * (precision * taper)).astype(BF16)
    full = lax.dot_general(scaled, window, NT, preferred_element_type=F32)
    forcing = jnp.sum(jnp.where(same, full[:, MEMBERS : MEMBERS + 1], 0.0), axis=0, keepdims=True)
    return full[:, :MEMBERS], forcing


def window_of(p):
    return pl.ds(p * CELLS, 3 * CELLS)


def centre_kernel(pert, wide, blocks_ref, background_ref, mask_ref,
                  gram_ref, force_ref, departure_ref, base_ref, rest_ref, rim_ref, rim_table_ref,
                  soil, held, lines, sems):
    copies = fetch_field(background_ref, 1, held, sems)
    r = lax.broadcasted_iota(jnp.int32, (MEMBERS, MEMBERS), 0)
    c = lax.broadcasted_iota(jnp.int32, (MEMBERS, MEMBERS), 1)
    same = r == c
    taper = tapers()[1]
    forcings = []
    for p in range(PATCHES):
        gram, forcing = patch_gram(pert, window_of(p), taper, same)
        gram_ref[p] = gram + jnp.where(same, MEMBERS - 1.0, 0.0)
        forcings.append(forcing)
    force_ref[...] = jnp.concatenate(forcings, axis=0)
    for place in range(4):
        rim_table_ref[pl.ds(place * COLS, COLS), :] = rim_stencil_rows(place)
    lane = lax.broadcasted_iota(jnp.int32, (CHANNELS, COLS), 1)
    for e in range(PATCHES + 4):
        upper = shift(wide[:, pl.ds(e * CELLS, COLS)], 32)
        lower = shift(wide[:, pl.ds(e * CELLS + COLS, COLS)], -32)
        rim_ref[:, pl.ds(e * COLS, COLS)] = jnp.where(lane < 64, upper, lower)
    widen_lines(copies, held, lines)
    to_blocks(lines, soil)
    for p in range(PATCHES):
        cells = pl.ds(p * CELLS, CELLS)
        land = mask_ref[p : p + 1, :] != 0.0
        for v, raw in enumerate((blocks_ref[pl.ds(0, MEMBERS), cells], soil[:, cells])):
            raw = raw.astype(F32)
            mean = jnp.sum(raw, axis=0, keepdims=True) * (1.0 / MEMBERS)
            place = pl.ds((2 * p + v) * CELLS, CELLS)
            coarse = mean.astype(BF16).astype(F32)
            departure_ref[:, place] = jnp.where(land, raw - mean, 0.0).astype(BF16)
            base_ref[:, place] = jnp.where(land, coarse, raw).astype(BF16)
            rest_ref[:, place] = jnp.broadcast_to(jnp.where(land, mean - coarse, 0.0), (8, CELLS))


def split(a):
    high = a.astype(BF16)
    return high, (a - high.astype(F32)).astype(BF16)


def product(a, b):
    a_high, a_low = split(a)
    b_high, b_low = split(b)
    wide = jnp.concatenate([b_high, b_low], axis=1)
    out = jnp.dot(
        jnp.concatenate([a_high, a_low], axis=1),
        jnp.concatenate([wide, wide], axis=0),
        preferred_element_type=F32,
    )
    return out[:, :MEMBERS] + out[:, MEMBERS:]


def halves(a):
    return jnp.concatenate(split(a), axis=1)


def product(a, b):
    out = jnp.dot(a, jnp.concatenate([b, b], axis=0), preferred_element_type=F32)
    return out[:, :MEMBERS] + out[:, MEMBERS:]


def rim_perts(first_ref, second_ref, rim_ref, rim_table_ref, wide_rim, pert):
    lat = lax.axis_index("lat")
    lat_odd = (lat & 1) == 1
    last = lax.axis_size("lat") - 1
    half = MEMBERS // 2

    def tiles_of(source):
        folded = source(RIMS + 2 * MEMBERS, half)
        tails = source(RIMS + 2 * MEMBERS + half, EXTRA).astype(F32)
        tiles = [source(RIMS, MEMBERS), source(RIMS + MEMBERS, MEMBERS)]
        return tiles + [jnp.concatenate([folded, shift(folded, 64)], axis=0)], tails

    def above(start, size):
        rows = pl.ds(start, size)
        return jnp.where(lat_odd, first_ref[rows, :], second_ref[rows, :])

    def below(start, size):
        rows = pl.ds(start, size)
        return jnp.where(lat_odd, second_ref[rows, :], first_ref[rows, :])

    top, top_tails = tiles_of(above)
    low, low_tails = tiles_of(below)
    lane = lax.broadcasted_iota(jnp.int32, (MEMBERS, COLS), 1)
    tail_lane = lax.broadcasted_iota(jnp.int32, (8, COLS), 1)
    wide_rim[:, pl.ds(0, COLS)] = jnp.zeros((MEMBERS, COLS), BF16)
    wide_rim[:, pl.ds((PATCHES + 3) * COLS, COLS)] = jnp.zeros((MEMBERS, COLS), BF16)
    tails = []
    for e in range(PATCHES + 2):
        t, q = divmod(e, 4)
        place = pl.ds((e + 1) * COLS, COLS)
        own = rim_ref[pl.ds(0, MEMBERS), place]
        mixed = jnp.where(lane < 32, shift(top[t], -32 * q), jnp.where(lane < 96, own, shift(low[t], 96 - 32 * q)))
        wide_rim[:, place] = mixed
        own = rim_ref[pl.ds(MEMBERS, EXTRA), place].astype(F32)[:8]
        row = jnp.zeros((6, COLS), F32)
        upper = shift(jnp.concatenate([top_tails[2 * t : 2 * t + 2], row], axis=0), -32 * q)
        lower = shift(jnp.concatenate([low_tails[2 * t : 2 * t + 2], row], axis=0), 96 - 32 * q)
        tails.append(jnp.where(tail_lane < 32, upper, jnp.where(tail_lane < 96, own, lower)))
    line = lax.broadcasted_iota(jnp.int32, (1, COLS), 1)
    row = (line >> 4) & 3
    short = ((row == 1) & (lat == 0)) | ((row == 2) & (lat == last))
    share = jnp.where(short, 1.0 / 6.0, 1.0 / 9.0)
    tail_row = lax.broadcasted_iota(jnp.int32, (EXTRA, COLS), 0)
    for t in range(PATCHES // 2 + 1):
        place = pl.ds(t * COLS, COLS)
        summed = jnp.dot(
            wide_rim[:, pl.ds(2 * t * COLS, 4 * COLS)], rim_table_ref[...], preferred_element_type=F32
        )
        mean = summed * share
        average = jnp.sum(mean, axis=0, keepdims=True) * (1.0 / MEMBERS)
        pert[pl.ds(0, MEMBERS), place] = (mean - average).astype(BF16)
        left, right = tails[2 * t], tails[2 * t + 1]
        group = tail_lane >> 5
        tail = jnp.where(
            group == 0,
            shift(left, -16),
            jnp.where(group == 1, shift(left, -48), jnp.where(group == 2, shift(right, 48), shift(right, 16))),
        )
        innovation = tail[1:2] - average
        pert[pl.ds(MEMBERS, EXTRA), place] = jnp.where(
            tail_row == 0, innovation, jnp.where(tail_row == 1, tail[0:1], 0.0)
        ).astype(BF16)


def solve_kernel(first_ref, second_ref, gram_ref, force_ref, departure_ref, base_ref, rest_ref,
                 rim_ref, rim_table_ref, out_ref,
                 pair_ref, scratch, spread, held, wide_rim, pert, sems):
    rim_perts(first_ref, second_ref, rim_ref, rim_table_ref, wide_rim, pert)
    r = lax.broadcasted_iota(jnp.int32, (MEMBERS, MEMBERS), 0)
    c = lax.broadcasted_iota(jnp.int32, (MEMBERS, MEMBERS), 1)
    eye = jnp.where(r == c, 1.0, 0.0)
    unit = eye.astype(BF16)
    base = (PATCHES // 2) * MEMBERS
    tail = first_ref[pl.ds(base, 16), :].astype(F32) + second_ref[pl.ds(base, 16), :].astype(F32)
    norms, rim_forcings = [], []
    for p in range(PATCHES):
        lanes = pl.ds(p // 2 * COLS, 2 * COLS)
        rim_gram, rim_forcing = patch_gram(pert, lanes, rim_taper(p % 2), r == c)
        rim_forcings.append(rim_forcing)
        spread[0, :, pl.ds(p * MEMBERS, MEMBERS)] = rim_gram
    for pair in range(PATCHES // 2):
        rows = pl.ds(pair * MEMBERS, MEMBERS)
        mixed = first_ref[rows, :].astype(F32) + second_ref[rows, :].astype(F32)
        turned = mixed.T
        diagonal = tail[8 + pair : 9 + pair]
        gains = (
            jnp.where(r >= c, mixed, turned),
            jnp.where(r > c, turned, jnp.where(r < c, mixed, diagonal)),
        )
        for k in range(2):
            p = 2 * pair + k
            system = gram_ref[p] + gains[k] + spread[0, :, pl.ds(p * MEMBERS, MEMBERS)]
            total = jnp.sum(jnp.sum(system * system, axis=0, keepdims=True), axis=1, keepdims=True)
            norm = jnp.sqrt(total)
            norms.append(norm)
            scaled = system * (1.0 / norm)
            split_scaled = halves(scaled)
            pair_ref[p, :MEMBERS] = halves(1.5 * scaled - 0.5 * product(split_scaled, split_scaled))
            pair_ref[p, MEMBERS:] = halves(1.5 * eye - 0.5 * scaled)

    def sweep():
        middles = [
            halves(1.5 * eye - 0.5 * product(pair_ref[p, MEMBERS:], pair_ref[p, :MEMBERS]))
            for p in range(PATCHES)
        ]
        for p in range(PATCHES):
            pair_ref[p] = halves(product(pair_ref[p], middles[p]))

    for _ in range(NS_ITERS - 2):
        sweep()
    middles = [
        halves(1.5 * eye - 0.5 * product(pair_ref[p, MEMBERS:], pair_ref[p, :MEMBERS]))
        for p in range(PATCHES)
    ]
    transforms = []
    for p in range(PATCHES):
        lower = product(pair_ref[p, MEMBERS:], middles[p])
        forcing = force_ref[p : p + 1] + tail[p : p + 1] + rim_forcings[p]
        once = jnp.sum(lower * forcing, axis=1, keepdims=True)
        mean_weight = jnp.sum(lower * once, axis=0, keepdims=True) * (1.0 / norms[p])
        scale = jnp.sqrt(MEMBERS - 1.0) / jnp.sqrt(norms[p])
        transform = (lower * scale + mean_weight).astype(BF16)
        transforms.append(jnp.concatenate([transform, unit], axis=1))

    copies = []
    for v in range(2):
        for p in range(PATCHES):
            cells = pl.ds((2 * p + v) * CELLS, CELLS)
            updated = jnp.dot(
                transforms[p],
                jnp.concatenate([departure_ref[:, cells], base_ref[:, cells]], axis=0),
                preferred_element_type=F32,
            )
            spread[v, :, pl.ds(p * CELLS, CELLS)] = updated + rest_ref[0:1, cells]
        for m in range(MEMBERS // 16):
            rows = pl.ds(m * 16, 16)
            for g in range(2):
                lines = swap_groups(
                    [spread[v, rows, pl.ds(b * CELLS + g * COLS, COLS)] for b in range(PATCHES)]
                )
                for k in range(8):
                    scratch[v, pl.ds(m * 256 + g * 8 + k, 16, stride=16), :] = lines[k]
            held[v, rows] = scratch[v, pl.ds(m * 256, 256), :].reshape(16, ROWS, COLS).astype(BF16)
            copies.append(fetch(held.at[v, rows], out_ref.at[v, rows], sems.at[v * (MEMBERS // 16) + m]))
    for copy in copies:
        copy.wait()


LIMITS = {strip_kernel: 53 * 1024 * 1024}


def call(kernel, out_shape, scratch, flops, moved, *operands, far=(), scalars=(), out_far=False):
    vmem = pl.BlockSpec(memory_space=pltpu.VMEM)
    smem = pl.BlockSpec(memory_space=pltpu.SMEM)
    anywhere = pl.BlockSpec(memory_space=pltpu.HBM)
    return pl.pallas_call(
        kernel,
        out_shape=out_shape,
        in_specs=[
            anywhere if i in far else smem if i in scalars else vmem for i in range(len(operands))
        ],
        out_specs=[anywhere if out_far else vmem] * len(out_shape),
        scratch_shapes=scratch,
        compiler_params=pltpu.CompilerParams(vmem_limit_bytes=LIMITS.get(kernel, VMEM_LIMIT)),
        cost_estimate=pl.CostEstimate(flops=flops, bytes_accessed=moved, transcendentals=0),
    )(*operands)


def pairs_inside(size):
    return [(i, i ^ 1) for i in range(size)]


def pairs_across(size, wrap):
    pairs = []
    for i in range(1, size - 1, 2):
        pairs += [(i, i + 1), (i + 1, i)]
    if wrap:
        pairs += [(size - 1, 0), (0, size - 1)]
    return pairs


def exchange(even, odd, axis, wrap):
    size = lax.axis_size(axis)
    return (
        lax.ppermute(even, axis, pairs_inside(size)),
        lax.ppermute(odd, axis, pairs_across(size, wrap)),
    )


def body(background, obs_cell, obs_count, obs_value, obs_err, land):
    slots = obs_cell.shape[-1]
    span = PATCHES * CELLS
    shape = jax.ShapeDtypeStruct
    field = pltpu.VMEM((MEMBERS, ROWS, COLS), BF16)
    lines_shape = (MEMBERS * ROWS, COLS)
    copies = pltpu.SemaphoreType.DMA
    parts = [array.reshape(1, -1) for array in (obs_cell, land, obs_count)]
    room = slots + (ROWS + 1) * COLS
    pack, start = 0, 0
    for part in parts:
        pack = pack + jnp.pad(part, ((0, 0), (start, room - start - part.shape[1])))
        start += part.shape[1]
    held, even, odd, tails, mask = call(
        strip_kernel,
        [
            shape((MEMBERS, ROWS, COLS), BF16),
            shape((CHANNELS, CELLS), BF16),
            shape((CHANNELS, CELLS), BF16),
            shape((EXTRA, span), BF16),
            shape((8, CELLS), F32),
        ],
        [pltpu.VMEM(lines_shape, F32), copies((PARTS,))],
        10**7, 2 * 10**6,
        background, pack, obs_value.reshape(1, slots), obs_err.reshape(1, slots),
        far=(0,),
    )
    neighbours = exchange(even, odd, "lon", True)
    blocks, table = call(
        block_kernel,
        [shape((CHANNELS, span), BF16), shape((2 * CELLS, CELLS), BF16)],
        [pltpu.VMEM(lines_shape, F32)],
        10**8, 4 * 10**6,
        held, tails,
    )
    even, odd, pert, wide = call(
        gram_kernel,
        [shape((PACKED, MEMBERS), BF16)] * 2
        + [shape((CHANNELS, span + 2 * CELLS), BF16), shape((CHANNELS, span + 4 * CELLS), BF16)],
        [],
        10**9, 3 * 10**6,
        blocks, *neighbours, table,
    )
    packed = exchange(even, odd, "lat", False)
    gram, force, departure, base, rest, rim, rim_table = call(
        centre_kernel,
        [
            shape((PATCHES, MEMBERS, MEMBERS), F32),
            shape((PATCHES, MEMBERS), F32),
            shape((MEMBERS, 2 * span), BF16),
            shape((MEMBERS, 2 * span), BF16),
            shape((8, 2 * span), F32),
            shape((CHANNELS, (PATCHES + 4) * COLS), BF16),
            shape((4 * COLS, COLS), BF16),
        ],
        [pltpu.VMEM((MEMBERS, span), BF16), field, pltpu.VMEM(lines_shape, F32), copies((PARTS,))],
        10**9, 5 * 10**6,
        pert, wide, blocks, background, mask,
        far=(3,),
    )
    (analysis,) = call(
        solve_kernel,
        [shape(background.shape, BF16)],
        [
            pltpu.VMEM((PATCHES, 2 * MEMBERS, 2 * MEMBERS), BF16),
            pltpu.VMEM((2,) + lines_shape, F32),
            pltpu.VMEM((2, MEMBERS, span), F32),
            pltpu.VMEM(background.shape, BF16),
            pltpu.VMEM((MEMBERS, (PATCHES + 4) * COLS), BF16),
            pltpu.VMEM((CHANNELS, (PATCHES // 2 + 1) * COLS), BF16),
            copies((2 * MEMBERS // 16,)),
        ],
        2 * 10**9, 5 * 10**6,
        *packed, gram, force, departure, base, rest, rim, rim_table,
        out_far=True,
    )
    return analysis


def solution(mesh):
    return jax.shard_map(
        body,
        mesh=mesh,
        in_specs=(
            P(None, None, "lat", "lon"),
            P("lat", "lon", None),
            P("lat", "lon"),
            P("lat", "lon", None),
            P("lat", "lon", None),
            P("lat", "lon"),
        ),
        out_specs=P(None, None, "lat", "lon"),
        check_vma=False,
    )
```

```python
import jax
import jax.numpy as jnp
import numpy as np
from jax import lax
from jax.experimental import pallas as pl
from jax.experimental.pallas import tpu as pltpu
from jax.sharding import PartitionSpec as P

MEMBERS = 128
PATCH = 16
RADIUS = 15
NS_ITERS = 5
ROWS = 16
COLS = 128
PATCHES = COLS // PATCH
CELLS = PATCH * PATCH
EXTRA = 16
CHANNELS = MEMBERS + EXTRA
RIMS = (PATCHES // 2) * MEMBERS + 16
PACKED = RIMS + 2 * MEMBERS + MEMBERS // 2 + EXTRA
NT = (((1,), (1,)), ((), ()))
PARTS = 4
VMEM_LIMIT = 48 * 1024 * 1024
F32 = jnp.float32
BF16 = jnp.bfloat16


def tapers():
    lane = lax.broadcasted_iota(jnp.int32, (1, 3 * CELLS), 1)
    side = lane >> 8
    row, column = (lane >> 4) & (PATCH - 1), lane & (PATCH - 1)
    span = 2.0 * (RADIUS + PATCH / 2.0)
    half = (PATCH - 1) / 2.0

    def line(place, shift):
        offset = jnp.abs(place.astype(F32) + (PATCH * shift - half))
        return jnp.where(offset < RADIUS + PATCH / 2.0, 1.0 - offset / span, 0.0)

    lon = jnp.where(side == 0, line(column, -1), jnp.where(side == 1, line(column, 0), line(column, 1)))
    inner = (row > 0) & (row < ROWS - 1)
    return [jnp.where(inner, line(row, shift) * lon, 0.0) for shift in (1, 0, -1)]


def rim_taper(first):
    lane = lax.broadcasted_iota(jnp.int32, (1, 2 * COLS), 1)
    side = (lane >> 6) - first - 1
    row, column = (lane >> 4) & 3, lane & (PATCH - 1)
    span = 2.0 * (RADIUS + PATCH / 2.0)
    half = (PATCH - 1) / 2.0
    across = jnp.where((row == 0) | (row == 3), 1.0 - (half + 1.0) / span, 1.0 - half / span)
    offset = jnp.abs(column.astype(F32) + side.astype(F32) * PATCH - half)
    along = jnp.where(offset < RADIUS + PATCH / 2.0, 1.0 - offset / span, 0.0)
    return across * along


def stencil_rows(first):
    cell = (first & (CELLS - 1)) + lax.broadcasted_iota(jnp.int32, (COLS, CELLS), 0)
    lane = lax.broadcasted_iota(jnp.int32, (COLS, CELLS), 1)
    near = jnp.abs((cell >> 4) - (lane >> 4)) <= 1
    apart = jnp.abs((cell & (PATCH - 1)) - (lane & (PATCH - 1)))
    beside = apart <= 1 if first < CELLS else apart == PATCH - 1
    return jnp.where(near & beside, 1.0, 0.0).astype(BF16)


def rim_stencil_rows(place):
    cell = lax.broadcasted_iota(jnp.int32, (COLS, COLS), 0)
    lane = lax.broadcasted_iota(jnp.int32, (COLS, COLS), 1)
    row = (lane >> 4) & 3
    step = (cell >> 4) - jnp.where(row < 2, row, row + 2)
    side = place - 1 - (lane >> 6)
    beside = jnp.abs(side * PATCH + (cell & (PATCH - 1)) - (lane & (PATCH - 1))) <= 1
    return jnp.where((step >= 0) & (step <= 2) & beside, 1.0, 0.0).astype(BF16)


def swap_groups(arrays):
    lane = lax.broadcasted_iota(jnp.int32, arrays[0].shape, 1)
    for step in (1, 2, 4):
        width = PATCH * step
        high = (lane & width) != 0
        mixed = list(arrays)
        for i in range(8):
            if i & step == 0:
                first, second = arrays[i], arrays[i + step]
                mixed[i] = jnp.where(high, pltpu.roll(second, width, 1), first)
                mixed[i + step] = jnp.where(high, second, pltpu.roll(first, COLS - width, 1))
        arrays = mixed
    return arrays


def shift(piece, lanes):
    return pltpu.roll(piece, lanes % COLS, 1) if lanes % COLS else piece


def turn_groups(block, p):
    return jnp.concatenate([shift(block[:, :COLS], PATCH * p), shift(block[:, COLS:], PATCH * p)], axis=1)


def turned_lines(arrays):
    group = lax.broadcasted_iota(jnp.int32, arrays[0].shape, 1) >> 4
    for step in (1, 2, 4):
        odd = (group & step) != 0
        arrays = [jnp.where(odd, arrays[(i + step) % 8], arrays[i]) for i in range(8)]
    return [shift(arrays[-r % 8], -PATCH * r) for r in range(8)]


def fetch(source, target, sem):
    copy = pltpu.make_async_copy(source, target, sem)
    copy.start()
    return copy


def fetch_field(background_ref, variable, held, sems):
    part = MEMBERS // PARTS
    return [
        fetch(
            background_ref.at[variable, pl.ds(k * part, part)], held.at[pl.ds(k * part, part)], sems.at[k]
        )
        for k in range(PARTS)
    ]


def widen_lines(copies, held, lines):
    part = MEMBERS // PARTS
    for k in range(PARTS):
        if copies:
            copies[k].wait()
        for m in range(k * part // 16, (k + 1) * part // 16):
            piece = held[pl.ds(m * 16, 16)].astype(F32)
            lines[pl.ds(m * 256, 256), :] = piece.reshape(256, COLS)


def to_blocks(lines, out_ref):
    for m in range(MEMBERS // 16):
        halves = []
        for g in range(2):
            rows = [lines[pl.ds(m * 256 + g * 8 + r, 16, stride=16), :].astype(BF16) for r in range(8)]
            halves.append(swap_groups(rows))
        for b in range(PATCHES):
            both = jnp.concatenate([halves[0][b], halves[1][b]], axis=1)
            out_ref[pl.ds(m * 16, 16), pl.ds(b * CELLS, CELLS)] = both


def strip_kernel(background_ref, pack_ref, value_ref, err_ref,
                 held, even_ref, odd_ref, tails_ref, mask_ref, lines, sems):
    lon_odd = (lax.axis_index("lon") & 1) == 1
    copies = fetch_field(background_ref, 0, held, sems)
    slots = value_ref.shape[1]
    halves = []
    for g in range(2):
        rows = [
            jnp.broadcast_to(pack_ref[:, pl.ds(slots + (g * 8 + r) * COLS, COLS)].astype(F32), (8, COLS))
            for r in range(8)
        ]
        halves.append(swap_groups(rows))
    which = lax.broadcasted_iota(jnp.int32, (8, CELLS), 0)
    mask = jnp.zeros((8, CELLS), F32)
    for b in range(PATCHES):
        mask = jnp.where(which == b, jnp.concatenate([halves[0][b], halves[1][b]], axis=1), mask)
    mask_ref[...] = mask
    cell = pack_ref[:, pl.ds(0, slots)]
    count = pack_ref[:, pl.ds(slots + ROWS * COLS, COLS)][:, 0:1]
    used = lax.broadcasted_iota(jnp.int32, (1, slots), 1) < count
    err = err_ref[...]
    inverse = jnp.where(used, 1.0 / (err * err), 0.0)
    value = jnp.where(used, value_ref[...].astype(F32), 0.0)
    column = cell & (COLS - 1)
    block = column >> 4
    place = ((cell >> 7) << 4) + (column & (PATCH - 1))
    slot_block = lax.broadcasted_iota(jnp.int32, (16, value.shape[1]), 0)
    chosen = (slot_block & 7) == block
    amount = jnp.where(slot_block < 8, inverse, value)
    left = jnp.where(chosen, amount, 0.0).astype(BF16)
    spot = lax.broadcasted_iota(jnp.int32, (CELLS, value.shape[1]), 0) == place
    right = jnp.where(spot, 1.0, 0.0).astype(BF16)
    grids = lax.dot_general(left, right, NT, preferred_element_type=F32)
    precision = grids[:8] * mask
    observed = grids[8:]
    channel = lax.broadcasted_iota(jnp.int32, (EXTRA, CELLS), 0)
    for b in range(PATCHES):
        tail = jnp.where(
            channel == 0, precision[b : b + 1], jnp.where(channel == 1, observed[b : b + 1], 0.0)
        ).astype(BF16)
        tails_ref[:, pl.ds(b * CELLS, CELLS)] = tail
        if b == 0:
            west = tail
    even_ref[pl.ds(MEMBERS, EXTRA), :] = jnp.where(lon_odd, west, tail)
    odd_ref[pl.ds(MEMBERS, EXTRA), :] = jnp.where(lon_odd, tail, west)

    widen_lines(copies, held, lines)
    group = lax.broadcasted_iota(jnp.int32, (16, COLS), 1) >> 4
    for m in range(MEMBERS // 16):
        for g in range(2):
            west = jnp.zeros((16, COLS), BF16)
            east = west
            for r in range(8):
                row = lines[pl.ds(m * 256 + g * 8 + r, 16, stride=16), :].astype(BF16)
                here = group == r
                west = jnp.where(here, pltpu.roll(row, PATCH * r, 1) if r else row, west)
                east = jnp.where(here, pltpu.roll(row, PATCH * (r + 1), 1) if r < 7 else row, east)
            even_ref[pl.ds(m * 16, 16), pl.ds(g * COLS, COLS)] = jnp.where(lon_odd, west, east)
            odd_ref[pl.ds(m * 16, 16), pl.ds(g * COLS, COLS)] = jnp.where(lon_odd, east, west)


def block_kernel(held, tails_ref, blocks_ref, table_ref, lines):
    for first in range(0, 2 * CELLS, COLS):
        table_ref[pl.ds(first, COLS), :] = stencil_rows(first)
    widen_lines((), held, lines)
    to_blocks(lines, blocks_ref)
    blocks_ref[pl.ds(MEMBERS, EXTRA), :] = tails_ref[...]


def quarters(pieces, lane):
    tile = pieces[0]
    for q in range(1, len(pieces)):
        tile = jnp.where((lane >> 5) == q, shift(pieces[q], 32 * q), tile)
    return tile


def gram_kernel(blocks_ref, first_ref, second_ref, table_ref, even_ref, odd_ref, pert, wide):
    lat_odd = (lax.axis_index("lat") & 1) == 1
    lon_odd = (lax.axis_index("lon") & 1) == 1
    span = PATCHES * CELLS
    wide[:, pl.ds(0, CELLS)] = jnp.zeros((CHANNELS, CELLS), BF16)
    wide[:, pl.ds(span + 3 * CELLS, CELLS)] = jnp.zeros((CHANNELS, CELLS), BF16)
    wide[:, pl.ds(2 * CELLS, span)] = blocks_ref[...]
    one, two = first_ref[...], second_ref[...]
    wide[:, pl.ds(CELLS, CELLS)] = jnp.where(lon_odd, one, two)
    wide[:, pl.ds(span + 2 * CELLS, CELLS)] = jnp.where(lon_odd, two, one)

    tail_row = lax.broadcasted_iota(jnp.int32, (EXTRA, CELLS), 0)
    column = lax.broadcasted_iota(jnp.int32, (MEMBERS, CELLS), 1) & (PATCH - 1)
    rows = pl.ds(0, MEMBERS)
    for e in range(PATCHES + 2):
        left, own, right = (wide[rows, pl.ds((e + k) * CELLS, CELLS)] for k in range(3))
        beside = jnp.where(column == PATCH - 1, left, jnp.where(column == 0, right, jnp.zeros_like(own)))
        summed = jnp.dot(
            jnp.concatenate([own, beside], axis=1), table_ref[...], preferred_element_type=F32
        )
        mean = summed * (1.0 / 9.0)
        average = jnp.sum(mean, axis=0, keepdims=True) * (1.0 / MEMBERS)
        pert[pl.ds(0, MEMBERS), pl.ds(e * CELLS, CELLS)] = (mean - average).astype(BF16)
        tail = wide[pl.ds(MEMBERS, EXTRA), pl.ds((e + 1) * CELLS, CELLS)].astype(F32)
        innovation = tail[1:2] - average
        pert[pl.ds(MEMBERS, EXTRA), pl.ds(e * CELLS, CELLS)] = jnp.where(
            tail_row == 0, innovation, jnp.where(tail_row == 1, tail[0:1], 0.0)
        ).astype(BF16)

    write_message(pert, wide, even_ref, lat_odd)
    write_message(pert, wide, odd_ref, jnp.logical_not(lat_odd))


def write_message(pert, wide, out_ref, upward):
    lane = lax.broadcasted_iota(jnp.int32, (MEMBERS, COLS), 1)
    tail_lane = lax.broadcasted_iota(jnp.int32, (EXTRA, COLS), 1)

    def near_rows(rows, e):
        first, last = (wide[rows, pl.ds((e + 1) * CELLS + part * COLS, COLS)] for part in range(2))
        return jnp.where(upward, first, shift(last, 32))

    tiles, tails = [], []
    for t in range(3):
        some = range(4 * t, min(4 * t + 4, PATCHES + 2))
        tiles.append(quarters([near_rows(pl.ds(0, MEMBERS), e) for e in some], lane))
        tail = [near_rows(pl.ds(MEMBERS, EXTRA), e).astype(F32) for e in some]
        tails.append(quarters(tail, tail_lane)[0:2])
    half = MEMBERS // 2
    tiles[2] = jnp.where(lane[:half] < 64, tiles[2][:half], shift(tiles[2][half:], 64))
    tiles.append(jnp.concatenate(tails + [jnp.zeros((EXTRA - 6, COLS), F32)], axis=0).astype(BF16))
    start = RIMS
    for tile in tiles:
        out_ref[pl.ds(start, tile.shape[0]), :] = tile
        start += tile.shape[0]

    r = lax.broadcasted_iota(jnp.int32, (MEMBERS, MEMBERS), 0)
    c = lax.broadcasted_iota(jnp.int32, (MEMBERS, MEMBERS), 1)
    lower = r >= c
    same = r == c
    above, _, below = tapers()
    taper = jnp.where(upward, above, below)
    forcings, diagonals = [], []
    for pair in range(PATCHES // 2):
        first, forcing = patch_gram(pert, window_of(2 * pair), taper, same)
        forcings.append(forcing)
        second, forcing = patch_gram(pert, window_of(2 * pair + 1), taper, same)
        forcings.append(forcing)
        diagonals.append(jnp.sum(jnp.where(same, second, 0.0), axis=0, keepdims=True))
        out_ref[pl.ds(pair * MEMBERS, MEMBERS), :] = jnp.where(lower, first, second).astype(BF16)
    tail = forcings + diagonals + [jnp.zeros((4, MEMBERS), F32)]
    out_ref[pl.ds((PATCHES // 2) * MEMBERS, 16), :] = jnp.concatenate(tail, axis=0).astype(BF16)


def patch_gram(pert, lanes, taper, same):
    window = pert[:, lanes]
    precision = window[MEMBERS:].astype(F32)[1:2]
    scaled = (window[:MEMBERS].astype(F32) * (precision * taper)).astype(BF16)
    full = lax.dot_general(scaled, window, NT, preferred_element_type=F32)
    forcing = jnp.sum(jnp.where(same, full[:, MEMBERS : MEMBERS + 1], 0.0), axis=0, keepdims=True)
    return full[:, :MEMBERS], forcing


def window_of(p):
    return pl.ds(p * CELLS, 3 * CELLS)


def centre_kernel(pert, wide, blocks_ref, background_ref, mask_ref,
                  gram_ref, force_ref, departure_ref, base_ref, rest_ref, rim_ref, rim_table_ref,
                  soil, held, lines, sems):
    copies = fetch_field(background_ref, 1, held, sems)
    r = lax.broadcasted_iota(jnp.int32, (MEMBERS, MEMBERS), 0)
    c = lax.broadcasted_iota(jnp.int32, (MEMBERS, MEMBERS), 1)
    same = r == c
    taper = tapers()[1]
    forcings = []
    for p in range(PATCHES):
        gram, forcing = patch_gram(pert, window_of(p), taper, same)
        gram_ref[p] = gram + jnp.where(same, MEMBERS - 1.0, 0.0)
        forcings.append(forcing)
    force_ref[...] = jnp.concatenate(forcings, axis=0)
    for place in range(4):
        rim_table_ref[pl.ds(place * COLS, COLS), :] = rim_stencil_rows(place)
    lane = lax.broadcasted_iota(jnp.int32, (CHANNELS, COLS), 1)
    for e in range(PATCHES + 4):
        upper = shift(wide[:, pl.ds(e * CELLS, COLS)], 32)
        lower = shift(wide[:, pl.ds(e * CELLS + COLS, COLS)], -32)
        rim_ref[:, pl.ds(e * COLS, COLS)] = jnp.where(lane < 64, upper, lower)
    widen_lines(copies, held, lines)
    to_blocks(lines, soil)
    for p in range(PATCHES):
        cells = pl.ds(p * CELLS, CELLS)
        land = mask_ref[p : p + 1, :] != 0.0
        for v, raw in enumerate((blocks_ref[pl.ds(0, MEMBERS), cells], soil[:, cells])):
            raw = raw.astype(F32)
            mean = jnp.sum(raw, axis=0, keepdims=True) * (1.0 / MEMBERS)
            place = pl.ds((2 * p + v) * CELLS, CELLS)
            coarse = mean.astype(BF16).astype(F32)
            departure_ref[:, place] = turn_groups(jnp.where(land, raw - mean, 0.0).astype(BF16), p)
            base_ref[:, place] = turn_groups(jnp.where(land, coarse, raw).astype(BF16), p)
            rest = jnp.broadcast_to(jnp.where(land, mean - coarse, 0.0), (8, CELLS))
            rest_ref[:, place] = turn_groups(rest, p)


def split(a):
    high = a.astype(BF16)
    return high, (a - high.astype(F32)).astype(BF16)


def product(a, b):
    a_high, a_low = split(a)
    b_high, b_low = split(b)
    wide = jnp.concatenate([b_high, b_low], axis=1)
    out = jnp.dot(
        jnp.concatenate([a_high, a_low], axis=1),
        jnp.concatenate([wide, wide], axis=0),
        preferred_element_type=F32,
    )
    return out[:, :MEMBERS] + out[:, MEMBERS:]


def halves(a):
    return jnp.concatenate(split(a), axis=1)


def product(a, b):
    out = jnp.dot(a, jnp.concatenate([b, b], axis=0), preferred_element_type=F32)
    return out[:, :MEMBERS] + out[:, MEMBERS:]


def rim_perts(first_ref, second_ref, rim_ref, rim_table_ref, wide_rim, pert):
    lat = lax.axis_index("lat")
    lat_odd = (lat & 1) == 1
    last = lax.axis_size("lat") - 1
    half = MEMBERS // 2

    def tiles_of(source):
        folded = source(RIMS + 2 * MEMBERS, half)
        tails = source(RIMS + 2 * MEMBERS + half, EXTRA).astype(F32)
        tiles = [source(RIMS, MEMBERS), source(RIMS + MEMBERS, MEMBERS)]
        return tiles + [jnp.concatenate([folded, shift(folded, 64)], axis=0)], tails

    def above(start, size):
        rows = pl.ds(start, size)
        return jnp.where(lat_odd, first_ref[rows, :], second_ref[rows, :])

    def below(start, size):
        rows = pl.ds(start, size)
        return jnp.where(lat_odd, second_ref[rows, :], first_ref[rows, :])

    top, top_tails = tiles_of(above)
    low, low_tails = tiles_of(below)
    lane = lax.broadcasted_iota(jnp.int32, (MEMBERS, COLS), 1)
    tail_lane = lax.broadcasted_iota(jnp.int32, (8, COLS), 1)
    wide_rim[:, pl.ds(0, COLS)] = jnp.zeros((MEMBERS, COLS), BF16)
    wide_rim[:, pl.ds((PATCHES + 3) * COLS, COLS)] = jnp.zeros((MEMBERS, COLS), BF16)
    tails = []
    for e in range(PATCHES + 2):
        t, q = divmod(e, 4)
        place = pl.ds((e + 1) * COLS, COLS)
        own = rim_ref[pl.ds(0, MEMBERS), place]
        mixed = jnp.where(lane < 32, shift(top[t], -32 * q), jnp.where(lane < 96, own, shift(low[t], 96 - 32 * q)))
        wide_rim[:, place] = mixed
        own = rim_ref[pl.ds(MEMBERS, EXTRA), place].astype(F32)[:8]
        row = jnp.zeros((6, COLS), F32)
        upper = shift(jnp.concatenate([top_tails[2 * t : 2 * t + 2], row], axis=0), -32 * q)
        lower = shift(jnp.concatenate([low_tails[2 * t : 2 * t + 2], row], axis=0), 96 - 32 * q)
        tails.append(jnp.where(tail_lane < 32, upper, jnp.where(tail_lane < 96, own, lower)))
    line = lax.broadcasted_iota(jnp.int32, (1, COLS), 1)
    row = (line >> 4) & 3
    short = ((row == 1) & (lat == 0)) | ((row == 2) & (lat == last))
    share = jnp.where(short, 1.0 / 6.0, 1.0 / 9.0)
    tail_row = lax.broadcasted_iota(jnp.int32, (EXTRA, COLS), 0)
    for t in range(PATCHES // 2 + 1):
        place = pl.ds(t * COLS, COLS)
        summed = jnp.dot(
            wide_rim[:, pl.ds(2 * t * COLS, 4 * COLS)], rim_table_ref[...], preferred_element_type=F32
        )
        mean = summed * share
        average = jnp.sum(mean, axis=0, keepdims=True) * (1.0 / MEMBERS)
        pert[pl.ds(0, MEMBERS), place] = (mean - average).astype(BF16)
        left, right = tails[2 * t], tails[2 * t + 1]
        group = tail_lane >> 5
        tail = jnp.where(
            group == 0,
            shift(left, -16),
            jnp.where(group == 1, shift(left, -48), jnp.where(group == 2, shift(right, 48), shift(right, 16))),
        )
        innovation = tail[1:2] - average
        pert[pl.ds(MEMBERS, EXTRA), place] = jnp.where(
            tail_row == 0, innovation, jnp.where(tail_row == 1, tail[0:1], 0.0)
        ).astype(BF16)


def solve_kernel(first_ref, second_ref, gram_ref, force_ref, departure_ref, base_ref, rest_ref,
                 rim_ref, rim_table_ref, out_ref,
                 pair_ref, scratch, spread, held, wide_rim, pert, sems):
    rim_perts(first_ref, second_ref, rim_ref, rim_table_ref, wide_rim, pert)
    r = lax.broadcasted_iota(jnp.int32, (MEMBERS, MEMBERS), 0)
    c = lax.broadcasted_iota(jnp.int32, (MEMBERS, MEMBERS), 1)
    eye = jnp.where(r == c, 1.0, 0.0)
    unit = eye.astype(BF16)
    base = (PATCHES // 2) * MEMBERS
    tail = first_ref[pl.ds(base, 16), :].astype(F32) + second_ref[pl.ds(base, 16), :].astype(F32)
    norms, rim_forcings = [], []
    for p in range(PATCHES):
        lanes = pl.ds(p // 2 * COLS, 2 * COLS)
        rim_gram, rim_forcing = patch_gram(pert, lanes, rim_taper(p % 2), r == c)
        rim_forcings.append(rim_forcing)
        spread[0, :, pl.ds(p * MEMBERS, MEMBERS)] = rim_gram
    for pair in range(PATCHES // 2):
        rows = pl.ds(pair * MEMBERS, MEMBERS)
        mixed = first_ref[rows, :].astype(F32) + second_ref[rows, :].astype(F32)
        turned = mixed.T
        diagonal = tail[8 + pair : 9 + pair]
        gains = (
            jnp.where(r >= c, mixed, turned),
            jnp.where(r > c, turned, jnp.where(r < c, mixed, diagonal)),
        )
        for k in range(2):
            p = 2 * pair + k
            system = gram_ref[p] + gains[k] + spread[0, :, pl.ds(p * MEMBERS, MEMBERS)]
            total = jnp.sum(jnp.sum(system * system, axis=0, keepdims=True), axis=1, keepdims=True)
            norm = jnp.sqrt(total)
            norms.append(norm)
            scaled = system * (1.0 / norm)
            split_scaled = halves(scaled)
            pair_ref[p, :MEMBERS] = halves(1.5 * scaled - 0.5 * product(split_scaled, split_scaled))
            pair_ref[p, MEMBERS:] = halves(1.5 * eye - 0.5 * scaled)

    def sweep():
        middles = [
            halves(1.5 * eye - 0.5 * product(pair_ref[p, MEMBERS:], pair_ref[p, :MEMBERS]))
            for p in range(PATCHES)
        ]
        for p in range(PATCHES):
            pair_ref[p] = halves(product(pair_ref[p], middles[p]))

    for _ in range(NS_ITERS - 2):
        sweep()
    middles = [
        halves(1.5 * eye - 0.5 * product(pair_ref[p, MEMBERS:], pair_ref[p, :MEMBERS]))
        for p in range(PATCHES)
    ]
    transforms = []
    for p in range(PATCHES):
        lower = product(pair_ref[p, MEMBERS:], middles[p])
        forcing = force_ref[p : p + 1] + tail[p : p + 1] + rim_forcings[p]
        once = jnp.sum(lower * forcing, axis=1, keepdims=True)
        mean_weight = jnp.sum(lower * once, axis=0, keepdims=True) * (1.0 / norms[p])
        scale = jnp.sqrt(MEMBERS - 1.0) / jnp.sqrt(norms[p])
        transform = (lower * scale + mean_weight).astype(BF16)
        transforms.append(jnp.concatenate([transform, unit], axis=1))

    copies = []
    for v in range(2):
        for p in range(PATCHES):
            cells = pl.ds((2 * p + v) * CELLS, CELLS)
            updated = jnp.dot(
                transforms[p],
                jnp.concatenate([departure_ref[:, cells], base_ref[:, cells]], axis=0),
                preferred_element_type=F32,
            )
            spread[v, :, pl.ds(p * CELLS, CELLS)] = updated + rest_ref[0:1, cells]
        for m in range(MEMBERS // 16):
            rows = pl.ds(m * 16, 16)
            for g in range(2):
                lines = turned_lines(
                    [spread[v, rows, pl.ds(b * CELLS + g * COLS, COLS)] for b in range(PATCHES)]
                )
                for k in range(8):
                    scratch[v, pl.ds(m * 256 + g * 8 + k, 16, stride=16), :] = lines[k]
            held[v, rows] = scratch[v, pl.ds(m * 256, 256), :].reshape(16, ROWS, COLS).astype(BF16)
            copies.append(fetch(held.at[v, rows], out_ref.at[v, rows], sems.at[v * (MEMBERS // 16) + m]))
    for copy in copies:
        copy.wait()


LIMITS = {strip_kernel: 53 * 1024 * 1024}


def call(kernel, out_shape, scratch, flops, moved, *operands, far=(), scalars=(), out_far=False):
    vmem = pl.BlockSpec(memory_space=pltpu.VMEM)
    smem = pl.BlockSpec(memory_space=pltpu.SMEM)
    anywhere = pl.BlockSpec(memory_space=pltpu.HBM)
    return pl.pallas_call(
        kernel,
        out_shape=out_shape,
        in_specs=[
            anywhere if i in far else smem if i in scalars else vmem for i in range(len(operands))
        ],
        out_specs=[anywhere if out_far else vmem] * len(out_shape),
        scratch_shapes=scratch,
        compiler_params=pltpu.CompilerParams(vmem_limit_bytes=LIMITS.get(kernel, VMEM_LIMIT)),
        cost_estimate=pl.CostEstimate(flops=flops, bytes_accessed=moved, transcendentals=0),
    )(*operands)


def pairs_inside(size):
    return [(i, i ^ 1) for i in range(size)]


def pairs_across(size, wrap):
    pairs = []
    for i in range(1, size - 1, 2):
        pairs += [(i, i + 1), (i + 1, i)]
    if wrap:
        pairs += [(size - 1, 0), (0, size - 1)]
    return pairs


def exchange(even, odd, axis, wrap):
    size = lax.axis_size(axis)
    return (
        lax.ppermute(even, axis, pairs_inside(size)),
        lax.ppermute(odd, axis, pairs_across(size, wrap)),
    )


def body(background, obs_cell, obs_count, obs_value, obs_err, land):
    slots = obs_cell.shape[-1]
    span = PATCHES * CELLS
    shape = jax.ShapeDtypeStruct
    field = pltpu.VMEM((MEMBERS, ROWS, COLS), BF16)
    lines_shape = (MEMBERS * ROWS, COLS)
    copies = pltpu.SemaphoreType.DMA
    parts = [array.reshape(1, -1) for array in (obs_cell, land, obs_count)]
    room = slots + (ROWS + 1) * COLS
    pack, start = 0, 0
    for part in parts:
        pack = pack + jnp.pad(part, ((0, 0), (start, room - start - part.shape[1])))
        start += part.shape[1]
    held, even, odd, tails, mask = call(
        strip_kernel,
        [
            shape((MEMBERS, ROWS, COLS), BF16),
            shape((CHANNELS, CELLS), BF16),
            shape((CHANNELS, CELLS), BF16),
            shape((EXTRA, span), BF16),
            shape((8, CELLS), F32),
        ],
        [pltpu.VMEM(lines_shape, F32), copies((PARTS,))],
        10**7, 2 * 10**6,
        background, pack, obs_value.reshape(1, slots), obs_err.reshape(1, slots),
        far=(0,),
    )
    neighbours = exchange(even, odd, "lon", True)
    blocks, table = call(
        block_kernel,
        [shape((CHANNELS, span), BF16), shape((2 * CELLS, CELLS), BF16)],
        [pltpu.VMEM(lines_shape, F32)],
        10**8, 4 * 10**6,
        held, tails,
    )
    even, odd, pert, wide = call(
        gram_kernel,
        [shape((PACKED, MEMBERS), BF16)] * 2
        + [shape((CHANNELS, span + 2 * CELLS), BF16), shape((CHANNELS, span + 4 * CELLS), BF16)],
        [],
        10**9, 3 * 10**6,
        blocks, *neighbours, table,
    )
    packed = exchange(even, odd, "lat", False)
    gram, force, departure, base, rest, rim, rim_table = call(
        centre_kernel,
        [
            shape((PATCHES, MEMBERS, MEMBERS), F32),
            shape((PATCHES, MEMBERS), F32),
            shape((MEMBERS, 2 * span), BF16),
            shape((MEMBERS, 2 * span), BF16),
            shape((8, 2 * span), F32),
            shape((CHANNELS, (PATCHES + 4) * COLS), BF16),
            shape((4 * COLS, COLS), BF16),
        ],
        [pltpu.VMEM((MEMBERS, span), BF16), field, pltpu.VMEM(lines_shape, F32), copies((PARTS,))],
        10**9, 5 * 10**6,
        pert, wide, blocks, background, mask,
        far=(3,),
    )
    (analysis,) = call(
        solve_kernel,
        [shape(background.shape, BF16)],
        [
            pltpu.VMEM((PATCHES, 2 * MEMBERS, 2 * MEMBERS), BF16),
            pltpu.VMEM((2,) + lines_shape, F32),
            pltpu.VMEM((2, MEMBERS, span), F32),
            pltpu.VMEM(background.shape, BF16),
            pltpu.VMEM((MEMBERS, (PATCHES + 4) * COLS), BF16),
            pltpu.VMEM((CHANNELS, (PATCHES // 2 + 1) * COLS), BF16),
            copies((2 * MEMBERS // 16,)),
        ],
        2 * 10**9, 5 * 10**6,
        *packed, gram, force, departure, base, rest, rim, rim_table,
        out_far=True,
    )
    return analysis


def solution(mesh):
    return jax.shard_map(
        body,
        mesh=mesh,
        in_specs=(
            P(None, None, "lat", "lon"),
            P("lat", "lon", None),
            P("lat", "lon"),
            P("lat", "lon", None),
            P("lat", "lon", None),
            P("lat", "lon"),
        ),
        out_specs=P(None, None, "lat", "lon"),
        check_vma=False,
    )
```

```python
import jax
import jax.numpy as jnp
import numpy as np
from jax import lax
from jax.experimental import pallas as pl
from jax.experimental.pallas import tpu as pltpu
from jax.sharding import PartitionSpec as P

MEMBERS = 128
PATCH = 16
RADIUS = 15
NS_ITERS = 5
ROWS = 16
COLS = 128
PATCHES = COLS // PATCH
CELLS = PATCH * PATCH
EXTRA = 16
CHANNELS = MEMBERS + EXTRA
RIMS = (PATCHES // 2) * MEMBERS + 16
PACKED = RIMS + 2 * MEMBERS + MEMBERS // 2 + EXTRA
NT = (((1,), (1,)), ((), ()))
PARTS = 4
VMEM_LIMIT = 48 * 1024 * 1024
F32 = jnp.float32
BF16 = jnp.bfloat16


def tapers():
    lane = lax.broadcasted_iota(jnp.int32, (1, 3 * CELLS), 1)
    side = lane >> 8
    row, column = (lane >> 4) & (PATCH - 1), lane & (PATCH - 1)
    span = 2.0 * (RADIUS + PATCH / 2.0)
    half = (PATCH - 1) / 2.0

    def line(place, shift):
        offset = jnp.abs(place.astype(F32) + (PATCH * shift - half))
        return jnp.where(offset < RADIUS + PATCH / 2.0, 1.0 - offset / span, 0.0)

    lon = jnp.where(side == 0, line(column, -1), jnp.where(side == 1, line(column, 0), line(column, 1)))
    inner = (row > 0) & (row < ROWS - 1)
    return [jnp.where(inner, line(row, shift) * lon, 0.0) for shift in (1, 0, -1)]


def rim_taper(first):
    lane = lax.broadcasted_iota(jnp.int32, (1, 2 * COLS), 1)
    side = (lane >> 6) - first - 1
    row, column = (lane >> 4) & 3, lane & (PATCH - 1)
    span = 2.0 * (RADIUS + PATCH / 2.0)
    half = (PATCH - 1) / 2.0
    across = jnp.where((row == 0) | (row == 3), 1.0 - (half + 1.0) / span, 1.0 - half / span)
    offset = jnp.abs(column.astype(F32) + side.astype(F32) * PATCH - half)
    along = jnp.where(offset < RADIUS + PATCH / 2.0, 1.0 - offset / span, 0.0)
    return across * along


def stencil_rows(first):
    cell = (first & (CELLS - 1)) + lax.broadcasted_iota(jnp.int32, (COLS, CELLS), 0)
    lane = lax.broadcasted_iota(jnp.int32, (COLS, CELLS), 1)
    near = jnp.abs((cell >> 4) - (lane >> 4)) <= 1
    apart = jnp.abs((cell & (PATCH - 1)) - (lane & (PATCH - 1)))
    beside = apart <= 1 if first < CELLS else apart == PATCH - 1
    return jnp.where(near & beside, 1.0, 0.0).astype(BF16)


def rim_stencil_rows(place):
    cell = lax.broadcasted_iota(jnp.int32, (COLS, COLS), 0)
    lane = lax.broadcasted_iota(jnp.int32, (COLS, COLS), 1)
    row = (lane >> 4) & 3
    step = (cell >> 4) - jnp.where(row < 2, row, row + 2)
    side = place - 1 - (lane >> 6)
    beside = jnp.abs(side * PATCH + (cell & (PATCH - 1)) - (lane & (PATCH - 1))) <= 1
    return jnp.where((step >= 0) & (step <= 2) & beside, 1.0, 0.0).astype(BF16)


def swap_groups(arrays):
    lane = lax.broadcasted_iota(jnp.int32, arrays[0].shape, 1)
    for step in (1, 2, 4):
        width = PATCH * step
        high = (lane & width) != 0
        mixed = list(arrays)
        for i in range(8):
            if i & step == 0:
                first, second = arrays[i], arrays[i + step]
                mixed[i] = jnp.where(high, pltpu.roll(second, width, 1), first)
                mixed[i + step] = jnp.where(high, second, pltpu.roll(first, COLS - width, 1))
        arrays = mixed
    return arrays


def shift(piece, lanes):
    return pltpu.roll(piece, lanes % COLS, 1) if lanes % COLS else piece


def turn_groups(block, p):
    return jnp.concatenate([shift(block[:, :COLS], PATCH * p), shift(block[:, COLS:], PATCH * p)], axis=1)


def turned_lines(arrays):
    group = lax.broadcasted_iota(jnp.int32, arrays[0].shape, 1) >> 4
    for step in (1, 2, 4):
        odd = (group & step) != 0
        arrays = [jnp.where(odd, arrays[(i + step) % 8], arrays[i]) for i in range(8)]
    return [shift(arrays[-r % 8], -PATCH * r) for r in range(8)]


def fetch(source, target, sem):
    copy = pltpu.make_async_copy(source, target, sem)
    copy.start()
    return copy


def fetch_field(background_ref, variable, held, sems):
    part = MEMBERS // PARTS
    return [
        fetch(
            background_ref.at[variable, pl.ds(k * part, part)], held.at[pl.ds(k * part, part)], sems.at[k]
        )
        for k in range(PARTS)
    ]


def widen_lines(copies, held, lines):
    part = MEMBERS // PARTS
    for k in range(PARTS):
        if copies:
            copies[k].wait()
        for m in range(k * part // 16, (k + 1) * part // 16):
            piece = held[pl.ds(m * 16, 16)].astype(F32)
            lines[pl.ds(m * 256, 256), :] = piece.reshape(256, COLS)


def to_blocks(lines, out_ref):
    for m in range(MEMBERS // 16):
        halves = []
        for g in range(2):
            rows = [lines[pl.ds(m * 256 + g * 8 + r, 16, stride=16), :].astype(BF16) for r in range(8)]
            halves.append(swap_groups(rows))
        for b in range(PATCHES):
            both = jnp.concatenate([halves[0][b], halves[1][b]], axis=1)
            out_ref[pl.ds(m * 16, 16), pl.ds(b * CELLS, CELLS)] = both


def strip_kernel(background_ref, pack_ref, value_ref, err_ref,
                 held, even_ref, odd_ref, tails_ref, mask_ref, lines, sems):
    lon_odd = (lax.axis_index("lon") & 1) == 1
    copies = fetch_field(background_ref, 0, held, sems)
    slots = value_ref.shape[1]
    halves = []
    for g in range(2):
        rows = [
            jnp.broadcast_to(pack_ref[:, pl.ds(slots + (g * 8 + r) * COLS, COLS)].astype(F32), (8, COLS))
            for r in range(8)
        ]
        halves.append(swap_groups(rows))
    which = lax.broadcasted_iota(jnp.int32, (8, CELLS), 0)
    mask = jnp.zeros((8, CELLS), F32)
    for b in range(PATCHES):
        mask = jnp.where(which == b, jnp.concatenate([halves[0][b], halves[1][b]], axis=1), mask)
    mask_ref[...] = mask
    cell = pack_ref[:, pl.ds(0, slots)]
    count = pack_ref[:, pl.ds(slots + ROWS * COLS, COLS)][:, 0:1]
    used = lax.broadcasted_iota(jnp.int32, (1, slots), 1) < count
    err = err_ref[...]
    inverse = jnp.where(used, 1.0 / (err * err), 0.0)
    value = jnp.where(used, value_ref[...].astype(F32), 0.0)
    column = cell & (COLS - 1)
    block = column >> 4
    place = ((cell >> 7) << 4) + (column & (PATCH - 1))
    slot_block = lax.broadcasted_iota(jnp.int32, (16, value.shape[1]), 0)
    chosen = (slot_block & 7) == block
    amount = jnp.where(slot_block < 8, inverse, value)
    left = jnp.where(chosen, amount, 0.0).astype(BF16)
    spot = lax.broadcasted_iota(jnp.int32, (CELLS, value.shape[1]), 0) == place
    right = jnp.where(spot, 1.0, 0.0).astype(BF16)
    grids = lax.dot_general(left, right, NT, preferred_element_type=F32)
    precision = grids[:8] * mask
    observed = grids[8:]
    channel = lax.broadcasted_iota(jnp.int32, (EXTRA, CELLS), 0)
    for b in range(PATCHES):
        tail = jnp.where(
            channel == 0, precision[b : b + 1], jnp.where(channel == 1, observed[b : b + 1], 0.0)
        ).astype(BF16)
        tails_ref[:, pl.ds(b * CELLS, CELLS)] = tail
        if b == 0:
            west = tail
    even_ref[pl.ds(MEMBERS, EXTRA), :] = jnp.where(lon_odd, west, tail)
    odd_ref[pl.ds(MEMBERS, EXTRA), :] = jnp.where(lon_odd, tail, west)

    widen_lines(copies, held, lines)
    group = lax.broadcasted_iota(jnp.int32, (16, COLS), 1) >> 4
    for m in range(MEMBERS // 16):
        for g in range(2):
            west = jnp.zeros((16, COLS), BF16)
            east = west
            for r in range(8):
                row = lines[pl.ds(m * 256 + g * 8 + r, 16, stride=16), :].astype(BF16)
                here = group == r
                turned = shift(row, PATCH * r)
                west = jnp.where(here, turned, west)
                east = jnp.where(group == (r + 7) % 8, turned, east)
            east = shift(east, PATCH)
            even_ref[pl.ds(m * 16, 16), pl.ds(g * COLS, COLS)] = jnp.where(lon_odd, west, east)
            odd_ref[pl.ds(m * 16, 16), pl.ds(g * COLS, COLS)] = jnp.where(lon_odd, east, west)


def block_kernel(held, tails_ref, blocks_ref, table_ref, lines):
    for first in range(0, 2 * CELLS, COLS):
        table_ref[pl.ds(first, COLS), :] = stencil_rows(first)
    widen_lines((), held, lines)
    to_blocks(lines, blocks_ref)
    blocks_ref[pl.ds(MEMBERS, EXTRA), :] = tails_ref[...]


def quarters(pieces, lane):
    tile = pieces[0]
    for q in range(1, len(pieces)):
        tile = jnp.where((lane >> 5) == q, shift(pieces[q], 32 * q), tile)
    return tile


def gram_kernel(blocks_ref, first_ref, second_ref, table_ref, even_ref, odd_ref, pert, wide):
    lat_odd = (lax.axis_index("lat") & 1) == 1
    lon_odd = (lax.axis_index("lon") & 1) == 1
    span = PATCHES * CELLS
    wide[:, pl.ds(0, CELLS)] = jnp.zeros((CHANNELS, CELLS), BF16)
    wide[:, pl.ds(span + 3 * CELLS, CELLS)] = jnp.zeros((CHANNELS, CELLS), BF16)
    wide[:, pl.ds(2 * CELLS, span)] = blocks_ref[...]
    one, two = first_ref[...], second_ref[...]
    wide[:, pl.ds(CELLS, CELLS)] = jnp.where(lon_odd, one, two)
    wide[:, pl.ds(span + 2 * CELLS, CELLS)] = jnp.where(lon_odd, two, one)

    tail_row = lax.broadcasted_iota(jnp.int32, (EXTRA, CELLS), 0)
    column = lax.broadcasted_iota(jnp.int32, (MEMBERS, CELLS), 1) & (PATCH - 1)
    rows = pl.ds(0, MEMBERS)
    for e in range(PATCHES + 2):
        left, own, right = (wide[rows, pl.ds((e + k) * CELLS, CELLS)] for k in range(3))
        beside = jnp.where(column == PATCH - 1, left, jnp.where(column == 0, right, jnp.zeros_like(own)))
        summed = jnp.dot(
            jnp.concatenate([own, beside], axis=1), table_ref[...], preferred_element_type=F32
        )
        mean = summed * (1.0 / 9.0)
        average = jnp.sum(mean, axis=0, keepdims=True) * (1.0 / MEMBERS)
        pert[pl.ds(0, MEMBERS), pl.ds(e * CELLS, CELLS)] = (mean - average).astype(BF16)
        tail = wide[pl.ds(MEMBERS, EXTRA), pl.ds((e + 1) * CELLS, CELLS)].astype(F32)
        innovation = tail[1:2] - average
        pert[pl.ds(MEMBERS, EXTRA), pl.ds(e * CELLS, CELLS)] = jnp.where(
            tail_row == 0, innovation, jnp.where(tail_row == 1, tail[0:1], 0.0)
        ).astype(BF16)

    write_message(pert, wide, even_ref, lat_odd)
    write_message(pert, wide, odd_ref, jnp.logical_not(lat_odd))


def write_message(pert, wide, out_ref, upward):
    lane = lax.broadcasted_iota(jnp.int32, (MEMBERS, COLS), 1)
    tail_lane = lax.broadcasted_iota(jnp.int32, (EXTRA, COLS), 1)

    def near_rows(rows, e):
        first, last = (wide[rows, pl.ds((e + 1) * CELLS + part * COLS, COLS)] for part in range(2))
        return jnp.where(upward, first, shift(last, 32))

    tiles, tails = [], []
    for t in range(3):
        some = range(4 * t, min(4 * t + 4, PATCHES + 2))
        tiles.append(quarters([near_rows(pl.ds(0, MEMBERS), e) for e in some], lane))
        tail = [near_rows(pl.ds(MEMBERS, EXTRA), e).astype(F32) for e in some]
        tails.append(quarters(tail, tail_lane)[0:2])
    half = MEMBERS // 2
    tiles[2] = jnp.where(lane[:half] < 64, tiles[2][:half], shift(tiles[2][half:], 64))
    tiles.append(jnp.concatenate(tails + [jnp.zeros((EXTRA - 6, COLS), F32)], axis=0).astype(BF16))
    start = RIMS
    for tile in tiles:
        out_ref[pl.ds(start, tile.shape[0]), :] = tile
        start += tile.shape[0]

    r = lax.broadcasted_iota(jnp.int32, (MEMBERS, MEMBERS), 0)
    c = lax.broadcasted_iota(jnp.int32, (MEMBERS, MEMBERS), 1)
    lower = r >= c
    same = r == c
    above, _, below = tapers()
    taper = jnp.where(upward, above, below)
    forcings, diagonals = [], []
    for pair in range(PATCHES // 2):
        first, forcing = patch_gram(pert, window_of(2 * pair), taper, same)
        forcings.append(forcing)
        second, forcing = patch_gram(pert, window_of(2 * pair + 1), taper, same)
        forcings.append(forcing)
        diagonals.append(jnp.sum(jnp.where(same, second, 0.0), axis=0, keepdims=True))
        out_ref[pl.ds(pair * MEMBERS, MEMBERS), :] = jnp.where(lower, first, second).astype(BF16)
    tail = forcings + diagonals + [jnp.zeros((4, MEMBERS), F32)]
    out_ref[pl.ds((PATCHES // 2) * MEMBERS, 16), :] = jnp.concatenate(tail, axis=0).astype(BF16)


def patch_gram(pert, lanes, taper, same):
    window = pert[:, lanes]
    precision = window[MEMBERS:].astype(F32)[1:2]
    scaled = (window[:MEMBERS].astype(F32) * (precision * taper)).astype(BF16)
    full = lax.dot_general(scaled, window, NT, preferred_element_type=F32)
    forcing = jnp.sum(jnp.where(same, full[:, MEMBERS : MEMBERS + 1], 0.0), axis=0, keepdims=True)
    return full[:, :MEMBERS], forcing


def window_of(p):
    return pl.ds(p * CELLS, 3 * CELLS)


def centre_kernel(pert, wide, blocks_ref, background_ref, mask_ref,
                  gram_ref, force_ref, departure_ref, base_ref, rest_ref, rim_ref, rim_table_ref,
                  soil, held, lines, sems):
    copies = fetch_field(background_ref, 1, held, sems)
    r = lax.broadcasted_iota(jnp.int32, (MEMBERS, MEMBERS), 0)
    c = lax.broadcasted_iota(jnp.int32, (MEMBERS, MEMBERS), 1)
    same = r == c
    taper = tapers()[1]
    forcings = []
    for p in range(PATCHES):
        gram, forcing = patch_gram(pert, window_of(p), taper, same)
        gram_ref[p] = gram + jnp.where(same, MEMBERS - 1.0, 0.0)
        forcings.append(forcing)
    force_ref[...] = jnp.concatenate(forcings, axis=0)
    for place in range(4):
        rim_table_ref[pl.ds(place * COLS, COLS), :] = rim_stencil_rows(place)
    lane = lax.broadcasted_iota(jnp.int32, (CHANNELS, COLS), 1)
    for e in range(PATCHES + 4):
        upper = shift(wide[:, pl.ds(e * CELLS, COLS)], 32)
        lower = shift(wide[:, pl.ds(e * CELLS + COLS, COLS)], -32)
        rim_ref[:, pl.ds(e * COLS, COLS)] = jnp.where(lane < 64, upper, lower)
    widen_lines(copies, held, lines)
    to_blocks(lines, soil)
    for p in range(PATCHES):
        cells = pl.ds(p * CELLS, CELLS)
        land = mask_ref[p : p + 1, :] != 0.0
        for v, raw in enumerate((blocks_ref[pl.ds(0, MEMBERS), cells], soil[:, cells])):
            raw = raw.astype(F32)
            mean = jnp.sum(raw, axis=0, keepdims=True) * (1.0 / MEMBERS)
            place = pl.ds((2 * p + v) * CELLS, CELLS)
            coarse = mean.astype(BF16).astype(F32)
            departure_ref[:, place] = turn_groups(jnp.where(land, raw - mean, 0.0).astype(BF16), p)
            base_ref[:, place] = turn_groups(jnp.where(land, coarse, raw).astype(BF16), p)
            rest = jnp.broadcast_to(jnp.where(land, mean - coarse, 0.0), (8, CELLS))
            rest_ref[:, place] = turn_groups(rest, p)


def split(a):
    high = a.astype(BF16)
    return high, (a - high.astype(F32)).astype(BF16)


def product(a, b):
    a_high, a_low = split(a)
    b_high, b_low = split(b)
    wide = jnp.concatenate([b_high, b_low], axis=1)
    out = jnp.dot(
        jnp.concatenate([a_high, a_low], axis=1),
        jnp.concatenate([wide, wide], axis=0),
        preferred_element_type=F32,
    )
    return out[:, :MEMBERS] + out[:, MEMBERS:]


def halves(a):
    return jnp.concatenate(split(a), axis=1)


def product(a, b):
    out = jnp.dot(a, jnp.concatenate([b, b], axis=0), preferred_element_type=F32)
    return out[:, :MEMBERS] + out[:, MEMBERS:]


def rim_perts(first_ref, second_ref, rim_ref, rim_table_ref, wide_rim, pert):
    lat = lax.axis_index("lat")
    lat_odd = (lat & 1) == 1
    last = lax.axis_size("lat") - 1
    half = MEMBERS // 2

    def tiles_of(source):
        folded = source(RIMS + 2 * MEMBERS, half)
        tails = source(RIMS + 2 * MEMBERS + half, EXTRA).astype(F32)
        tiles = [source(RIMS, MEMBERS), source(RIMS + MEMBERS, MEMBERS)]
        return tiles + [jnp.concatenate([folded, shift(folded, 64)], axis=0)], tails

    def above(start, size):
        rows = pl.ds(start, size)
        return jnp.where(lat_odd, first_ref[rows, :], second_ref[rows, :])

    def below(start, size):
        rows = pl.ds(start, size)
        return jnp.where(lat_odd, second_ref[rows, :], first_ref[rows, :])

    top, top_tails = tiles_of(above)
    low, low_tails = tiles_of(below)
    lane = lax.broadcasted_iota(jnp.int32, (MEMBERS, COLS), 1)
    tail_lane = lax.broadcasted_iota(jnp.int32, (8, COLS), 1)
    wide_rim[:, pl.ds(0, COLS)] = jnp.zeros((MEMBERS, COLS), BF16)
    wide_rim[:, pl.ds((PATCHES + 3) * COLS, COLS)] = jnp.zeros((MEMBERS, COLS), BF16)
    tails = []
    for e in range(PATCHES + 2):
        t, q = divmod(e, 4)
        place = pl.ds((e + 1) * COLS, COLS)
        own = rim_ref[pl.ds(0, MEMBERS), place]
        mixed = jnp.where(lane < 32, shift(top[t], -32 * q), jnp.where(lane < 96, own, shift(low[t], 96 - 32 * q)))
        wide_rim[:, place] = mixed
        own = rim_ref[pl.ds(MEMBERS, EXTRA), place].astype(F32)[:8]
        row = jnp.zeros((6, COLS), F32)
        upper = shift(jnp.concatenate([top_tails[2 * t : 2 * t + 2], row], axis=0), -32 * q)
        lower = shift(jnp.concatenate([low_tails[2 * t : 2 * t + 2], row], axis=0), 96 - 32 * q)
        tails.append(jnp.where(tail_lane < 32, upper, jnp.where(tail_lane < 96, own, lower)))
    line = lax.broadcasted_iota(jnp.int32, (1, COLS), 1)
    row = (line >> 4) & 3
    short = ((row == 1) & (lat == 0)) | ((row == 2) & (lat == last))
    share = jnp.where(short, 1.0 / 6.0, 1.0 / 9.0)
    tail_row = lax.broadcasted_iota(jnp.int32, (EXTRA, COLS), 0)
    for t in range(PATCHES // 2 + 1):
        place = pl.ds(t * COLS, COLS)
        summed = jnp.dot(
            wide_rim[:, pl.ds(2 * t * COLS, 4 * COLS)], rim_table_ref[...], preferred_element_type=F32
        )
        mean = summed * share
        average = jnp.sum(mean, axis=0, keepdims=True) * (1.0 / MEMBERS)
        pert[pl.ds(0, MEMBERS), place] = (mean - average).astype(BF16)
        left, right = tails[2 * t], tails[2 * t + 1]
        group = tail_lane >> 5
        tail = jnp.where(
            group == 0,
            shift(left, -16),
            jnp.where(group == 1, shift(left, -48), jnp.where(group == 2, shift(right, 48), shift(right, 16))),
        )
        innovation = tail[1:2] - average
        pert[pl.ds(MEMBERS, EXTRA), place] = jnp.where(
            tail_row == 0, innovation, jnp.where(tail_row == 1, tail[0:1], 0.0)
        ).astype(BF16)


def solve_kernel(first_ref, second_ref, gram_ref, force_ref, departure_ref, base_ref, rest_ref,
                 rim_ref, rim_table_ref, out_ref,
                 pair_ref, scratch, spread, held, wide_rim, pert, sems):
    rim_perts(first_ref, second_ref, rim_ref, rim_table_ref, wide_rim, pert)
    r = lax.broadcasted_iota(jnp.int32, (MEMBERS, MEMBERS), 0)
    c = lax.broadcasted_iota(jnp.int32, (MEMBERS, MEMBERS), 1)
    eye = jnp.where(r == c, 1.0, 0.0)
    unit = eye.astype(BF16)
    base = (PATCHES // 2) * MEMBERS
    tail = first_ref[pl.ds(base, 16), :].astype(F32) + second_ref[pl.ds(base, 16), :].astype(F32)
    norms, rim_forcings = [], []
    for p in range(PATCHES):
        lanes = pl.ds(p // 2 * COLS, 2 * COLS)
        rim_gram, rim_forcing = patch_gram(pert, lanes, rim_taper(p % 2), r == c)
        rim_forcings.append(rim_forcing)
        spread[0, :, pl.ds(p * MEMBERS, MEMBERS)] = rim_gram
    for pair in range(PATCHES // 2):
        rows = pl.ds(pair * MEMBERS, MEMBERS)
        mixed = first_ref[rows, :].astype(F32) + second_ref[rows, :].astype(F32)
        turned = mixed.T
        diagonal = tail[8 + pair : 9 + pair]
        gains = (
            jnp.where(r >= c, mixed, turned),
            jnp.where(r > c, turned, jnp.where(r < c, mixed, diagonal)),
        )
        for k in range(2):
            p = 2 * pair + k
            system = gram_ref[p] + gains[k] + spread[0, :, pl.ds(p * MEMBERS, MEMBERS)]
            total = jnp.sum(jnp.sum(system * system, axis=0, keepdims=True), axis=1, keepdims=True)
            norm = jnp.sqrt(total)
            norms.append(norm)
            scaled = system * (1.0 / norm)
            split_scaled = halves(scaled)
            pair_ref[p, :MEMBERS] = halves(1.5 * scaled - 0.5 * product(split_scaled, split_scaled))
            pair_ref[p, MEMBERS:] = halves(1.5 * eye - 0.5 * scaled)

    def sweep():
        middles = [
            halves(1.5 * eye - 0.5 * product(pair_ref[p, MEMBERS:], pair_ref[p, :MEMBERS]))
            for p in range(PATCHES)
        ]
        for p in range(PATCHES):
            pair_ref[p] = halves(product(pair_ref[p], middles[p]))

    for _ in range(NS_ITERS - 2):
        sweep()
    middles = [
        halves(1.5 * eye - 0.5 * product(pair_ref[p, MEMBERS:], pair_ref[p, :MEMBERS]))
        for p in range(PATCHES)
    ]
    transforms = []
    for p in range(PATCHES):
        lower = product(pair_ref[p, MEMBERS:], middles[p])
        forcing = force_ref[p : p + 1] + tail[p : p + 1] + rim_forcings[p]
        once = jnp.sum(lower * forcing, axis=1, keepdims=True)
        mean_weight = jnp.sum(lower * once, axis=0, keepdims=True) * (1.0 / norms[p])
        scale = jnp.sqrt(MEMBERS - 1.0) / jnp.sqrt(norms[p])
        transform = (lower * scale + mean_weight).astype(BF16)
        transforms.append(jnp.concatenate([transform, unit], axis=1))

    copies = []
    for v in range(2):
        for p in range(PATCHES):
            cells = pl.ds((2 * p + v) * CELLS, CELLS)
            updated = jnp.dot(
                transforms[p],
                jnp.concatenate([departure_ref[:, cells], base_ref[:, cells]], axis=0),
                preferred_element_type=F32,
            )
            spread[v, :, pl.ds(p * CELLS, CELLS)] = updated + rest_ref[0:1, cells]
        for m in range(MEMBERS // 16):
            rows = pl.ds(m * 16, 16)
            for g in range(2):
                lines = turned_lines(
                    [spread[v, rows, pl.ds(b * CELLS + g * COLS, COLS)] for b in range(PATCHES)]
                )
                for k in range(8):
                    scratch[v, pl.ds(m * 256 + g * 8 + k, 16, stride=16), :] = lines[k]
            held[v, rows] = scratch[v, pl.ds(m * 256, 256), :].reshape(16, ROWS, COLS).astype(BF16)
            copies.append(fetch(held.at[v, rows], out_ref.at[v, rows], sems.at[v * (MEMBERS // 16) + m]))
    for copy in copies:
        copy.wait()


LIMITS = {strip_kernel: 53 * 1024 * 1024}


def call(kernel, out_shape, scratch, flops, moved, *operands, far=(), scalars=(), out_far=False):
    vmem = pl.BlockSpec(memory_space=pltpu.VMEM)
    smem = pl.BlockSpec(memory_space=pltpu.SMEM)
    anywhere = pl.BlockSpec(memory_space=pltpu.HBM)
    return pl.pallas_call(
        kernel,
        out_shape=out_shape,
        in_specs=[
            anywhere if i in far else smem if i in scalars else vmem for i in range(len(operands))
        ],
        out_specs=[anywhere if out_far else vmem] * len(out_shape),
        scratch_shapes=scratch,
        compiler_params=pltpu.CompilerParams(vmem_limit_bytes=LIMITS.get(kernel, VMEM_LIMIT)),
        cost_estimate=pl.CostEstimate(flops=flops, bytes_accessed=moved, transcendentals=0),
    )(*operands)


def pairs_inside(size):
    return [(i, i ^ 1) for i in range(size)]


def pairs_across(size, wrap):
    pairs = []
    for i in range(1, size - 1, 2):
        pairs += [(i, i + 1), (i + 1, i)]
    if wrap:
        pairs += [(size - 1, 0), (0, size - 1)]
    return pairs


def exchange(even, odd, axis, wrap):
    size = lax.axis_size(axis)
    return (
        lax.ppermute(even, axis, pairs_inside(size)),
        lax.ppermute(odd, axis, pairs_across(size, wrap)),
    )


def body(background, obs_cell, obs_count, obs_value, obs_err, land):
    slots = obs_cell.shape[-1]
    span = PATCHES * CELLS
    shape = jax.ShapeDtypeStruct
    field = pltpu.VMEM((MEMBERS, ROWS, COLS), BF16)
    lines_shape = (MEMBERS * ROWS, COLS)
    copies = pltpu.SemaphoreType.DMA
    parts = [array.reshape(1, -1) for array in (obs_cell, land, obs_count)]
    room = slots + (ROWS + 1) * COLS
    pack, start = 0, 0
    for part in parts:
        pack = pack + jnp.pad(part, ((0, 0), (start, room - start - part.shape[1])))
        start += part.shape[1]
    held, even, odd, tails, mask = call(
        strip_kernel,
        [
            shape((MEMBERS, ROWS, COLS), BF16),
            shape((CHANNELS, CELLS), BF16),
            shape((CHANNELS, CELLS), BF16),
            shape((EXTRA, span), BF16),
            shape((8, CELLS), F32),
        ],
        [pltpu.VMEM(lines_shape, F32), copies((PARTS,))],
        10**7, 2 * 10**6,
        background, pack, obs_value.reshape(1, slots), obs_err.reshape(1, slots),
        far=(0,),
    )
    neighbours = exchange(even, odd, "lon", True)
    blocks, table = call(
        block_kernel,
        [shape((CHANNELS, span), BF16), shape((2 * CELLS, CELLS), BF16)],
        [pltpu.VMEM(lines_shape, F32)],
        10**8, 4 * 10**6,
        held, tails,
    )
    even, odd, pert, wide = call(
        gram_kernel,
        [shape((PACKED, MEMBERS), BF16)] * 2
        + [shape((CHANNELS, span + 2 * CELLS), BF16), shape((CHANNELS, span + 4 * CELLS), BF16)],
        [],
        10**9, 3 * 10**6,
        blocks, *neighbours, table,
    )
    packed = exchange(even, odd, "lat", False)
    gram, force, departure, base, rest, rim, rim_table = call(
        centre_kernel,
        [
            shape((PATCHES, MEMBERS, MEMBERS), F32),
            shape((PATCHES, MEMBERS), F32),
            shape((MEMBERS, 2 * span), BF16),
            shape((MEMBERS, 2 * span), BF16),
            shape((8, 2 * span), F32),
            shape((CHANNELS, (PATCHES + 4) * COLS), BF16),
            shape((4 * COLS, COLS), BF16),
        ],
        [pltpu.VMEM((MEMBERS, span), BF16), field, pltpu.VMEM(lines_shape, F32), copies((PARTS,))],
        10**9, 5 * 10**6,
        pert, wide, blocks, background, mask,
        far=(3,),
    )
    (analysis,) = call(
        solve_kernel,
        [shape(background.shape, BF16)],
        [
            pltpu.VMEM((PATCHES, 2 * MEMBERS, 2 * MEMBERS), BF16),
            pltpu.VMEM((2,) + lines_shape, F32),
            pltpu.VMEM((2, MEMBERS, span), F32),
            pltpu.VMEM(background.shape, BF16),
            pltpu.VMEM((MEMBERS, (PATCHES + 4) * COLS), BF16),
            pltpu.VMEM((CHANNELS, (PATCHES // 2 + 1) * COLS), BF16),
            copies((2 * MEMBERS // 16,)),
        ],
        2 * 10**9, 5 * 10**6,
        *packed, gram, force, departure, base, rest, rim, rim_table,
        out_far=True,
    )
    return analysis


def solution(mesh):
    return jax.shard_map(
        body,
        mesh=mesh,
        in_specs=(
            P(None, None, "lat", "lon"),
            P("lat", "lon", None),
            P("lat", "lon"),
            P("lat", "lon", None),
            P("lat", "lon", None),
            P("lat", "lon"),
        ),
        out_specs=P(None, None, "lat", "lon"),
        check_vma=False,
    )
```
